512 devices in a mesh: dp: 32 (over z, x_hi, core), sub: 16 (over x_lo, y).
Axes of the slice: x: 4 (x_hi: 2, x_lo: 2; x = x_hi * 2 + x_lo), y: 8, z: 8, core: 2. Of those that a mesh axis runs over, the one named last changes fastest.
Arguments:
- samples: bfloat16 [65536, 1024], P(('dp', 'sub')), may hold values from -12 to 12
- rotation: bfloat16 [1024, 1024], P(None, 'sub'), may hold values from -0.1875 to 0.1875
- codebook: float32 [16, 256, 64], P('sub'), may hold values from -4 to 4
Outputs:
- recon: bfloat16 [65536, 1024], P(('dp', 'sub'))
- new_codebook: float32 [16, 256, 64], P('sub')
- cross: float32 [1024, 1024], P(('dp', 'sub'))
The draws below stay inside these ranges and needn't reach their ends.
All inputs are finite; a program needn't handle non-finite values.
Results may differ from the reference program's by a relative error of at most 0.02.
Values may be sent and summed in bfloat16 or wider, within the bound.
No kernel may reach another device: no remote copies, remote signals or barrier semaphores. Data moves between devices by JAX's collectives and lax.ppermute only.
A program may use at most 64 MiB of HBM per device.

```python
import jax
import jax.numpy as jnp

SUB_DIM = 64
CODES = 256
ROWS_DEV = 128
SUBS = 16
DIM = 1024
ROWS = 65536


def draw_samples(key, part):
    key = jax.random.fold_in(key, 7)
    first = jax.random.fold_in(key, 0)
    fourth = jax.random.fold_in(key, 3)
    values = jax.random.normal(first, (ROWS, DIM), jnp.float32)
    blocks = ROWS // ROWS_DEV
    width = DIM // blocks
    pairing = jax.random.permutation(fourth, blocks)
    row_block = jnp.arange(ROWS) // ROWS_DEV
    column_block = jnp.arange(DIM) // width
    heavy = pairing[row_block][:, None] == column_block[None, :]
    values = jnp.where(heavy, 6.0 * values, values)
    return jnp.clip(values, -12.0, 12.0).astype(jnp.bfloat16)


def block_levels(key, shape, shards, low, largest):
    gain, own = 1.0, jax.random.fold_in(key, 6)
    for dim, shards_of in shards:
        draws = jnp.exp(jax.random.uniform(jax.random.fold_in(own, dim), (shards_of,), jnp.float32, low / len(shards), largest / len(shards)))
        gain = gain * jnp.repeat(draws, shape[dim] // shards_of).reshape([-1 if axis == dim else 1 for axis in range(len(shape))])
    return gain


def centred(stream_key, shape, scale, most, shards=(), kind=jnp.bfloat16):
    values = jax.random.normal(stream_key, shape, jnp.float32) * scale
    if len(shards) > 0:
        values = block_levels(stream_key, shape, shards, -0.22, 0.18) * values
    return jnp.clip(values, min=-most, max=most).astype(kind)


def setup_inputs(seed: int = 0) -> dict:
    key_list = jax.random.split(jax.random.key(seed), 4)
    samples = draw_samples(jax.random.fold_in(key_list[3], 71), 0)
    rotation = centred(key_list[1], (DIM, DIM), DIM ** -0.5, 0.1875, ((1, 16),))
    codebook = centred(key_list[2], (SUBS, CODES, SUB_DIM), 1.0, 4.0, ((0, 16),), jnp.float32)
    return {"samples": samples, "rotation": rotation, "codebook": codebook}


def reference(samples, rotation, codebook):
    total_rows = samples.shape[0]
    block_rows = min(8192, total_rows)
    count_blocks = total_rows // block_rows
    codes_low = codebook.astype(jnp.bfloat16).astype(jnp.float32)
    code_square = jnp.sum(codebook * codebook, axis=-1)

    def step(carry, sample_block):
        sums, counts, cross = carry
        rotated = jnp.dot(sample_block, rotation, preferred_element_type=jnp.float32).astype(jnp.bfloat16)
        parts = rotated.reshape(block_rows, SUBS, SUB_DIM).astype(jnp.float32)
        inner = jnp.einsum('bsk,sck->bsc', parts, codes_low)
        row_square = jnp.sum(parts * parts, axis=-1)[..., None]
        logits = -0.125 * (row_square - 2.0 * inner + code_square[None])
        weights = jax.nn.softmax(logits, axis=-1).astype(jnp.bfloat16).astype(jnp.float32)
        rebuilt = jnp.einsum('bsc,sck->bsk', weights, codes_low).astype(jnp.bfloat16).reshape(block_rows, DIM)
        sums = sums + jnp.einsum('bsc,bsk->sck', weights, parts)
        counts = counts + jnp.sum(weights, axis=0)
        cross = cross + jnp.dot(sample_block.T, rebuilt, preferred_element_type=jnp.float32)
        return (sums, counts, cross), rebuilt

    start = (jnp.zeros((SUBS, CODES, SUB_DIM), jnp.float32), jnp.zeros((SUBS, CODES), jnp.float32), jnp.zeros((DIM, DIM), jnp.float32))
    (sums, counts, cross), rebuilt = jax.lax.scan(step, start, samples.reshape(count_blocks, block_rows, DIM))
    new_codebook = (sums + codebook) / (counts[..., None] + 1.0)
    return rebuilt.reshape(total_rows, DIM), new_codebook, cross
```

```python
import functools

import jax
import jax.numpy as jnp
from jax import lax
from jax.experimental import pallas as pl
from jax.experimental.pallas import tpu as pltpu
from jax.sharding import Mesh
from jax.sharding import PartitionSpec as P

SIZES = (8, 2, 2, 2, 4, 2)
NAMES = ("z", "xh", "core", "xl", "yh", "yl")
DP = ("z", "xh", "core")
SUB = ("xl", "yh", "yl")
TEAM = ("core", "xl", "yl")
TEAMS = ("z", "xh", "yh")
BF = jnp.bfloat16
F32 = jnp.float32
NT = (((1,), (1,)), ((), ()))
VMEM = pl.BlockSpec(memory_space=pltpu.VMEM)
SMEM = pl.BlockSpec(memory_space=pltpu.SMEM)


def half_mask(shape):
    return lax.broadcasted_iota(jnp.int32, shape, len(shape) - 1) < 64


def swap_halves(x):
    return pltpu.roll(x, 64, 1)


def pack_kernel(turn_t, codes_t, pack):
    codes = codes_t[...]
    square = jnp.sum(codes * codes, axis=0, keepdims=True)
    high = square.astype(BF).astype(F32)
    mid = (square - high).astype(BF).astype(F32)
    low = square - high - mid
    pack[0:64, 0:1024] = turn_t[...]
    pack[0:64, 1024:] = codes.astype(BF)
    pack[64:80, 0:1024] = jnp.zeros((16, 1024), BF)
    pack[64:80, 1024:] = jnp.concatenate([high, mid, low, jnp.zeros((13, 256), F32)], axis=0).astype(BF)


def assign_kernel(place, mine, other, first, second, send, recon, cross, sums):
    rows, chunk = 512, 256
    core, odd = place[0], place[1]
    w0, w1 = first[...], second[...]
    wa = jnp.where(odd == 0, w0, w1)
    wb = jnp.where(odd == 0, w1, w0)
    turn = jnp.concatenate([wa[:64, :1024], wb[:64, :1024]], axis=0)
    zero = jnp.zeros((64, 256), BF)
    codes_t = jnp.concatenate(
        [
            jnp.concatenate([wa[:64, 1024:], zero], axis=1),
            jnp.concatenate([zero, wb[:64, 1024:]], axis=1),
        ],
        axis=0,
    )
    squares = jnp.concatenate([wa[64:80, 1024:], wb[64:80, 1024:]], axis=1)
    left = jnp.concatenate(
        [codes_t * BF(-2.0), squares, jnp.zeros((112, 512), BF)], axis=0
    ).T
    lane = lax.broadcasted_iota(jnp.int32, (chunk, 128), 1)
    three = jnp.where(lane < 3, 1.0, 0.0).astype(BF)
    ones = jnp.ones((chunk, 128), BF)
    row8 = lax.broadcasted_iota(jnp.int32, (8, 128), 0)
    low = half_mask((8, 128))
    pick = jnp.where(low == (row8 == 0), 1.0, 0.0).astype(F32)
    for part, ref in enumerate((mine, other)):
        for c in range(rows // chunk):
            x = ref[c * chunk : (c + 1) * chunk, :]
            rot = lax.dot_general(x, turn, NT, preferred_element_type=F32).astype(BF)
            wide = rot.astype(F32)
            row_square = lax.dot_general(
                pick, wide * wide, NT, precision=lax.Precision.HIGHEST, preferred_element_type=F32
            )
            near = lax.dot_general(
                left, jnp.concatenate([rot, three], axis=1), NT, preferred_element_type=F32
            )
            parts = []
            for i in range(2):
                logits = -0.125 * (row_square[i : i + 1] + near[i * 256 : (i + 1) * 256])
                e = jnp.exp(logits - jnp.max(logits, axis=0, keepdims=True))
                parts.append((e * (1.0 / jnp.sum(e, axis=0, keepdims=True))).astype(BF))
            weights = jnp.concatenate(parts, axis=0)
            rebuilt = jnp.dot(codes_t, weights, preferred_element_type=F32).astype(BF)
            s = jnp.dot(weights, jnp.concatenate([rot, ones], axis=1), preferred_element_type=F32)
            k = jnp.dot(rebuilt, x, preferred_element_type=F32)
            if part == 0 and c == 0:
                sums[...] = s
                cross[...] = k
            else:
                sums[...] += s
                cross[...] += k
            block = (core if part == 0 else 1 - core) * 4 + c * 2
            back = rebuilt.T
            recon[block, 0:128, :] = back[:128]
            recon[block + 1, 0:128, :] = back[128:]
    recon[:, 128:144, :] = jnp.zeros((8, 16, 128), BF)
    r = lax.broadcasted_iota(jnp.int32, (128, 128), 0)
    wanted = (
        (r & 64) | ((r & 8) << 2) | ((r & 4) << 2) | ((r & 48) >> 2) | (r & 3)
    )
    order = jnp.where(lax.broadcasted_iota(jnp.int32, (128, 128), 1) == wanted, 1.0, 0.0).astype(BF)
    for z in range(8):
        piece = lax.dot_general(
            order, cross[:, z * 128 : (z + 1) * 128].astype(BF), NT, preferred_element_type=F32
        ).astype(BF)
        for t in range(8):
            send[z * 8 + t, 0:16, :] = piece[t * 16 : (t + 1) * 16]
    for i in range(2):
        for q in range(16):
            at = i * 256 + q * 16
            a, b = sums[at : at + 8, :128], sums[at + 8 : at + 16, :128]
            if i == 0:
                total = jnp.where(low, a, swap_halves(b))
            else:
                total = jnp.where(low, swap_halves(a), b)
            count = jnp.where(low, sums[at : at + 8, 128:], sums[at + 8 : at + 16, 128:])
            tile = jnp.concatenate([total, count], axis=0).astype(BF)
            send[q * 4 + i, 16:32, :] = tile
            send[q * 4 + i + 2, 16:32, :] = tile


def reduce_kernel(place, got, codes, recon_in, recon, new_codes):
    recon[:, 0:128, :] = recon_in[:, 0:128, :]
    total = jnp.sum(got[...].astype(F32), axis=0)
    cross = total[:16]
    high = cross.astype(BF)
    rest = (cross - high.astype(F32)).astype(BF)
    both = jnp.concatenate([high, rest], axis=0).astype(F32)
    for c in range(8):
        tile = jnp.concatenate(
            [both[2 * c : 2 * c + 2], both[16 + 2 * c : 18 + 2 * c], jnp.zeros((12, 128), F32)], axis=0
        )
        recon[c, 128:144, :] = tile.astype(BF)
    at = pl.multiple_of(place[0] * 16, 16)
    own = codes[pl.ds(at, 16), :]
    own = jnp.concatenate([own[:8], own[8:]], axis=1)
    fresh = (total[16:24] + own) / (total[24:32] + 1.0)
    for c in range(32):
        new_codes[c] = fresh


def finish_kernel(got, recon, cross):
    low = half_mask((144, 128))
    for xl in range(2):
        for core in range(2):
            a = got[core * 4 + xl * 2].astype(F32)
            b = got[core * 4 + xl * 2 + 1].astype(F32)
            at = (xl * 2 + core) * 256
            for i in range(2):
                if i == 0:
                    t = jnp.where(low, a, swap_halves(b))
                else:
                    t = jnp.where(low, swap_halves(a), b)
                recon[:, at + i * 128 : at + (i + 1) * 128] = t[:128].astype(BF)
                cross[:, at + i * 128 : at + (i + 1) * 128] = t[128:130] + t[130:132]


def per_device(samples, rotation, codebook):
    core, yh = lax.axis_index("core"), lax.axis_index("yh")
    codes_t = codebook[0].T
    pack = pl.pallas_call(
        pack_kernel,
        out_shape=jax.ShapeDtypeStruct((80, 1280), BF),
        in_specs=[VMEM] * 2,
        out_specs=VMEM,
        name="pack",
    )(rotation.T, codes_t)
    packs = []
    for p in range(2):
        pairs = [
            (c * 4 + y, (y >> 1) * 4 + 2 * c + ((y & 1) ^ p)) for c in range(2) for y in range(4)
        ]
        packs.append(lax.ppermute(pack, ("core", "yh"), pairs))
    mine = lax.all_to_all(
        jnp.broadcast_to(samples[None], (4, 128, 1024)), ("xl", "yl"), 0, 0, tiled=True
    ).reshape(512, 1024)
    mine, *packs = lax.optimization_barrier((mine, *packs))
    other = lax.ppermute(mine, "core", [(0, 1), (1, 0)])
    place = jnp.stack([core, yh & 1]).astype(jnp.int32)
    send, recon = pl.pallas_call(
        assign_kernel,
        out_shape=(
            jax.ShapeDtypeStruct((64, 32, 128), BF),
            jax.ShapeDtypeStruct((8, 144, 128), BF),
        ),
        in_specs=[SMEM] + [VMEM] * 4,
        out_specs=(VMEM, VMEM),
        scratch_shapes=[pltpu.VMEM((128, 1024), F32), pltpu.VMEM((512, 256), F32)],
        compiler_params=pltpu.CompilerParams(vmem_limit_bytes=40 * 1024 * 1024),
        name="assign",
    )(place, mine, other, packs[0], packs[1])
    got = lax.all_to_all(send, TEAMS, 0, 0, tiled=True)
    chunk = (lax.axis_index("z") * 2 + lax.axis_index("xh")).astype(jnp.int32).reshape(1)
    recon, fresh = pl.pallas_call(
        reduce_kernel,
        out_shape=(
            jax.ShapeDtypeStruct((8, 144, 128), BF),
            jax.ShapeDtypeStruct((32, 8, 128), F32),
        ),
        in_specs=[SMEM] + [VMEM] * 3,
        out_specs=(VMEM, VMEM),
        compiler_params=pltpu.CompilerParams(vmem_limit_bytes=40 * 1024 * 1024),
        name="reduce",
    )(chunk, got, codebook[0], recon)
    back = lax.all_to_all(recon, TEAM, 0, 0, tiled=True)
    spread = lax.all_to_all(fresh, DP, 0, 0, tiled=True)
    recon, cross = pl.pallas_call(
        finish_kernel,
        out_shape=(
            jax.ShapeDtypeStruct((128, 1024), BF),
            jax.ShapeDtypeStruct((2, 1024), F32),
        ),
        in_specs=[VMEM],
        out_specs=(VMEM, VMEM),
        compiler_params=pltpu.CompilerParams(vmem_limit_bytes=40 * 1024 * 1024),
        name="finish",
    )(back)
    spread = lax.dynamic_index_in_dim(spread.reshape(16, 2, 8, 128), yh >> 1, 1, keepdims=False)
    new_codes = spread.reshape(16, 8, 2, 64).transpose(0, 2, 1, 3).reshape(1, 256, 64)
    return recon, new_codes, cross


def solution(mesh):
    fine = Mesh(mesh.devices.reshape(SIZES), NAMES)
    rows = P(DP + SUB, None)
    return jax.shard_map(
        per_device,
        mesh=fine,
        in_specs=(rows, P(None, SUB), P(SUB, None, None)),
        out_specs=(rows, P(SUB, None, None), rows),
        check_vma=False,
    )
```

```python
import functools

import jax
import jax.numpy as jnp
from jax import lax
from jax.experimental import pallas as pl
from jax.experimental.pallas import tpu as pltpu
from jax.sharding import Mesh
from jax.sharding import PartitionSpec as P

SIZES = (8, 2, 2, 2, 4, 2)
NAMES = ("z", "xh", "core", "xl", "yh", "yl")
DP = ("z", "xh", "core")
SUB = ("xl", "yh", "yl")
TEAM = ("core", "xl", "yl")
TEAMS = ("z", "xh", "yh")
BF = jnp.bfloat16
F32 = jnp.float32
NT = (((1,), (1,)), ((), ()))
VMEM = pl.BlockSpec(memory_space=pltpu.VMEM)
SMEM = pl.BlockSpec(memory_space=pltpu.SMEM)


def half_mask(shape):
    return lax.broadcasted_iota(jnp.int32, shape, len(shape) - 1) < 64


def swap_halves(x):
    return pltpu.roll(x, 64, 1)


def pack_kernel(turn_t, codes_t, pack):
    codes = codes_t[...]
    square = jnp.sum(codes * codes, axis=0, keepdims=True)
    high = square.astype(BF).astype(F32)
    mid = (square - high).astype(BF).astype(F32)
    low = square - high - mid
    pack[0:64, 0:1024] = turn_t[...]
    pack[0:64, 1024:] = codes.astype(BF)
    pack[64:80, 0:1024] = jnp.zeros((16, 1024), BF)
    pack[64:80, 1024:] = jnp.concatenate([high, mid, low, jnp.zeros((13, 256), F32)], axis=0).astype(BF)


def prepare_kernel(place, first, second, turn, codes_t, left):
    odd = place[1]
    w0, w1 = first[...], second[...]
    wa = jnp.where(odd == 0, w0, w1)
    wb = jnp.where(odd == 0, w1, w0)
    turn[0:64, :] = wa[:64, :1024]
    turn[64:128, :] = wb[:64, :1024]
    zero = jnp.zeros((64, 256), BF)
    both = jnp.concatenate(
        [
            jnp.concatenate([wa[:64, 1024:], zero], axis=1),
            jnp.concatenate([zero, wb[:64, 1024:]], axis=1),
        ],
        axis=0,
    )
    codes_t[...] = both
    squares = jnp.concatenate([wa[64:80, 1024:], wb[64:80, 1024:]], axis=1)
    left[...] = jnp.concatenate([both * BF(-2.0), squares, jnp.zeros((112, 512), BF)], axis=0).T


def assign_rows(samples, turn, codes_t, left, sums, cross, first, put):
    rows, chunk = 512, 256
    lane = lax.broadcasted_iota(jnp.int32, (chunk, 128), 1)
    three = jnp.where(lane < 3, 1.0, 0.0).astype(BF)
    ones = jnp.ones((chunk, 128), BF)
    row8 = lax.broadcasted_iota(jnp.int32, (8, 128), 0)
    pick = jnp.where(half_mask((8, 128)) == (row8 == 0), 1.0, 0.0).astype(F32)
    for c in range(rows // chunk):
        x = samples[c * chunk : (c + 1) * chunk, :]
        rot = lax.dot_general(x, turn[...], NT, preferred_element_type=F32).astype(BF)
        wide = rot.astype(F32)
        row_square = lax.dot_general(
            pick, wide * wide, NT, precision=lax.Precision.HIGHEST, preferred_element_type=F32
        )
        near = lax.dot_general(
            left[...], jnp.concatenate([rot, three], axis=1), NT, preferred_element_type=F32
        )
        parts = []
        for i in range(2):
            logits = -0.125 * (row_square[i : i + 1] + near[i * 256 : (i + 1) * 256])
            e = jnp.exp(logits - jnp.max(logits, axis=0, keepdims=True))
            parts.append((e * (1.0 / jnp.sum(e, axis=0, keepdims=True))).astype(BF))
        weights = jnp.concatenate(parts, axis=0)
        rebuilt = jnp.dot(codes_t[...], weights, preferred_element_type=F32).astype(BF)
        s = jnp.dot(weights, jnp.concatenate([rot, ones], axis=1), preferred_element_type=F32)
        k = jnp.dot(rebuilt, x, preferred_element_type=F32)
        if first and c == 0:
            sums[...] = s
            cross[...] = k
        else:
            sums[...] += s
            cross[...] += k
        back = rebuilt.T
        put(2 * c, back[:128])
        put(2 * c + 1, back[128:])


def early_kernel(samples, turn, codes_t, left, sums, cross, recon):
    def put(block, tile):
        recon[block] = tile

    assign_rows(samples, turn, codes_t, left, sums, cross, True, put)


def late_kernel(
    place, samples, turn, codes_t, left, sums_in, cross_in, recon_in, send, recon, sums, cross
):
    core = place[0]
    sums[...] = sums_in[...]
    cross[...] = cross_in[...]

    def put(block, tile):
        recon[(1 - core) * 4 + block, 0:128, :] = tile

    assign_rows(samples, turn, codes_t, left, sums, cross, False, put)
    for block in range(4):
        recon[core * 4 + block, 0:128, :] = recon_in[block]
    recon[:, 128:144, :] = jnp.zeros((8, 16, 128), BF)
    r = lax.broadcasted_iota(jnp.int32, (128, 128), 0)
    wanted = (r & 64) | ((r & 8) << 2) | ((r & 4) << 2) | ((r & 48) >> 2) | (r & 3)
    order = jnp.where(lax.broadcasted_iota(jnp.int32, (128, 128), 1) == wanted, 1.0, 0.0).astype(BF)
    for z in range(8):
        piece = lax.dot_general(
            order, cross[:, z * 128 : (z + 1) * 128].astype(BF), NT, preferred_element_type=F32
        ).astype(BF)
        for t in range(8):
            send[z * 8 + t, 0:16, :] = piece[t * 16 : (t + 1) * 16]
    low = half_mask((8, 128))
    for i in range(2):
        for q in range(16):
            at = i * 256 + q * 16
            a, b = sums[at : at + 8, :128], sums[at + 8 : at + 16, :128]
            if i == 0:
                total = jnp.where(low, a, swap_halves(b))
            else:
                total = jnp.where(low, swap_halves(a), b)
            count = jnp.where(low, sums[at : at + 8, 128:], sums[at + 8 : at + 16, 128:])
            tile = jnp.concatenate([total, count], axis=0).astype(BF)
            send[q * 4 + i, 16:32, :] = tile
            send[q * 4 + i + 2, 16:32, :] = tile


def reduce_kernel(place, got, codes, recon_in, recon):
    total = jnp.sum(got[...].astype(F32), axis=0)
    cross = total[:16]
    high = cross.astype(BF)
    rest = (cross - high.astype(F32)).astype(BF)
    both = jnp.concatenate([high, rest], axis=0).astype(F32)
    at = pl.multiple_of(place[0] * 16, 16)
    own = codes[pl.ds(at, 16), :]
    own = jnp.concatenate([own[:8], own[8:]], axis=1)
    fresh = (total[16:24] + own) / (total[24:32] + 1.0)
    for c in range(8):
        recon[c, 0:128, :] = recon_in[c, 0:128, :]
        tile = jnp.concatenate(
            [both[2 * c : 2 * c + 2], both[16 + 2 * c : 18 + 2 * c], jnp.zeros((4, 128), F32), fresh],
            axis=0,
        )
        recon[c, 128:144, :] = tile.astype(BF)


def pick_kernel(place, got, spread):
    tile = got[place[0], 128:144, :]
    for q in range(16):
        spread[q] = tile


def finish_kernel(got, recon, cross):
    low = half_mask((144, 128))
    for xl in range(2):
        for core in range(2):
            a = got[core * 4 + xl * 2].astype(F32)
            b = got[core * 4 + xl * 2 + 1].astype(F32)
            at = (xl * 2 + core) * 256
            for i in range(2):
                if i == 0:
                    t = jnp.where(low, a, swap_halves(b))
                else:
                    t = jnp.where(low, swap_halves(a), b)
                recon[:, at + i * 128 : at + (i + 1) * 128] = t[:128].astype(BF)
                cross[:, at + i * 128 : at + (i + 1) * 128] = t[128:130] + t[130:132]


def codes_kernel(got, codes_t):
    tiles = []
    for q in range(16):
        t = got[q].astype(F32)[8:]
        tiles += [t, swap_halves(t)]
    codes_t[...] = jnp.concatenate(tiles, axis=0).T[:64]


def call(kernel, name, outs, args, flops=0, moved=0, scratch=()):
    return pl.pallas_call(
        kernel,
        out_shape=tuple(jax.ShapeDtypeStruct(*o) for o in outs),
        in_specs=[SMEM if a.ndim == 1 else VMEM for a in args],
        out_specs=(VMEM,) * len(outs),
        scratch_shapes=list(scratch),
        compiler_params=pltpu.CompilerParams(vmem_limit_bytes=40 * 1024 * 1024),
        cost_estimate=pl.CostEstimate(flops=flops, bytes_accessed=moved, transcendentals=0),
        name=name,
    )(*args)


def per_device(samples, rotation, codebook):
    core, yh = lax.axis_index("core"), lax.axis_index("yh")
    codes_t = codebook[0].T
    pack = pl.pallas_call(
        pack_kernel,
        out_shape=jax.ShapeDtypeStruct((80, 1280), BF),
        in_specs=[VMEM] * 2,
        out_specs=VMEM,
        name="pack",
    )(rotation.T, codes_t)
    packs = []
    for p in range(2):
        pairs = [
            (c * 4 + y, (y >> 1) * 4 + 2 * c + ((y & 1) ^ p)) for c in range(2) for y in range(4)
        ]
        packs.append(lax.ppermute(pack, ("core", "yh"), pairs))
    mine = lax.all_to_all(
        jnp.broadcast_to(samples[None], (4, 128, 1024)), ("xl", "yl"), 0, 0, tiled=True
    ).reshape(512, 1024)
    place = jnp.stack([core, yh & 1]).astype(jnp.int32)
    tools = call(
        prepare_kernel,
        "prepare",
        [((128, 1024), BF), ((128, 512), BF), ((512, 256), BF)],
        (place, *packs),
        moved=300_000_000,
    )
    mine, *tools = lax.optimization_barrier((mine, *tools))
    other = lax.ppermute(mine, "core", [(0, 1), (1, 0)])
    sums, cross, early = call(
        early_kernel,
        "early",
        [((512, 256), F32), ((128, 1024), F32), ((4, 128, 128), BF)],
        (mine, *tools),
        moved=8_000_000,
    )
    send, recon = call(
        late_kernel,
        "late",
        [((64, 32, 128), BF), ((8, 144, 128), BF)],
        (place, other, *tools, sums, cross, early),
        moved=8_000_000,
        scratch=[pltpu.VMEM((512, 256), F32), pltpu.VMEM((128, 1024), F32)],
    )
    got = lax.all_to_all(send, TEAMS, 0, 0, tiled=True)
    chunk = (lax.axis_index("z") * 2 + lax.axis_index("xh")).astype(jnp.int32).reshape(1)
    (recon,) = call(
        reduce_kernel, "reduce", [((8, 144, 128), BF)], (chunk, got, codebook[0], recon)
    )
    back = lax.all_to_all(recon, TEAM, 0, 0, tiled=True)
    source = (yh >> 1) * 4 + lax.axis_index("xl") * 2 + lax.axis_index("yl")
    (spread,) = call(
        pick_kernel, "pick", [((16, 16, 128), BF)], (source.astype(jnp.int32).reshape(1), back)
    )
    spread = lax.all_to_all(spread, ("z", "xh"), 0, 0, tiled=True)
    recon, cross = call(finish_kernel, "finish", [((128, 1024), BF), ((2, 1024), F32)], (back,))
    (new_codes,) = call(codes_kernel, "codes", [((64, 256), F32)], (spread,))
    return recon, new_codes.T[None], cross


def solution(mesh):
    fine = Mesh(mesh.devices.reshape(SIZES), NAMES)
    rows = P(DP + SUB, None)
    return jax.shard_map(
        per_device,
        mesh=fine,
        in_specs=(rows, P(None, SUB), P(SUB, None, None)),
        out_specs=(rows, P(SUB, None, None), rows),
        check_vma=False,
    )
```

```python
import functools

import jax
import jax.numpy as jnp
from jax import lax
from jax.experimental import pallas as pl
from jax.experimental.pallas import tpu as pltpu
from jax.sharding import Mesh
from jax.sharding import PartitionSpec as P

SIZES = (4, 2, 2, 2, 2, 8)
NAMES = ("zh", "zl", "xh", "core", "xl", "y")
DP = ("zh", "zl", "xh", "core")
SUB = ("xl", "y")
TEAM = ("zl", "core", "xl")
FAR = ("zh", "xh")
BF = jnp.bfloat16
F32 = jnp.float32
NT = (((1,), (1,)), ((), ()))
VMEM = pl.BlockSpec(memory_space=pltpu.VMEM)
SMEM = pl.BlockSpec(memory_space=pltpu.SMEM)


def half_mask(shape):
    return lax.broadcasted_iota(jnp.int32, shape, len(shape) - 1) < 64


def swap_halves(x):
    return pltpu.roll(x, 64, 1)


def pack_kernel(turn_t, codes_t, pack):
    codes = codes_t[...]
    square = jnp.sum(codes * codes, axis=0, keepdims=True)
    high = square.astype(BF).astype(F32)
    mid = (square - high).astype(BF).astype(F32)
    low = square - high - mid
    squares = jnp.concatenate([high, mid, low, jnp.zeros((13, 256), F32)], axis=0).astype(BF)
    pack[:, 0:1024] = turn_t[...]
    pack[:, 1024:1280] = codes.astype(BF)
    pack[0:16, 1280:] = squares[:, :128]
    pack[16:32, 1280:] = squares[:, 128:]
    pack[32:64, 1280:] = jnp.zeros((32, 128), BF)


def prepare_kernel(place, first, second, turn, codes_t, left):
    odd = place[1]
    w0, w1 = first[...], second[...]
    wa = jnp.where(odd == 0, w0, w1)
    wb = jnp.where(odd == 0, w1, w0)
    turn[0:64, :] = wa[:, :1024]
    turn[64:128, :] = wb[:, :1024]
    zero = jnp.zeros((64, 256), BF)
    both = jnp.concatenate(
        [
            jnp.concatenate([wa[:, 1024:1280], zero], axis=1),
            jnp.concatenate([zero, wb[:, 1024:1280]], axis=1),
        ],
        axis=0,
    )
    codes_t[...] = both
    squares = jnp.concatenate(
        [wa[0:16, 1280:], wa[16:32, 1280:], wb[0:16, 1280:], wb[16:32, 1280:]], axis=1
    )
    left[...] = jnp.concatenate([both * BF(-2.0), squares, jnp.zeros((112, 512), BF)], axis=0).T


def assign_rows(samples, turn, codes_t, left, sums, cross, first, put):
    rows, chunk = 512, 256
    lane = lax.broadcasted_iota(jnp.int32, (chunk, 128), 1)
    three = jnp.where(lane < 3, 1.0, 0.0).astype(BF)
    ones = jnp.ones((chunk, 128), BF)
    row8 = lax.broadcasted_iota(jnp.int32, (8, 128), 0)
    pick = jnp.where(half_mask((8, 128)) == (row8 == 0), 1.0, 0.0).astype(F32)
    for c in range(rows // chunk):
        x = samples[c * chunk : (c + 1) * chunk, :]
        rot = lax.dot_general(x, turn[...], NT, preferred_element_type=F32).astype(BF)
        wide = rot.astype(F32)
        row_square = lax.dot_general(
            pick, wide * wide, NT, precision=lax.Precision.HIGHEST, preferred_element_type=F32
        )
        near = lax.dot_general(
            left[...], jnp.concatenate([rot, three], axis=1), NT, preferred_element_type=F32
        )
        parts = []
        for i in range(2):
            logits = -0.125 * (row_square[i : i + 1] + near[i * 256 : (i + 1) * 256])
            e = jnp.exp(logits - jnp.max(logits, axis=0, keepdims=True))
            parts.append((e * (1.0 / jnp.sum(e, axis=0, keepdims=True))).astype(BF))
        weights = jnp.concatenate(parts, axis=0)
        rebuilt = jnp.dot(codes_t[...], weights, preferred_element_type=F32).astype(BF)
        s = jnp.dot(weights, jnp.concatenate([rot, ones], axis=1), preferred_element_type=F32)
        k = jnp.dot(rebuilt, x, preferred_element_type=F32)
        if first and c == 0:
            sums[...] = s
            cross[...] = k
        else:
            sums[...] += s
            cross[...] += k
        back = rebuilt.T
        put(2 * c, back[:128])
        put(2 * c + 1, back[128:])


def early_kernel(samples, turn, codes_t, left, sums, cross, recon):
    def put(block, tile):
        recon[block] = tile

    assign_rows(samples, turn, codes_t, left, sums, cross, True, put)


def late_kernel(
    place, samples, turn, codes_t, left, sums_in, cross_in, recon_in, send, recon, sums, cross
):
    core = place[0]
    sums[...] = sums_in[...]
    cross[...] = cross_in[...]

    def put(block, tile):
        recon[(block >> 1) * 4 + (1 - core) * 2 + (block & 1), 0:128, :] = tile

    assign_rows(samples, turn, codes_t, left, sums, cross, False, put)
    for block in range(4):
        recon[(block >> 1) * 4 + core * 2 + (block & 1), 0:128, :] = recon_in[block]
    recon[:, 128:160, :] = jnp.zeros((8, 32, 128), BF)
    r = lax.broadcasted_iota(jnp.int32, (256, 256), 0)
    wanted = (
        ((r & 8) << 4) | ((r & 128) >> 1) | ((r & 4) << 3) | ((r & 2) << 3) | ((r & 112) >> 3) | (r & 1)
    )
    order = jnp.where(lax.broadcasted_iota(jnp.int32, (256, 256), 1) == wanted, 1.0, 0.0).astype(BF)
    for zh in range(4):
        piece = lax.dot_general(
            order, cross[:, zh * 256 : (zh + 1) * 256].astype(BF), NT, preferred_element_type=F32
        ).astype(BF)
        send[zh * 2, 0:128, :] = piece[:128]
        send[zh * 2 + 1, 0:128, :] = piece[128:]
    low = half_mask((32, 128))
    even = (lax.broadcasted_iota(jnp.int32, (16, 128), 1) & 32) == 0
    for q in range(8):
        at = q * 32
        a, b = sums[at : at + 32, :], sums[256 + at : 288 + at, :]
        send[q, 128:160, :] = jnp.where(low, a[:, :128], b[:, :128]).astype(BF)
        count = jnp.where(low, a[:, 128:], b[:, 128:])
        send[q, 160:176, :] = jnp.where(even, count[:16], count[16:]).astype(BF)


def middle_kernel(got, send):
    total = jnp.sum(got[...].astype(F32), axis=0)
    sums, count = total[128:160], total[160:176]
    lane = lax.broadcasted_iota(jnp.int32, (16, 128), 1)
    low = half_mask((16, 128))
    halves = []
    for i in range(2):
        if i == 0:
            base = count
            tile = jnp.where(low, sums[:16], swap_halves(sums[16:]))
        else:
            base = swap_halves(count)
            tile = jnp.where(low, swap_halves(sums[:16]), sums[16:])
        wide = jnp.where(
            lane < 32, base, jnp.where(lane < 96, pltpu.roll(base, 32, 1), swap_halves(base))
        )
        halves.append(jnp.concatenate([tile, wide], axis=0).astype(BF))
    for y in range(8):
        send[y, 0:16, :] = total[y * 16 : y * 16 + 16].astype(BF)
        send[y, 16:48, :] = halves[y & 1]


def reduce_kernel(place, got, codes, recon_in, recon):
    total = jnp.sum(got[...].astype(F32), axis=0)
    cross = total[:16]
    high = cross.astype(BF)
    rest = (cross - high.astype(F32)).astype(BF)
    both = jnp.concatenate([high, rest], axis=0).astype(F32)
    at = pl.multiple_of(place[0] * 32, 32)
    own = codes[pl.ds(at, 32), :]
    own = jnp.concatenate([own[:16], own[16:]], axis=1)
    fresh = ((total[16:32] + own) / (total[32:48] + 1.0)).astype(BF)
    for c in range(8):
        recon[c, 0:128, :] = recon_in[c, 0:128, :]
        tile = jnp.concatenate(
            [both[2 * c : 2 * c + 2], both[16 + 2 * c : 18 + 2 * c], jnp.zeros((12, 128), F32)], axis=0
        )
        recon[c, 128:144, :] = tile.astype(BF)
        recon[c, 144:160, :] = fresh


def pick_kernel(place, got, spread):
    tile = got[place[0], 144:160, :]
    for q in range(8):
        spread[q] = tile


def finish_kernel(got, recon, cross):
    for c in range(8):
        zl, core, xl = c >> 2, (c >> 1) & 1, c & 1
        at = (xl * 4 + zl * 2 + core) * 128
        recon[:, at : at + 128] = got[c, 0:128, :]
        t = got[c, 128:144, :].astype(F32)
        cross[:, at : at + 128] = t[0:2] + t[2:4]


def codes_kernel(got, codes_t):
    tiles = []
    for q in range(8):
        t = got[q].astype(F32)
        tiles += [t, swap_halves(t)]
    codes_t[...] = jnp.concatenate(tiles, axis=0).T[:64]


def call(kernel, name, outs, args, flops=0, moved=0, scratch=()):
    return pl.pallas_call(
        kernel,
        out_shape=tuple(jax.ShapeDtypeStruct(*o) for o in outs),
        in_specs=[SMEM if a.ndim == 1 else VMEM for a in args],
        out_specs=(VMEM,) * len(outs),
        scratch_shapes=list(scratch),
        compiler_params=pltpu.CompilerParams(vmem_limit_bytes=40 * 1024 * 1024),
        cost_estimate=pl.CostEstimate(flops=flops, bytes_accessed=moved, transcendentals=0),
        name=name,
    )(*args)


def per_device(samples, rotation, codebook):
    core, xl, y = lax.axis_index("core"), lax.axis_index("xl"), lax.axis_index("y")
    (pack,) = call(pack_kernel, "pack", [((64, 1408), BF)], (rotation.T, codebook[0].T))
    packs = []
    for p in range(2):
        pairs = [(k * 8 + n, (n >> 1) * 8 + 2 * k + ((n & 1) ^ p)) for k in range(4) for n in range(8)]
        packs.append(lax.ppermute(pack, ("zl", "core", "y"), pairs))
    mine = lax.all_to_all(
        jnp.broadcast_to(samples[None], (4, 128, 1024)), ("zl", "xl"), 0, 0, tiled=True
    ).reshape(512, 1024)
    place = jnp.stack([core, y & 1]).astype(jnp.int32)
    tools = call(
        prepare_kernel,
        "prepare",
        [((128, 1024), BF), ((128, 512), BF), ((512, 256), BF)],
        (place, *packs),
    )
    mine, *tools = lax.optimization_barrier((mine, *tools))
    other = lax.ppermute(mine, "core", [(0, 1), (1, 0)])
    sums, cross, early = call(
        early_kernel,
        "early",
        [((512, 256), F32), ((128, 1024), F32), ((4, 128, 128), BF)],
        (mine, *tools),
        moved=8_000_000,
    )
    send, recon = call(
        late_kernel,
        "late",
        [((8, 176, 128), BF), ((8, 160, 128), BF)],
        (place, other, *tools, sums, cross, early),
        moved=8_000_000,
        scratch=[pltpu.VMEM((512, 256), F32), pltpu.VMEM((128, 1024), F32)],
    )
    got = lax.all_to_all(send, FAR, 0, 0, tiled=True)
    (send,) = call(middle_kernel, "middle", [((8, 48, 128), BF)], (got,))
    got = lax.all_to_all(send, "y", 0, 0, tiled=True)
    chunk = (lax.axis_index("zh") * 2 + lax.axis_index("xh")).astype(jnp.int32).reshape(1)
    (recon,) = call(
        reduce_kernel, "reduce", [((8, 160, 128), BF)], (chunk, got, codebook[0], recon)
    )
    back = lax.all_to_all(recon, TEAM, 0, 0, tiled=True)
    source = (y >> 1) * 2 + xl
    (spread,) = call(
        pick_kernel, "pick", [((8, 16, 128), BF)], (source.astype(jnp.int32).reshape(1), back)
    )
    spread = lax.all_to_all(spread, FAR, 0, 0, tiled=True)
    recon, cross = call(finish_kernel, "finish", [((128, 1024), BF), ((2, 1024), F32)], (back,))
    (new_codes,) = call(codes_kernel, "codes", [((64, 256), F32)], (spread,))
    return recon, new_codes.T[None], cross


def solution(mesh):
    fine = Mesh(mesh.devices.reshape(SIZES), NAMES)
    rows = P(DP + SUB, None)
    return jax.shard_map(
        per_device,
        mesh=fine,
        in_specs=(rows, P(None, SUB), P(SUB, None, None)),
        out_specs=(rows, P(SUB, None, None), rows),
        check_vma=False,
    )
```

```python
import functools

import jax
import jax.numpy as jnp
from jax import lax
from jax.experimental import pallas as pl
from jax.experimental.pallas import tpu as pltpu
from jax.sharding import Mesh
from jax.sharding import PartitionSpec as P

SIZES = (8, 2, 2, 2, 4, 2)
NAMES = ("z", "xh", "core", "xl", "yh", "yl")
DP = ("z", "xh", "core")
SUB = ("xl", "yh", "yl")
FAR = ("z", "xh")
NEAR = ("core", "xl", "yh", "yl")
BF = jnp.bfloat16
F32 = jnp.float32
NT = (((1,), (1,)), ((), ()))
VMEM = pl.BlockSpec(memory_space=pltpu.VMEM)
SMEM = pl.BlockSpec(memory_space=pltpu.SMEM)


def half_mask(shape):
    return lax.broadcasted_iota(jnp.int32, shape, len(shape) - 1) < 64


def swap_halves(x):
    return pltpu.roll(x, 64, 1)


def pack_kernel(turn_t, codes_t, pack):
    codes = codes_t[...]
    square = jnp.sum(codes * codes, axis=0, keepdims=True)
    high = square.astype(BF).astype(F32)
    mid = (square - high).astype(BF).astype(F32)
    low = square - high - mid
    squares = jnp.concatenate([high, mid, low, jnp.zeros((13, 256), F32)], axis=0).astype(BF)
    pack[:, 0:1024] = turn_t[...]
    pack[:, 1024:1280] = codes.astype(BF)
    pack[0:16, 1280:] = squares[:, :128]
    pack[16:32, 1280:] = squares[:, 128:]
    pack[32:64, 1280:] = jnp.zeros((32, 128), BF)


def prepare_kernel(place, first, second, turn, codes_t, left):
    odd = place[1]
    w0, w1 = first[...], second[...]
    wa = jnp.where(odd == 0, w0, w1)
    wb = jnp.where(odd == 0, w1, w0)
    turn[0:64, :] = wa[:, :1024]
    turn[64:128, :] = wb[:, :1024]
    zero = jnp.zeros((64, 256), BF)
    both = jnp.concatenate(
        [
            jnp.concatenate([wa[:, 1024:1280], zero], axis=1),
            jnp.concatenate([zero, wb[:, 1024:1280]], axis=1),
        ],
        axis=0,
    )
    codes_t[...] = both
    squares = jnp.concatenate(
        [wa[0:16, 1280:], wa[16:32, 1280:], wb[0:16, 1280:], wb[16:32, 1280:]], axis=1
    )
    left[...] = jnp.concatenate([both * BF(-2.0), squares, jnp.zeros((112, 512), BF)], axis=0).T


def assign_rows(samples, turn, codes_t, left, sums, cross, first, put):
    rows, chunk = 512, 256
    lane = lax.broadcasted_iota(jnp.int32, (chunk, 128), 1)
    three = jnp.where(lane < 3, 1.0, 0.0).astype(BF)
    ones = jnp.ones((chunk, 128), BF)
    row8 = lax.broadcasted_iota(jnp.int32, (8, 128), 0)
    pick = jnp.where(half_mask((8, 128)) == (row8 == 0), 1.0, 0.0).astype(F32)
    for c in range(rows // chunk):
        x = samples[c * chunk : (c + 1) * chunk, :]
        rot = lax.dot_general(x, turn[...], NT, preferred_element_type=F32).astype(BF)
        wide = rot.astype(F32)
        row_square = lax.dot_general(
            pick, wide * wide, NT, precision=lax.Precision.HIGHEST, preferred_element_type=F32
        )
        near = lax.dot_general(
            left[...], jnp.concatenate([rot, three], axis=1), NT, preferred_element_type=F32
        )
        parts = []
        for i in range(2):
            logits = -0.125 * (row_square[i : i + 1] + near[i * 256 : (i + 1) * 256])
            e = jnp.exp(logits - jnp.max(logits, axis=0, keepdims=True))
            parts.append((e * (1.0 / jnp.sum(e, axis=0, keepdims=True))).astype(BF))
        weights = jnp.concatenate(parts, axis=0)
        rebuilt = jnp.dot(codes_t[...], weights, preferred_element_type=F32).astype(BF)
        s = jnp.dot(weights, jnp.concatenate([rot, ones], axis=1), preferred_element_type=F32)
        k = jnp.dot(rebuilt, x, preferred_element_type=F32)
        if first and c == 0:
            sums[...] = s
            cross[...] = k
        else:
            sums[...] += s
            cross[...] += k
        back = rebuilt.T
        put(2 * c, back[:128])
        put(2 * c + 1, back[128:])


def early_kernel(samples, turn, codes_t, left, sums, cross, recon):
    def put(block, tile):
        recon[block] = tile

    assign_rows(samples, turn, codes_t, left, sums, cross, True, put)


def late_kernel(samples, turn, codes_t, left, sums_in, cross_in, send, recon, sums, cross):
    sums[...] = sums_in[...]
    cross[...] = cross_in[...]

    def put(block, tile):
        recon[block] = tile

    assign_rows(samples, turn, codes_t, left, sums, cross, False, put)
    eye = (
        lax.broadcasted_iota(jnp.int32, (128, 128), 0)
        == lax.broadcasted_iota(jnp.int32, (128, 128), 1)
    )
    eye = jnp.where(eye, 1.0, 0.0).astype(BF)
    for z in range(8):
        piece = lax.dot_general(
            eye, cross[:, z * 128 : (z + 1) * 128].astype(BF), NT, preferred_element_type=F32
        ).astype(BF)
        send[z * 2, 0:64, :] = piece[:64]
        send[z * 2 + 1, 0:64, :] = piece[64:]
    low = half_mask((16, 128))
    for q in range(16):
        at = q * 16
        a, b = sums[at : at + 16, :], sums[256 + at : 272 + at, :]
        send[q, 64:80, :] = jnp.where(low, a[:, :128], b[:, :128]).astype(BF)
        send[q, 80:96, :] = jnp.where(low, a[:, 128:], b[:, 128:]).astype(BF)


def split(x):
    high = x.astype(BF).astype(F32)
    return high, x - high


def middle_kernel(got, send):
    total = jnp.sum(got[...].astype(F32), axis=0)
    cross_high, cross_low = split(total[:64])
    sums, count = total[64:80], total[80:96]
    low = half_mask((8, 128))
    wide_low = half_mask((16, 128))
    lane = lax.broadcasted_iota(jnp.int32, (16, 128), 1)
    own = (lane >> 3) == lax.broadcasted_iota(jnp.int32, (16, 128), 0)
    turned = swap_halves(count)
    heads, tails = [], []
    for i in range(2):
        if i == 0:
            tail = jnp.where(low, sums[:8], swap_halves(sums[8:]))
            each = jnp.where(wide_low, count, turned)
        else:
            tail = jnp.where(low, swap_halves(sums[:8]), sums[8:])
            each = jnp.where(wide_low, turned, count)
        line_high, line_low = split(jnp.sum(jnp.where(own, each, 0.0), axis=0, keepdims=True))
        heads.append(jnp.concatenate([line_high, line_low, jnp.zeros((2, 128), F32)], axis=0))
        tails.append(tail)
    for d in range(32):
        i = (d >> 1) & 1
        send[d] = jnp.concatenate(
            [cross_high[2 * d : 2 * d + 2], cross_low[2 * d : 2 * d + 2], heads[i], tails[i]], axis=0
        ).astype(BF)


def reduce_kernel(place, got, codes, cross, spread):
    low = half_mask((2, 128))
    for xl in range(2):
        for core in range(2):
            ab = []
            for yl in range(2):
                t = jnp.zeros((16, 128), F32)
                for yh in range(4):
                    t += got[core * 16 + xl * 8 + yh * 2 + yl].astype(F32)
                ab.append(t[0:2] + t[2:4])
            a, b = ab
            at = (xl * 2 + core) * 256
            cross[:, at : at + 128] = jnp.where(low, a, swap_halves(b))
            cross[:, at + 128 : at + 256] = jnp.where(low, swap_halves(a), b)
    t = jnp.zeros((16, 128), F32)
    for yh in range(4):
        t += got[place[1] + yh * 2].astype(F32)
    lane = lax.broadcasted_iota(jnp.int32, (16, 128), 1)
    mine = (lane >> 3) == lax.broadcasted_iota(jnp.int32, (16, 128), 0)
    line = jnp.broadcast_to(t[4:5] + t[5:6], (16, 128))
    count = 0.125 * jnp.sum(jnp.where(mine, line, 0.0), axis=1, keepdims=True)
    count = jnp.where(half_mask((8, 128)), count[:8], count[8:])
    at = pl.multiple_of(place[0] * 16, 16)
    own = codes[pl.ds(at, 16), :]
    own = jnp.concatenate([own[:8], own[8:]], axis=1)
    fresh = (t[8:16] + own) / (count + 1.0)
    for q in range(16):
        spread[q] = fresh


def codes_kernel(got, codes_t):
    tiles = []
    for q in range(16):
        t = got[q]
        tiles += [t, swap_halves(t)]
    codes_t[...] = jnp.concatenate(tiles, axis=0).T[:64]


def second_kernel(place, early, got, send):
    xl = place[1]
    for yl in range(2):
        send[yl] = early[(1 - xl) * 2 + yl]
        send[2 + yl] = got[(1 - xl) * 2 + yl]


def third_kernel(place, early, got, got2, send):
    xl, yl = place[1], place[2]
    send[0] = early[xl * 2 + 1 - yl]
    send[1] = got[xl * 2 + 1 - yl]
    send[2] = got2[1 - yl]
    send[3] = got2[2 + 1 - yl]


def home_kernel(place, early, got, got2, got3, recon):
    core, xl, yl = place[0], place[1], place[2]
    low = half_mask((128, 128))
    here = [[early[xl * 2 + yl], got[xl * 2 + yl]], [got2[yl], got2[2 + yl]]]
    for across in range(2):
        for other in range(2):
            near = here[across][other].astype(F32)
            far = got3[across * 2 + other].astype(F32)
            a = jnp.where(yl == 0, near, far)
            b = jnp.where(yl == 0, far, near)
            side = (1 - xl) if across else xl
            half = (1 - core) if other else core
            at = pl.multiple_of((side * 2 + half) * 256, 256)
            recon[:, pl.ds(at, 128)] = jnp.where(low, a, swap_halves(b)).astype(BF)
            recon[:, pl.ds(at + 128, 128)] = jnp.where(low, swap_halves(a), b).astype(BF)


def call(kernel, name, outs, args, flops=0, moved=0, scratch=()):
    return pl.pallas_call(
        kernel,
        out_shape=tuple(jax.ShapeDtypeStruct(*o) for o in outs),
        in_specs=[SMEM if a.ndim == 1 else VMEM for a in args],
        out_specs=(VMEM,) * len(outs),
        scratch_shapes=list(scratch),
        compiler_params=pltpu.CompilerParams(vmem_limit_bytes=40 * 1024 * 1024),
        cost_estimate=pl.CostEstimate(flops=flops, bytes_accessed=moved, transcendentals=0),
        name=name,
    )(*args)


def per_device(samples, rotation, codebook):
    core, xl = lax.axis_index("core"), lax.axis_index("xl")
    yh, yl = lax.axis_index("yh"), lax.axis_index("yl")
    (pack,) = call(pack_kernel, "pack", [((64, 1408), BF)], (rotation.T, codebook[0].T))
    packs = []
    for p in range(2):
        pairs = [
            (c * 4 + y, (y >> 1) * 4 + 2 * c + ((y & 1) ^ p)) for c in range(2) for y in range(4)
        ]
        packs.append(lax.ppermute(pack, ("core", "yh"), pairs))
    mine = lax.all_to_all(
        jnp.broadcast_to(samples[None], (4, 128, 1024)), ("xl", "yl"), 0, 0, tiled=True
    ).reshape(512, 1024)
    tools = call(
        prepare_kernel,
        "prepare",
        [((128, 1024), BF), ((128, 512), BF), ((512, 256), BF)],
        (jnp.stack([core, yh & 1]).astype(jnp.int32), *packs),
    )
    mine, *tools = lax.optimization_barrier((mine, *tools))
    swap = [(0, 1), (1, 0)]
    other = lax.ppermute(mine, "core", swap)
    sums, cross, early = call(
        early_kernel,
        "early",
        [((512, 256), F32), ((128, 1024), F32), ((4, 128, 128), BF)],
        (mine, *tools),
        moved=8_000_000,
    )
    send, late = call(
        late_kernel,
        "late",
        [((16, 96, 128), BF), ((4, 128, 128), BF)],
        (other, *tools, sums, cross),
        moved=8_000_000,
        scratch=[pltpu.VMEM((512, 256), F32), pltpu.VMEM((128, 1024), F32)],
    )
    place = jnp.stack([core, xl, yl]).astype(jnp.int32)
    block = [((4, 128, 128), BF)]
    home = lax.ppermute(late, "core", swap)
    (second,) = call(second_kernel, "second", block, (place, early, home))
    home2 = lax.ppermute(second, "xl", swap)
    got = lax.all_to_all(send, FAR, 0, 0, tiled=True)
    got, home2 = lax.optimization_barrier((got, home2))
    (send,) = call(middle_kernel, "middle", [((32, 16, 128), BF)], (got,))
    (third,) = call(third_kernel, "third", block, (place, early, home, home2))
    home3 = lax.ppermute(third, "yl", swap)
    got = lax.all_to_all(send, NEAR, 0, 0, tiled=True)
    got, home3 = lax.optimization_barrier((got, home3))
    chunk = lax.axis_index("z") * 2 + lax.axis_index("xh")
    source = (yh >> 1) * 16 + xl * 8 + yl
    cross, spread = call(
        reduce_kernel,
        "reduce",
        [((2, 1024), F32), ((16, 8, 128), F32)],
        (jnp.stack([chunk, source]).astype(jnp.int32), got, codebook[0]),
    )
    spread = lax.all_to_all(spread, FAR, 0, 0, tiled=True)
    (recon,) = call(home_kernel, "home", [((128, 1024), BF)], (place, early, home, home2, home3))
    (new_codes,) = call(codes_kernel, "codes", [((64, 256), F32)], (spread,))
    return recon, new_codes.T[None], cross


def solution(mesh):
    fine = Mesh(mesh.devices.reshape(SIZES), NAMES)
    rows = P(DP + SUB, None)
    return jax.shard_map(
        per_device,
        mesh=fine,
        in_specs=(rows, P(None, SUB), P(SUB, None, None)),
        out_specs=(rows, P(SUB, None, None), rows),
        check_vma=False,
    )
```

```python
import functools

import jax
import jax.numpy as jnp
from jax import lax
from jax.experimental import pallas as pl
from jax.experimental.pallas import tpu as pltpu
from jax.sharding import Mesh
from jax.sharding import PartitionSpec as P

SIZES = (8, 2, 2, 2, 4, 2)
NAMES = ("z", "xh", "core", "xl", "yh", "yl")
DP = ("z", "xh", "core")
SUB = ("xl", "yh", "yl")
FAR = ("z", "xh")
NEAR = ("core", "xl", "yh", "yl")
BF = jnp.bfloat16
F32 = jnp.float32
NT = (((1,), (1,)), ((), ()))
VMEM = pl.BlockSpec(memory_space=pltpu.VMEM)
SMEM = pl.BlockSpec(memory_space=pltpu.SMEM)


def half_mask(shape):
    return lax.broadcasted_iota(jnp.int32, shape, len(shape) - 1) < 64


def swap_halves(x):
    return pltpu.roll(x, 64, 1)


def pack_kernel(turn_t, codes_t, pack):
    codes = codes_t[...]
    square = jnp.sum(codes * codes, axis=0, keepdims=True)
    high = square.astype(BF).astype(F32)
    mid = (square - high).astype(BF).astype(F32)
    low = square - high - mid
    squares = jnp.concatenate([high, mid, low, jnp.zeros((13, 256), F32)], axis=0).astype(BF)
    pack[:, 0:1024] = turn_t[...]
    pack[:, 1024:1280] = codes.astype(BF)
    pack[0:16, 1280:] = squares[:, :128]
    pack[16:32, 1280:] = squares[:, 128:]
    pack[32:64, 1280:] = jnp.zeros((32, 128), BF)


def prepare_kernel(place, pack, first, second, turn, codes_t, left):
    core, yl = place[0], place[3]
    w0, w1, w2 = pack[...], first[...], second[...]
    wa = jnp.where(core == 0, w0, jnp.where(yl == 0, w2, w1))
    wb = jnp.where(core == 0, w1, jnp.where(yl == 0, w1, w2))
    turn[0:64, :] = wa[:, :1024]
    turn[64:128, :] = wb[:, :1024]
    zero = jnp.zeros((64, 256), BF)
    both = jnp.concatenate(
        [
            jnp.concatenate([wa[:, 1024:1280], zero], axis=1),
            jnp.concatenate([zero, wb[:, 1024:1280]], axis=1),
        ],
        axis=0,
    )
    codes_t[...] = both
    squares = jnp.concatenate(
        [wa[0:16, 1280:], wa[16:32, 1280:], wb[0:16, 1280:], wb[16:32, 1280:]], axis=1
    )
    left[...] = jnp.concatenate([both * BF(-2.0), squares, jnp.zeros((112, 512), BF)], axis=0).T


def assign_rows(samples, turn, codes_t, left, sums, cross, first, put):
    rows, chunk = 512, 256
    lane = lax.broadcasted_iota(jnp.int32, (chunk, 128), 1)
    three = jnp.where(lane < 3, 1.0, 0.0).astype(BF)
    ones = jnp.ones((chunk, 128), BF)
    row8 = lax.broadcasted_iota(jnp.int32, (8, 128), 0)
    pick = jnp.where(half_mask((8, 128)) == (row8 == 0), 1.0, 0.0).astype(F32)
    for c in range(rows // chunk):
        x = samples[c * chunk : (c + 1) * chunk, :]
        rot = lax.dot_general(x, turn[...], NT, preferred_element_type=F32).astype(BF)
        wide = rot.astype(F32)
        row_square = lax.dot_general(
            pick, wide * wide, NT, precision=lax.Precision.HIGHEST, preferred_element_type=F32
        )
        near = lax.dot_general(
            left[...], jnp.concatenate([rot, three], axis=1), NT, preferred_element_type=F32
        )
        parts = []
        for i in range(2):
            logits = -0.125 * (row_square[i : i + 1] + near[i * 256 : (i + 1) * 256])
            e = jnp.exp(logits - jnp.max(logits, axis=0, keepdims=True))
            parts.append((e * (1.0 / jnp.sum(e, axis=0, keepdims=True))).astype(BF))
        weights = jnp.concatenate(parts, axis=0)
        rebuilt = jnp.dot(codes_t[...], weights, preferred_element_type=F32).astype(BF)
        s = jnp.dot(weights, jnp.concatenate([rot, ones], axis=1), preferred_element_type=F32)
        k = jnp.dot(rebuilt, x, preferred_element_type=F32)
        if first and c == 0:
            sums[...] = s
            cross[...] = k
        else:
            sums[...] += s
            cross[...] += k
        back = rebuilt.T
        put(2 * c, back[:128])
        put(2 * c + 1, back[128:])


def early_kernel(samples, turn, codes_t, left, sums, cross, recon):
    def put(block, tile):
        recon[block] = tile

    assign_rows(samples, turn, codes_t, left, sums, cross, True, put)


def late_kernel(
    place, samples, turn, codes_t, left, sums_in, cross_in, early, send, recon, give, sums, cross
):
    sums[...] = sums_in[...]
    cross[...] = cross_in[...]

    def put(block, tile):
        recon[block] = tile

    assign_rows(samples, turn, codes_t, left, sums, cross, False, put)
    xl = place[1]
    for yl in range(2):
        give[yl] = early[(1 - xl) * 2 + yl]
        give[2 + yl] = recon[(1 - xl) * 2 + yl]
    eye = (
        lax.broadcasted_iota(jnp.int32, (128, 128), 0)
        == lax.broadcasted_iota(jnp.int32, (128, 128), 1)
    )
    eye = jnp.where(eye, 1.0, 0.0).astype(BF)
    for z in range(8):
        piece = lax.dot_general(
            eye, cross[:, z * 128 : (z + 1) * 128].astype(BF), NT, preferred_element_type=F32
        ).astype(BF)
        send[z * 2, 0:64, :] = piece[:64]
        send[z * 2 + 1, 0:64, :] = piece[64:]
    low = half_mask((16, 128))
    for q in range(16):
        at = q * 16
        a, b = sums[at : at + 16, :], sums[256 + at : 272 + at, :]
        send[q, 64:80, :] = jnp.where(low, a[:, :128], b[:, :128]).astype(BF)
        send[q, 80:96, :] = jnp.where(low, a[:, 128:], b[:, 128:]).astype(BF)


def split(x):
    high = x.astype(BF).astype(F32)
    return high, x - high


def middle_kernel(place, got, send):
    total = jnp.sum(got[...].astype(F32), axis=0)
    cross_high, cross_low = split(total[:64])
    sums, count = total[64:80], total[80:96]
    low = half_mask((8, 128))
    wide_low = half_mask((16, 128))
    lane = lax.broadcasted_iota(jnp.int32, (16, 128), 1)
    own = (lane >> 3) == lax.broadcasted_iota(jnp.int32, (16, 128), 0)
    turned = swap_halves(count)
    heads, tails = [], []
    for i in range(2):
        if i == 0:
            tail = jnp.where(low, sums[:8], swap_halves(sums[8:]))
            each = jnp.where(wide_low, count, turned)
        else:
            tail = jnp.where(low, swap_halves(sums[:8]), sums[8:])
            each = jnp.where(wide_low, turned, count)
        line_high, line_low = split(jnp.sum(jnp.where(own, each, 0.0), axis=0, keepdims=True))
        heads.append(jnp.concatenate([line_high, line_low, jnp.zeros((2, 128), F32)], axis=0))
        tails.append(tail)
    core, yh, yl = place[0], place[2], place[3]
    last = jnp.where(core == 0, 5 - yl, 7 - 4 * yl)
    for y in range(8):
        is_last = ((y + 8 - 2 * yh) & 7) == last
        head = jnp.where(is_last, heads[1], heads[0])
        tail = jnp.where(is_last, tails[1], tails[0])
        for c in range(4):
            d = c * 8 + y
            send[d] = jnp.concatenate(
                [cross_high[2 * d : 2 * d + 2], cross_low[2 * d : 2 * d + 2], head, tail], axis=0
            ).astype(BF)


def arrange(low, a, b, c, d):
    turned = swap_halves(b)
    return [jnp.where(low, a, turned), d, jnp.where(low, turned, a), c]


def reduce_kernel(place, got, codes, cross, spread):
    low = half_mask((2, 128))
    for xl in range(2):
        total = [jnp.zeros((2, 128), F32)] * 4
        for yh in range(4):
            blocks = []
            for core in range(2):
                for yl in range(2):
                    t = got[core * 16 + xl * 8 + yh * 2 + yl].astype(F32)
                    blocks.append(t[0:2] + t[2:4])
            for p, tile in enumerate(arrange(low, *blocks)):
                total[(yh + p) & 3] += tile
        for p in range(4):
            at = (xl * 4 + p) * 128
            cross[:, at : at + 128] = total[p]
    my_xl, my_yh, my_yl = place[1], place[2], place[3]
    t = jnp.zeros((16, 128), F32)
    for yh in range(4):
        r = (2 * my_yh + my_yl + 8 - 2 * yh) & 7
        yl = jnp.where((r >= 1) & (r <= 4), 1, 0)
        t += got[((r >> 1) & 1) * 16 + my_xl * 8 + yh * 2 + yl].astype(F32)
    lane = lax.broadcasted_iota(jnp.int32, (16, 128), 1)
    mine = (lane >> 3) == lax.broadcasted_iota(jnp.int32, (16, 128), 0)
    line = jnp.broadcast_to(t[4:5] + t[5:6], (16, 128))
    count = 0.125 * jnp.sum(jnp.where(mine, line, 0.0), axis=1, keepdims=True)
    count = jnp.where(half_mask((8, 128)), count[:8], count[8:])
    at = pl.multiple_of(place[4] * 16, 16)
    own = codes[pl.ds(at, 16), :]
    own = jnp.concatenate([own[:8], own[8:]], axis=1)
    fresh = (t[8:16] + own) / (count + 1.0)
    for q in range(16):
        spread[q] = fresh


def codes_kernel(got, codes_t):
    tiles = []
    for q in range(16):
        t = got[q]
        tiles += [t, swap_halves(t)]
    codes_t[...] = jnp.concatenate(tiles, axis=0).T[:64]


def second_kernel(place, early, late, got, send):
    xl, yl = place[1], place[3]
    send[0] = early[xl * 2 + 1 - yl]
    send[1] = late[xl * 2 + 1 - yl]
    send[2] = got[1 - yl]
    send[3] = got[2 + 1 - yl]


def third_kernel(place, late, got, got2, send):
    xl, yl = place[1], place[3]
    send[0] = late[xl * 2 + yl]
    send[1] = got2[1]
    send[2] = got[2 + yl]
    send[3] = got2[3]


def home_kernel(place, early, got, got2, got3, recon):
    core, xl, yh, yl = place[0], place[1], place[2], place[3]
    low = half_mask((128, 128))
    same = [[early[xl * 2 + yl], got2[0]], [got[yl], got2[2]]]
    for across in range(2):
        mine = same[across]
        theirs = [got3[across * 2], got3[across * 2 + 1]]
        blocks = []
        for c in range(2):
            near = jnp.where(core == c, mine[0], theirs[0])
            far = jnp.where(core == c, mine[1], theirs[1])
            for y in range(2):
                blocks.append(jnp.where(yl == y, near, far).astype(F32))
        side = (1 - xl) if across else xl
        for p, tile in enumerate(arrange(low, *blocks)):
            at = pl.multiple_of((side * 4 + ((yh + p) & 3)) * 128, 128)
            recon[:, pl.ds(at, 128)] = tile.astype(BF)


def call(kernel, name, outs, args, flops=0, moved=0, scratch=()):
    return pl.pallas_call(
        kernel,
        out_shape=tuple(jax.ShapeDtypeStruct(*o) for o in outs),
        in_specs=[SMEM if a.ndim == 1 else VMEM for a in args],
        out_specs=(VMEM,) * len(outs),
        scratch_shapes=list(scratch),
        compiler_params=pltpu.CompilerParams(vmem_limit_bytes=40 * 1024 * 1024),
        cost_estimate=pl.CostEstimate(flops=flops, bytes_accessed=moved, transcendentals=0),
        name=name,
    )(*args)


def per_device(samples, rotation, codebook):
    core, xl = lax.axis_index("core"), lax.axis_index("xl")
    yh, yl = lax.axis_index("yh"), lax.axis_index("yl")
    chunk = lax.axis_index("z") * 2 + lax.axis_index("xh")
    place = jnp.stack([core, xl, yh, yl, chunk]).astype(jnp.int32)
    (pack,) = call(pack_kernel, "pack", [((64, 1408), BF)], (rotation.T, codebook[0].T))
    packs = []
    for steps in ((3, 1), (None, 2)):
        pairs = [
            (c * 8 + ((y + step if y & 1 else y - step) & 7), c * 8 + y)
            for c, step in enumerate(steps)
            for y in range(8)
            if step is not None
        ]
        packs.append(lax.ppermute(pack, ("core", "yh", "yl"), pairs))
    mine = lax.all_to_all(
        jnp.broadcast_to(samples[None], (4, 128, 1024)), ("xl", "yl"), 0, 0, tiled=True
    ).reshape(512, 1024)
    tools = call(
        prepare_kernel,
        "prepare",
        [((128, 1024), BF), ((128, 512), BF), ((512, 256), BF)],
        (place, pack, *packs),
    )
    mine, *tools = lax.optimization_barrier((mine, *tools))
    swap = [(0, 1), (1, 0)]
    other = lax.ppermute(mine, "core", swap)
    block = ((4, 128, 128), BF)
    sums, cross, early = call(
        early_kernel,
        "early",
        [((512, 256), F32), ((128, 1024), F32), block],
        (mine, *tools),
        moved=8_000_000,
    )
    send, late, give = call(
        late_kernel,
        "late",
        [((16, 96, 128), BF), block, block],
        (place, other, *tools, sums, cross, early),
        moved=8_000_000,
        scratch=[pltpu.VMEM((512, 256), F32), pltpu.VMEM((128, 1024), F32)],
    )
    home = lax.ppermute(give, "xl", swap)
    got = lax.all_to_all(send, FAR, 0, 0, tiled=True)
    got, home = lax.optimization_barrier((got, home))
    (send,) = call(middle_kernel, "middle", [((32, 16, 128), BF)], (place, got))
    (second,) = call(second_kernel, "second", [block], (place, early, late, home))
    home2 = lax.ppermute(second, "yl", swap)
    got = lax.all_to_all(send, NEAR, 0, 0, tiled=True)
    got, home2 = lax.optimization_barrier((got, home2))
    cross, spread = call(
        reduce_kernel,
        "reduce",
        [((2, 1024), F32), ((16, 8, 128), F32)],
        (place, got, codebook[0]),
    )
    spread = lax.all_to_all(spread, FAR, 0, 0, tiled=True)
    (third,) = call(third_kernel, "third", [block], (place, late, home, home2))
    home3 = lax.ppermute(third, "core", swap)
    (recon,) = call(home_kernel, "home", [((128, 1024), BF)], (place, early, home, home2, home3))
    spread, recon = lax.optimization_barrier((spread, recon))
    (new_codes,) = call(codes_kernel, "codes", [((64, 256), F32)], (spread,))
    return recon, new_codes.T[None], cross


def solution(mesh):
    fine = Mesh(mesh.devices.reshape(SIZES), NAMES)
    rows = P(DP + SUB, None)
    return jax.shard_map(
        per_device,
        mesh=fine,
        in_specs=(rows, P(None, SUB), P(SUB, None, None)),
        out_specs=(rows, P(SUB, None, None), rows),
        check_vma=False,
    )
```

```python
import functools

import jax
import jax.numpy as jnp
from jax import lax
from jax.experimental import pallas as pl
from jax.experimental.pallas import tpu as pltpu
from jax.sharding import Mesh
from jax.sharding import PartitionSpec as P

SIZES = (8, 2, 2, 2, 4, 2)
NAMES = ("z", "xh", "core", "xl", "yh", "yl")
DP = ("z", "xh", "core")
SUB = ("xl", "yh", "yl")
FAR = ("z", "xh")
NEAR = ("core", "xl", "yh", "yl")
BF = jnp.bfloat16
F32 = jnp.float32
NT = (((1,), (1,)), ((), ()))
VMEM = pl.BlockSpec(memory_space=pltpu.VMEM)
SMEM = pl.BlockSpec(memory_space=pltpu.SMEM)


def half_mask(shape):
    return lax.broadcasted_iota(jnp.int32, shape, len(shape) - 1) < 64


def swap_halves(x):
    return pltpu.roll(x, 64, 1)


def split(x):
    high = x.astype(BF).astype(F32)
    return high, x - high


def open_kernel(samples, turn_t, codes_t, pack, copies):
    for n in range(4):
        copies[n] = samples[...]
    codes = codes_t[...]
    square = jnp.sum(codes * codes, axis=0, keepdims=True)
    high = square.astype(BF).astype(F32)
    mid = (square - high).astype(BF).astype(F32)
    low = square - high - mid
    squares = jnp.concatenate([high, mid, low, jnp.zeros((13, 256), F32)], axis=0).astype(BF)
    pack[:, 0:1024] = turn_t[...]
    pack[:, 1024:1280] = codes.astype(BF)
    pack[0:16, 1280:] = squares[:, :128]
    pack[16:32, 1280:] = squares[:, 128:]
    pack[32:64, 1280:] = jnp.zeros((32, 128), BF)


def prepare_kernel(place, pack, first, second, turn, codes_t, left):
    core, yl = place[0], place[3]
    w0, w1, w2 = pack[...], first[...], second[...]
    wa = jnp.where(core == 0, w0, jnp.where(yl == 0, w2, w1))
    wb = jnp.where(core == 0, w1, jnp.where(yl == 0, w1, w2))
    turn[0:64, :] = wa[:, :1024]
    turn[64:128, :] = wb[:, :1024]
    zero = jnp.zeros((64, 256), BF)
    both = jnp.concatenate(
        [
            jnp.concatenate([wa[:, 1024:1280], zero], axis=1),
            jnp.concatenate([zero, wb[:, 1024:1280]], axis=1),
        ],
        axis=0,
    )
    codes_t[...] = both
    squares = jnp.concatenate(
        [wa[0:16, 1280:], wa[16:32, 1280:], wb[0:16, 1280:], wb[16:32, 1280:]], axis=1
    )
    left[...] = jnp.concatenate([both * BF(-2.0), squares, jnp.zeros((112, 512), BF)], axis=0).T


def assign_rows(samples, turn, codes_t, left, sums, cross, put):
    rows, chunk = 512, 256
    lane = lax.broadcasted_iota(jnp.int32, (chunk, 128), 1)
    three = jnp.where(lane < 3, 1.0, 0.0).astype(BF)
    ones = jnp.ones((chunk, 128), BF)
    row16 = lax.broadcasted_iota(jnp.int32, (16, 256), 0)
    pick = (lax.broadcasted_iota(jnp.int32, (16, 256), 1) & 64) == 0
    pick = jnp.where(pick == (row16 == 0), 1.0, 0.0).astype(BF)
    for c in range(rows // chunk):
        x = samples[c * chunk : (c + 1) * chunk, :]
        rot = lax.dot_general(x, turn[...], NT, preferred_element_type=F32).astype(BF)
        square_high, square_low = split(jnp.square(rot.astype(F32)))
        square = jnp.concatenate([square_high, square_low], axis=1).astype(BF)
        row_square = lax.dot_general(pick, square, NT, preferred_element_type=F32)
        near = lax.dot_general(
            left[...], jnp.concatenate([rot, three], axis=1), NT, preferred_element_type=F32
        )
        parts = []
        for i in range(2):
            logits = -0.125 * (row_square[i : i + 1] + near[i * 256 : (i + 1) * 256])
            e = jnp.exp(logits - jnp.max(logits, axis=0, keepdims=True))
            parts.append((e * (1.0 / jnp.sum(e, axis=0, keepdims=True))).astype(BF))
        weights = jnp.concatenate(parts, axis=0)
        rebuilt = jnp.dot(codes_t[...], weights, preferred_element_type=F32).astype(BF)
        s = jnp.dot(weights, jnp.concatenate([rot, ones], axis=1), preferred_element_type=F32)
        k = jnp.dot(rebuilt, x, preferred_element_type=F32)
        sums = s if sums is None else sums + s
        cross = k if cross is None else cross + k
        back = rebuilt.T
        put(2 * c, back[:128])
        put(2 * c + 1, back[128:])
    return sums, cross


def early_kernel(samples, turn, codes_t, left, sums, cross, recon):
    def put(block, tile):
        recon[block] = tile

    sums[...], cross[...] = assign_rows(samples, turn, codes_t, left, None, None, put)


def late_kernel(
    place, samples, turn, codes_t, left, sums, cross, early, send, recon, give
):
    def put(block, tile):
        recon[block] = tile

    sums, cross = assign_rows(samples, turn, codes_t, left, sums[...], cross[...], put)
    cross = cross.astype(BF)
    xl = place[1]
    for yl in range(2):
        give[yl] = early[(1 - xl) * 2 + yl]
        give[2 + yl] = recon[(1 - xl) * 2 + yl]
    eye = (
        lax.broadcasted_iota(jnp.int32, (128, 128), 0)
        == lax.broadcasted_iota(jnp.int32, (128, 128), 1)
    )
    eye = jnp.where(eye, 1.0, 0.0).astype(BF)
    for z in range(8):
        piece = lax.dot_general(
            eye, cross[:, z * 128 : (z + 1) * 128], NT, preferred_element_type=F32
        ).astype(BF)
        send[z * 2, 0:64, :] = piece[:64]
        send[z * 2 + 1, 0:64, :] = piece[64:]
    low = half_mask((16, 128))
    even = (lax.broadcasted_iota(jnp.int32, (8, 128), 1) & 32) == 0
    for q in range(16):
        at = q * 16
        a, b = sums[at : at + 16, :], sums[256 + at : 272 + at, :]
        total = jnp.where(low, a[:, :128], b[:, :128])
        count = jnp.where(low, a[:, 128:], b[:, 128:])
        count = jnp.where(even, count[:8], count[8:])
        send[q, 64:88, :] = jnp.concatenate([total, count], axis=0).astype(BF)


def middle_kernel(place, got, send):
    total = jnp.sum(got[...].astype(F32), axis=0)
    cross_high, cross_low = split(total[:64])
    sums, count = total[64:80], total[80:88]
    low = half_mask((8, 128))
    row, lane = (lax.broadcasted_iota(jnp.int32, (8, 128), n) for n in range(2))
    turned = swap_halves(count)
    heads, tails = [], []
    for i in range(2):
        if i == 0:
            tail = jnp.where(low, sums[:8], swap_halves(sums[8:]))
            base = count
        else:
            tail = jnp.where(low, swap_halves(sums[:8]), sums[8:])
            base = turned
        each = jnp.where(
            lane < 32, base, jnp.where(lane < 96, pltpu.roll(base, 32, 1), swap_halves(base))
        )
        line = jnp.sum(jnp.where(((lane >> 3) & 7) == row, each, 0.0), axis=0, keepdims=True)
        line_high, line_low = split(line)
        heads.append(jnp.concatenate([line_high, line_low, jnp.zeros((2, 128), F32)], axis=0))
        tails.append(tail)
    core, yh, yl = place[0], place[2], place[3]
    last = jnp.where(core == 0, 5 - yl, 7 - 4 * yl)
    for y in range(8):
        is_last = ((y + 8 - 2 * yh) & 7) == last
        head = jnp.where(is_last, heads[1], heads[0])
        tail = jnp.where(is_last, tails[1], tails[0])
        for c in range(4):
            d = c * 8 + y
            send[d] = jnp.concatenate(
                [cross_high[2 * d : 2 * d + 2], cross_low[2 * d : 2 * d + 2], head, tail], axis=0
            ).astype(BF)


def arrange(low, a, b, c, d):
    turned = swap_halves(b)
    return [jnp.where(low, a, turned), d, jnp.where(low, turned, a), c]


def reduce_kernel(place, got, codes, cross, spread):
    low = half_mask((2, 128))
    for xl in range(2):
        total = [jnp.zeros((2, 128), F32)] * 4
        for yh in range(4):
            blocks = []
            for core in range(2):
                for yl in range(2):
                    t = got[core * 16 + xl * 8 + yh * 2 + yl].astype(F32)
                    blocks.append(t[0:2] + t[2:4])
            for p, tile in enumerate(arrange(low, *blocks)):
                total[(yh + p) & 3] += tile
        for p in range(4):
            at = (xl * 4 + p) * 128
            cross[:, at : at + 128] = total[p]
    my_xl, my_yh, my_yl = place[1], place[2], place[3]
    t = jnp.zeros((16, 128), F32)
    for yh in range(4):
        r = (2 * my_yh + my_yl + 8 - 2 * yh) & 7
        yl = jnp.where((r >= 1) & (r <= 4), 1, 0)
        t += got[((r >> 1) & 1) * 16 + my_xl * 8 + yh * 2 + yl].astype(F32)
    lane = lax.broadcasted_iota(jnp.int32, (16, 128), 1)
    mine = (lane >> 3) == lax.broadcasted_iota(jnp.int32, (16, 128), 0)
    line = jnp.broadcast_to(t[4:5] + t[5:6], (16, 128))
    count = 0.125 * jnp.sum(jnp.where(mine, line, 0.0), axis=1, keepdims=True)
    count = jnp.where(half_mask((8, 128)), count[:8], count[8:])
    at = pl.multiple_of(place[4] * 16, 16)
    own = codes[pl.ds(at, 16), :]
    own = jnp.concatenate([own[:8], own[8:]], axis=1)
    fresh = (t[8:16] + own) / (count + 1.0)
    for q in range(16):
        spread[q] = fresh


def codes_kernel(got, codes_t):
    tiles = []
    for q in range(16):
        t = got[q]
        tiles += [t, swap_halves(t)]
    codes_t[...] = jnp.concatenate(tiles, axis=0).T[:64]


def second_kernel(place, late, got, send):
    xl = place[1]
    for yl in range(2):
        send[yl] = late[xl * 2 + yl]
        send[2 + yl] = got[2 + yl]


def third_kernel(place, early, got, got2, send):
    xl, yl = place[1], place[3]
    send[0] = early[xl * 2 + 1 - yl]
    send[1] = got[1 - yl]
    send[2] = got2[1 - yl]
    send[3] = got2[2 + 1 - yl]


def home_kernel(place, early, got, got2, got3, recon):
    core, xl, yh, yl = place[0], place[1], place[2], place[3]
    low = half_mask((128, 128))
    same = [[early[xl * 2 + yl], got[yl]], [got2[yl], got2[2 + yl]]]
    for across in range(2):
        blocks = []
        for c in range(2):
            near = jnp.where(core == c, same[0][across], same[1][across])
            far = jnp.where(core == c, got3[across], got3[2 + across])
            for y in range(2):
                blocks.append(jnp.where(yl == y, near, far).astype(F32))
        side = (1 - xl) if across else xl
        for p, tile in enumerate(arrange(low, *blocks)):
            at = pl.multiple_of((side * 4 + ((yh + p) & 3)) * 128, 128)
            recon[:, pl.ds(at, 128)] = tile.astype(BF)


def call(kernel, name, outs, args, flops=0, moved=0, scratch=(), vmem=40):
    return pl.pallas_call(
        kernel,
        out_shape=tuple(jax.ShapeDtypeStruct(*o) for o in outs),
        in_specs=[SMEM if a.ndim == 1 else VMEM for a in args],
        out_specs=(VMEM,) * len(outs),
        scratch_shapes=list(scratch),
        compiler_params=pltpu.CompilerParams(vmem_limit_bytes=vmem * 1024 * 1024),
        cost_estimate=pl.CostEstimate(flops=flops, bytes_accessed=moved, transcendentals=0),
        name=name,
    )(*args)


def per_device(samples, rotation, codebook):
    core, xl = lax.axis_index("core"), lax.axis_index("xl")
    yh, yl = lax.axis_index("yh"), lax.axis_index("yl")
    chunk = lax.axis_index("z") * 2 + lax.axis_index("xh")
    place = jnp.stack([core, xl, yh, yl, chunk]).astype(jnp.int32)
    pack, copies = call(
        open_kernel,
        "open",
        [((64, 1408), BF), ((4, 128, 1024), BF)],
        (samples, rotation.T, codebook[0].T),
        vmem=60,
    )
    packs = []
    for steps in ((3, 1), (None, 2)):
        pairs = [
            (c * 8 + ((y + step if y & 1 else y - step) & 7), c * 8 + y)
            for c, step in enumerate(steps)
            for y in range(8)
            if step is not None
        ]
        packs.append(lax.ppermute(pack, ("core", "yh", "yl"), pairs))
    mine = lax.all_to_all(copies, ("xl", "yl"), 0, 0, tiled=True).reshape(512, 1024)
    tools = call(
        prepare_kernel,
        "prepare",
        [((128, 1024), BF), ((128, 512), BF), ((512, 256), BF)],
        (place, pack, *packs),
    )
    mine, *tools = lax.optimization_barrier((mine, *tools))
    swap = [(0, 1), (1, 0)]
    other = lax.ppermute(mine, "core", swap)
    block = ((4, 128, 128), BF)
    sums, cross, early = call(
        early_kernel,
        "early",
        [((512, 256), F32), ((128, 1024), F32), block],
        (mine, *tools),
        moved=8_000_000,
    )
    send, late, give = call(
        late_kernel,
        "late",
        [((16, 88, 128), BF), block, block],
        (place, other, *tools, sums, cross, early),
        moved=8_000_000,
    )
    home = lax.ppermute(give, "xl", swap)
    (second,) = call(second_kernel, "second", [block], (place, late, home))
    home2 = lax.ppermute(second, "core", swap)
    got = lax.all_to_all(send, FAR, 0, 0, tiled=True)
    got, home2 = lax.optimization_barrier((got, home2))
    (send,) = call(middle_kernel, "middle", [((32, 16, 128), BF)], (place, got))
    (third,) = call(third_kernel, "third", [block], (place, early, home, home2))
    home3 = lax.ppermute(third, "yl", swap)
    got = lax.all_to_all(send, NEAR, 0, 0, tiled=True)
    got, home3 = lax.optimization_barrier((got, home3))
    cross, spread = call(
        reduce_kernel,
        "reduce",
        [((2, 1024), F32), ((16, 8, 128), F32)],
        (place, got, codebook[0]),
    )
    spread = lax.all_to_all(spread, FAR, 0, 0, tiled=True)
    (recon,) = call(home_kernel, "home", [((128, 1024), BF)], (place, early, home, home2, home3))
    spread, recon = lax.optimization_barrier((spread, recon))
    (new_codes,) = call(codes_kernel, "codes", [((64, 256), F32)], (spread,))
    return recon, new_codes.T[None], cross


def solution(mesh):
    fine = Mesh(mesh.devices.reshape(SIZES), NAMES)
    rows = P(DP + SUB, None)
    return jax.shard_map(
        per_device,
        mesh=fine,
        in_specs=(rows, P(None, SUB), P(SUB, None, None)),
        out_specs=(rows, P(SUB, None, None), rows),
        check_vma=False,
    )
```

```python
import functools

import jax
import jax.numpy as jnp
from jax import lax
from jax.experimental import pallas as pl
from jax.experimental.pallas import tpu as pltpu
from jax.sharding import Mesh
from jax.sharding import PartitionSpec as P

SIZES = (8, 2, 2, 2, 4, 2)
NAMES = ("z", "xh", "core", "xl", "yh", "yl")
DP = ("z", "xh", "core")
SUB = ("xl", "yh", "yl")
FAR = ("z", "xh")
NEAR = ("core", "xl", "yh", "yl")
BF = jnp.bfloat16
F32 = jnp.float32
NT = (((1,), (1,)), ((), ()))
VMEM = pl.BlockSpec(memory_space=pltpu.VMEM)
SMEM = pl.BlockSpec(memory_space=pltpu.SMEM)


def half_mask(shape):
    return lax.broadcasted_iota(jnp.int32, shape, len(shape) - 1) < 64


def swap_halves(x):
    return pltpu.roll(x, 64, 1)


def split(x):
    high = x.astype(BF).astype(F32)
    return high, x - high


def open_kernel(samples, turn_t, codes_t, pack, copies):
    for n in range(4):
        copies[n] = samples[...]
    codes = codes_t[...]
    square = jnp.sum(codes * codes, axis=0, keepdims=True)
    high = square.astype(BF).astype(F32)
    mid = (square - high).astype(BF).astype(F32)
    low = square - high - mid
    squares = jnp.concatenate([high, mid, low, jnp.zeros((13, 256), F32)], axis=0).astype(BF)
    pack[:, 0:1024] = turn_t[...]
    pack[:, 1024:1280] = codes.astype(BF)
    pack[0:16, 1280:] = squares[:, :128]
    pack[16:32, 1280:] = squares[:, 128:]
    pack[32:64, 1280:] = jnp.zeros((32, 128), BF)


def prepare_kernel(place, pack, first, second, turn, codes_t, left):
    core, yl = place[0], place[3]
    w0, w1, w2 = pack[...], first[...], second[...]
    wa = jnp.where(core == 0, w0, jnp.where(yl == 0, w1, w2))
    wb = jnp.where(core == 0, w1, jnp.where(yl == 0, w2, w1))
    turn[0:64, :] = wa[:, :1024]
    turn[64:128, :] = wb[:, :1024]
    zero = jnp.zeros((64, 256), BF)
    both = jnp.concatenate(
        [
            jnp.concatenate([wa[:, 1024:1280], zero], axis=1),
            jnp.concatenate([zero, wb[:, 1024:1280]], axis=1),
        ],
        axis=0,
    )
    codes_t[...] = both
    squares = jnp.concatenate(
        [wa[0:16, 1280:], wa[16:32, 1280:], wb[0:16, 1280:], wb[16:32, 1280:]], axis=1
    )
    left[...] = jnp.concatenate([both * BF(-2.0), squares, jnp.zeros((112, 512), BF)], axis=0).T


def assign_rows(samples, turn, codes_t, left, sums, cross, put):
    rows, chunk = 512, 256
    lane = lax.broadcasted_iota(jnp.int32, (chunk, 128), 1)
    three = jnp.where(lane < 3, 1.0, 0.0).astype(BF)
    ones = jnp.ones((chunk, 128), BF)
    row16 = lax.broadcasted_iota(jnp.int32, (16, 256), 0)
    pick = (lax.broadcasted_iota(jnp.int32, (16, 256), 1) & 64) == 0
    pick = jnp.where(pick == (row16 == 0), 1.0, 0.0).astype(BF)
    for c in range(rows // chunk):
        x = samples[c * chunk : (c + 1) * chunk, :]
        rot = lax.dot_general(x, turn[...], NT, preferred_element_type=F32).astype(BF)
        square_high, square_low = split(jnp.square(rot.astype(F32)))
        square = jnp.concatenate([square_high, square_low], axis=1).astype(BF)
        row_square = lax.dot_general(pick, square, NT, preferred_element_type=F32)
        near = lax.dot_general(
            left[...], jnp.concatenate([rot, three], axis=1), NT, preferred_element_type=F32
        )
        parts = []
        for i in range(2):
            logits = -0.125 * (row_square[i : i + 1] + near[i * 256 : (i + 1) * 256])
            e = jnp.exp(logits - jnp.max(logits, axis=0, keepdims=True))
            parts.append((e * (1.0 / jnp.sum(e, axis=0, keepdims=True))).astype(BF))
        weights = jnp.concatenate(parts, axis=0)
        rebuilt = jnp.dot(codes_t[...], weights, preferred_element_type=F32).astype(BF)
        s = jnp.dot(weights, jnp.concatenate([rot, ones], axis=1), preferred_element_type=F32)
        k = jnp.dot(rebuilt, x, preferred_element_type=F32)
        sums = s if sums is None else sums + s
        cross = k if cross is None else cross + k
        back = rebuilt.T
        put(2 * c, back[:128])
        put(2 * c + 1, back[128:])
    return sums, cross


def early_kernel(samples, turn, codes_t, left, sums, cross, recon):
    def put(block, tile):
        recon[block] = tile

    sums[...], cross[...] = assign_rows(samples, turn, codes_t, left, None, None, put)


def late_kernel(
    place, samples, turn, codes_t, left, sums, cross, early, send, recon, give_x, give_y, give_xy
):
    def put(block, tile):
        recon[block] = tile

    sums, cross = assign_rows(samples, turn, codes_t, left, sums[...], cross[...], put)
    cross = cross.astype(BF)
    xl, yl = place[1], place[3]
    for n, block in enumerate((early, recon)):
        give_x[n] = block[(1 - xl) * 2 + yl]
        give_y[n] = block[xl * 2 + 1 - yl]
        give_xy[n] = block[(1 - xl) * 2 + 1 - yl]
    eye = (
        lax.broadcasted_iota(jnp.int32, (128, 128), 0)
        == lax.broadcasted_iota(jnp.int32, (128, 128), 1)
    )
    eye = jnp.where(eye, 1.0, 0.0).astype(BF)
    for z in range(8):
        piece = lax.dot_general(
            eye, cross[:, z * 128 : (z + 1) * 128], NT, preferred_element_type=F32
        ).astype(BF)
        send[z * 2, 0:64, :] = piece[:64]
        send[z * 2 + 1, 0:64, :] = piece[64:]
    low = half_mask((16, 128))
    even = (lax.broadcasted_iota(jnp.int32, (8, 128), 1) & 32) == 0
    for q in range(16):
        at = q * 16
        a, b = sums[at : at + 16, :], sums[256 + at : 272 + at, :]
        total = jnp.where(low, a[:, :128], b[:, :128])
        count = jnp.where(low, a[:, 128:], b[:, 128:])
        count = jnp.where(even, count[:8], count[8:])
        send[q, 64:88, :] = jnp.concatenate([total, count], axis=0).astype(BF)


def middle_kernel(place, got, send):
    total = jnp.sum(got[...].astype(F32), axis=0)
    cross_high, cross_low = split(total[:64])
    sums, count = total[64:80], total[80:88]
    low = half_mask((8, 128))
    row, lane = (lax.broadcasted_iota(jnp.int32, (8, 128), n) for n in range(2))
    turned = swap_halves(count)
    heads, tails = [], []
    for i in range(2):
        if i == 0:
            tail = jnp.where(low, sums[:8], swap_halves(sums[8:]))
            base = count
        else:
            tail = jnp.where(low, swap_halves(sums[:8]), sums[8:])
            base = turned
        each = jnp.where(
            lane < 32, base, jnp.where(lane < 96, pltpu.roll(base, 32, 1), swap_halves(base))
        )
        line = jnp.sum(jnp.where(((lane >> 3) & 7) == row, each, 0.0), axis=0, keepdims=True)
        line_high, line_low = split(line)
        heads.append(jnp.concatenate([line_high, line_low, jnp.zeros((2, 128), F32)], axis=0))
        tails.append(tail)
    core, yh, yl = place[0], place[2], place[3]
    last = jnp.where(core == 0, 5 - yl, 7 - 4 * yl)
    for y in range(8):
        is_last = ((y + 8 - 2 * yh) & 7) == last
        head = jnp.where(is_last, heads[1], heads[0])
        tail = jnp.where(is_last, tails[1], tails[0])
        for c in range(4):
            d = c * 8 + y
            send[d] = jnp.concatenate(
                [cross_high[2 * d : 2 * d + 2], cross_low[2 * d : 2 * d + 2], head, tail], axis=0
            ).astype(BF)


def arrange(low, a, b, c, d):
    turned = swap_halves(b)
    return [jnp.where(low, a, turned), d, jnp.where(low, turned, a), c]


def cross_kernel(got, cross):
    low = half_mask((2, 128))
    for xl in range(2):
        total = [jnp.zeros((2, 128), F32)] * 4
        for yh in range(4):
            blocks = []
            for core in range(2):
                for yl in range(2):
                    t = got[core * 16 + xl * 8 + yh * 2 + yl].astype(F32)
                    blocks.append(t[0:2] + t[2:4])
            for p, tile in enumerate(arrange(low, *blocks)):
                total[(yh + p) & 3] += tile
        for p in range(4):
            at = (xl * 4 + p) * 128
            cross[:, at : at + 128] = total[p]


def fresh_kernel(place, got, codes, spread):
    my_xl, my_yh, my_yl = place[1], place[2], place[3]
    t = jnp.zeros((16, 128), F32)
    for yh in range(4):
        r = (2 * my_yh + my_yl + 8 - 2 * yh) & 7
        yl = jnp.where((r >= 1) & (r <= 4), 1, 0)
        t += got[((r >> 1) & 1) * 16 + my_xl * 8 + yh * 2 + yl].astype(F32)
    lane = lax.broadcasted_iota(jnp.int32, (16, 128), 1)
    mine = (lane >> 3) == lax.broadcasted_iota(jnp.int32, (16, 128), 0)
    line = jnp.broadcast_to(t[4:5] + t[5:6], (16, 128))
    count = 0.125 * jnp.sum(jnp.where(mine, line, 0.0), axis=1, keepdims=True)
    count = jnp.where(half_mask((8, 128)), count[:8], count[8:])
    at = pl.multiple_of(place[4] * 16, 16)
    own = codes[pl.ds(at, 16), :]
    own = jnp.concatenate([own[:8], own[8:]], axis=1)
    fresh = (t[8:16] + own) / (count + 1.0)
    for q in range(16):
        spread[q] = fresh


def codes_kernel(got, codes_t):
    tiles = []
    for q in range(16):
        t = got[q]
        tiles += [t, swap_halves(t)]
    codes_t[...] = jnp.concatenate(tiles, axis=0).T[:64]


def second_kernel(place, late, got_x, got_y, got_xy, send):
    xl, yl = place[1], place[3]
    send[0] = late[xl * 2 + yl]
    send[1] = got_y[1]
    send[2] = got_x[1]
    send[3] = got_xy[1]


def home_kernel(place, early, got_x, got_y, got_xy, got_core, recon):
    core, xl, yh, yl = place[0], place[1], place[2], place[3]
    low = half_mask((128, 128))
    here = [[early[xl * 2 + yl], got_y[0]], [got_x[0], got_xy[0]]]
    for across in range(2):
        blocks = []
        for c in range(2):
            near = jnp.where(core == c, here[across][0], got_core[across * 2])
            far = jnp.where(core == c, here[across][1], got_core[across * 2 + 1])
            for y in range(2):
                blocks.append(jnp.where(yl == y, near, far).astype(F32))
        side = (1 - xl) if across else xl
        for p, tile in enumerate(arrange(low, *blocks)):
            at = pl.multiple_of((side * 4 + ((yh + p) & 3)) * 128, 128)
            recon[:, pl.ds(at, 128)] = tile.astype(BF)


def call(kernel, name, outs, args, flops=0, moved=0, scratch=(), vmem=40):
    return pl.pallas_call(
        kernel,
        out_shape=tuple(jax.ShapeDtypeStruct(*o) for o in outs),
        in_specs=[SMEM if a.ndim == 1 else VMEM for a in args],
        out_specs=(VMEM,) * len(outs),
        scratch_shapes=list(scratch),
        compiler_params=pltpu.CompilerParams(vmem_limit_bytes=vmem * 1024 * 1024),
        cost_estimate=pl.CostEstimate(flops=flops, bytes_accessed=moved, transcendentals=0),
        name=name,
    )(*args)


def per_device(samples, rotation, codebook):
    core, xl = lax.axis_index("core"), lax.axis_index("xl")
    yh, yl = lax.axis_index("yh"), lax.axis_index("yl")
    chunk = lax.axis_index("z") * 2 + lax.axis_index("xh")
    place = jnp.stack([core, xl, yh, yl, chunk]).astype(jnp.int32)
    pack, copies = call(
        open_kernel,
        "open",
        [((64, 1408), BF), ((4, 128, 1024), BF)],
        (samples, rotation.T, codebook[0].T),
        vmem=60,
    )
    packs = []
    for steps in ((3, 2), (None, 1)):
        pairs = [
            (c * 8 + ((y + step if y & 1 else y - step) & 7), c * 8 + y)
            for c, step in enumerate(steps)
            for y in range(8)
            if step is not None
        ]
        packs.append(lax.ppermute(pack, ("core", "yh", "yl"), pairs))
    mine = lax.all_to_all(copies, ("xl", "yl"), 0, 0, tiled=True).reshape(512, 1024)
    tools = call(
        prepare_kernel,
        "prepare",
        [((128, 1024), BF), ((128, 512), BF), ((512, 256), BF)],
        (place, pack, *packs),
    )
    mine, *tools = lax.optimization_barrier((mine, *tools))
    swap = [(0, 1), (1, 0)]
    other = lax.ppermute(mine, "core", swap)
    block, pair = ((4, 128, 128), BF), ((2, 128, 128), BF)
    sums, cross, early = call(
        early_kernel,
        "early",
        [((512, 256), F32), ((128, 1024), F32), block],
        (mine, *tools),
        moved=8_000_000,
    )
    send, late, *gives = call(
        late_kernel,
        "late",
        [((16, 88, 128), BF), block, pair, pair, pair],
        (place, other, *tools, sums, cross, early),
        moved=8_000_000,
    )
    both = [(0, 3), (1, 2), (2, 1), (3, 0)]
    got_x = lax.ppermute(gives[0], "xl", swap)
    got_y = lax.ppermute(gives[1], "yl", swap)
    got_xy = lax.ppermute(gives[2], ("xl", "yl"), both)
    got = lax.all_to_all(send, FAR, 0, 0, tiled=True)
    got, got_x, got_y, got_xy = lax.optimization_barrier((got, got_x, got_y, got_xy))
    (send,) = call(middle_kernel, "middle", [((32, 16, 128), BF)], (place, got))
    (other_half,) = call(second_kernel, "second", [block], (place, late, got_x, got_y, got_xy))
    got_core = lax.ppermute(other_half, "core", swap)
    got = lax.all_to_all(send, NEAR, 0, 0, tiled=True)
    got, got_core = lax.optimization_barrier((got, got_core))
    (spread,) = call(
        fresh_kernel, "fresh", [((16, 8, 128), F32)], (place, got, codebook[0])
    )
    (cross,) = call(cross_kernel, "cross", [((2, 1024), F32)], (got,))
    spread = lax.all_to_all(spread, FAR, 0, 0, tiled=True)
    (recon,) = call(
        home_kernel, "home", [((128, 1024), BF)], (place, early, got_x, got_y, got_xy, got_core)
    )
    spread, recon, cross = lax.optimization_barrier((spread, recon, cross))
    (new_codes,) = call(codes_kernel, "codes", [((64, 256), F32)], (spread,))
    return recon, new_codes.T[None], cross


def solution(mesh):
    fine = Mesh(mesh.devices.reshape(SIZES), NAMES)
    rows = P(DP + SUB, None)
    return jax.shard_map(
        per_device,
        mesh=fine,
        in_specs=(rows, P(None, SUB), P(SUB, None, None)),
        out_specs=(rows, P(SUB, None, None), rows),
        check_vma=False,
    )
```

```python
import functools

import jax
import jax.numpy as jnp
from jax import lax
from jax.experimental import pallas as pl
from jax.experimental.pallas import tpu as pltpu
from jax.sharding import Mesh
from jax.sharding import PartitionSpec as P

SIZES = (8, 2, 2, 2, 4, 2)
NAMES = ("z", "xh", "core", "xl", "yh", "yl")
DP = ("z", "xh", "core")
SUB = ("xl", "yh", "yl")
PLACES = (((0, 5), (1, 4)), ((6, 7), (3, 2)))
FAR = ("z", "xh")
NEAR = ("core", "xl", "yh", "yl")
BF = jnp.bfloat16
F32 = jnp.float32
NT = (((1,), (1,)), ((), ()))
VMEM = pl.BlockSpec(memory_space=pltpu.VMEM)
SMEM = pl.BlockSpec(memory_space=pltpu.SMEM)


def half_mask(shape):
    return lax.broadcasted_iota(jnp.int32, shape, len(shape) - 1) < 64


def swap_halves(x):
    return pltpu.roll(x, 64, 1)


def split(x):
    high = x.astype(BF).astype(F32)
    return high, x - high


def open_kernel(samples, turn_t, codes_t, pack, copies):
    for n in range(4):
        copies[n] = samples[...]
    codes = codes_t[...]
    square = jnp.sum(codes * codes, axis=0, keepdims=True)
    high = square.astype(BF).astype(F32)
    mid = (square - high).astype(BF).astype(F32)
    low = square - high - mid
    squares = jnp.concatenate([high, mid, low, jnp.zeros((13, 256), F32)], axis=0).astype(BF)
    pack[:, 0:1024] = turn_t[...]
    pack[:, 1024:1280] = codes.astype(BF)
    pack[0:16, 1280:] = squares[:, :128]
    pack[16:32, 1280:] = squares[:, 128:]
    pack[32:64, 1280:] = jnp.zeros((32, 128), BF)


def prepare_kernel(place, pack, first, second, turn, codes_t, left):
    core = place[0]
    w0, w1, w2 = pack[...], first[...], second[...]
    wa = jnp.where(core == 0, w0, w1)
    wb = jnp.where(core == 0, w1, w2)
    turn[0:64, :] = wa[:, :1024]
    turn[64:128, :] = wb[:, :1024]
    zero = jnp.zeros((64, 256), BF)
    both = jnp.concatenate(
        [
            jnp.concatenate([wa[:, 1024:1280], zero], axis=1),
            jnp.concatenate([zero, wb[:, 1024:1280]], axis=1),
        ],
        axis=0,
    )
    codes_t[...] = both
    squares = jnp.concatenate(
        [wa[0:16, 1280:], wa[16:32, 1280:], wb[0:16, 1280:], wb[16:32, 1280:]], axis=1
    )
    left[...] = jnp.concatenate([both * BF(-2.0), squares, jnp.zeros((112, 512), BF)], axis=0).T


def assign_rows(samples, turn, codes_t, left, sums, cross, put):
    rows, chunk = 512, 256
    lane = lax.broadcasted_iota(jnp.int32, (chunk, 128), 1)
    three = jnp.where(lane < 3, 1.0, 0.0).astype(BF)
    ones = jnp.ones((chunk, 128), BF)
    row16 = lax.broadcasted_iota(jnp.int32, (16, 256), 0)
    pick = (lax.broadcasted_iota(jnp.int32, (16, 256), 1) & 64) == 0
    pick = jnp.where(pick == (row16 == 0), 1.0, 0.0).astype(BF)
    for c in range(rows // chunk):
        x = samples[c * chunk : (c + 1) * chunk, :]
        rot = lax.dot_general(x, turn[...], NT, preferred_element_type=F32).astype(BF)
        square_high, square_low = split(jnp.square(rot.astype(F32)))
        square = jnp.concatenate([square_high, square_low], axis=1).astype(BF)
        row_square = lax.dot_general(pick, square, NT, preferred_element_type=F32)
        near = lax.dot_general(
            left[...], jnp.concatenate([rot, three], axis=1), NT, preferred_element_type=F32
        )
        parts = []
        for i in range(2):
            logits = -0.125 * (row_square[i : i + 1] + near[i * 256 : (i + 1) * 256])
            e = jnp.exp(logits - jnp.max(logits, axis=0, keepdims=True))
            parts.append((e * (1.0 / jnp.sum(e, axis=0, keepdims=True))).astype(BF))
        weights = jnp.concatenate(parts, axis=0)
        rebuilt = jnp.dot(codes_t[...], weights, preferred_element_type=F32).astype(BF)
        s = jnp.dot(weights, jnp.concatenate([rot, ones], axis=1), preferred_element_type=F32)
        k = jnp.dot(rebuilt, x, preferred_element_type=F32)
        sums = s if sums is None else sums + s
        cross = k if cross is None else cross + k
        back = rebuilt.T
        put(2 * c, back[:128])
        put(2 * c + 1, back[128:])
    return sums, cross


def early_kernel(samples, turn, codes_t, left, sums, cross, recon):
    def put(block, tile):
        recon[block] = tile

    sums[...], cross[...] = assign_rows(samples, turn, codes_t, left, None, None, put)


def late_kernel(samples, turn, codes_t, left, sums, cross, send, recon, sums_a, sums_b):
    def put(block, tile):
        recon[block] = tile

    sums, cross = assign_rows(samples, turn, codes_t, left, sums[...], cross[...], put)
    cross = cross.astype(BF)
    r = lax.broadcasted_iota(jnp.int32, (256, 256), 0)
    wanted = ((r & 4) << 5) | ((r & 2) << 5) | ((r >> 3) << 1) | (r & 1)
    order = jnp.where(lax.broadcasted_iota(jnp.int32, (256, 256), 1) == wanted, 1.0, 0.0).astype(BF)
    pieces = [
        lax.dot_general(order, cross[:, n * 256 : (n + 1) * 256], NT, preferred_element_type=F32)
        for n in range(4)
    ]
    for d in range(32):
        tiles = [piece[8 * d : 8 * d + 8] for piece in pieces]
        send[d] = jnp.concatenate(tiles, axis=0).astype(BF)
    low = half_mask((64, 128))
    diagonal = (
        lax.broadcasted_iota(jnp.int32, (128, 128), 0)
        == lax.broadcasted_iota(jnp.int32, (128, 128), 1)
    )
    for i, out in enumerate((sums_a, sums_b)):
        lines = []
        for h in range(2):
            at = i * 256 + h * 128
            a, b = sums[at : at + 64, :128], sums[at + 64 : at + 128, :128]
            if i == 0:
                tile = jnp.where(low, a, swap_halves(b))
            else:
                tile = jnp.where(low, swap_halves(a), b)
            out[h * 64 : h * 64 + 64, :] = tile.astype(BF)
            count = jnp.where(diagonal, sums[at : at + 128, 128:], 0.0)
            lines += split(jnp.sum(count, axis=0, keepdims=True))
        out[128:144, :] = jnp.concatenate(lines + [jnp.zeros((12, 128), F32)], axis=0).astype(BF)


def half_kernel(place, first, second, keep, give):
    core = place[0]
    both = first[...].astype(F32) + second[...].astype(F32)
    empty = jnp.zeros((14, 128), F32)
    halves = []
    for h in range(2):
        line = both[128 + 2 * h : 129 + 2 * h] + both[129 + 2 * h : 130 + 2 * h]
        halves.append(jnp.concatenate([both[h * 64 : h * 64 + 64], *split(line), empty], axis=0))
    keep[...] = jnp.where(core == 0, halves[0], halves[1])
    give[...] = jnp.where(core == 0, halves[1], halves[0]).astype(BF)


def arrange(low, a, b, c, d):
    turned = swap_halves(b)
    return [jnp.where(low, a, turned), swap_halves(d), jnp.where(low, turned, a), c]


def middle_kernel(got, keep, half, send):
    low = half_mask((32, 128))
    columns = []
    for xl in range(2):
        total = [jnp.zeros((32, 128), F32)] * 4
        for yh in range(4):
            blocks = [got[core * 16 + xl * 8 + yh * 2 + yl].astype(F32) for core in range(2) for yl in range(2)]
            for p, tile in enumerate(arrange(low, *blocks)):
                total[(yh + p) & 3] += tile
        columns += total
    r = lax.broadcasted_iota(jnp.int32, (256, 256), 0)
    wanted = (((r >> 1) & 7) << 5) | ((r >> 4) << 1) | (r & 1)
    order = jnp.where(lax.broadcasted_iota(jnp.int32, (256, 256), 1) == wanted, 1.0, 0.0).astype(BF)
    cross = jnp.dot(
        order, jnp.concatenate(columns, axis=0).astype(BF), preferred_element_type=F32
    ).astype(BF)
    both = keep[...] + half[...].astype(F32)
    line = both[64:65] + both[65:66]
    both = jnp.concatenate([both[:64], *split(line), jnp.zeros((6, 128), F32)], axis=0).astype(BF)
    for q in range(16):
        send[q, 0:16, :] = cross[q * 16 : q * 16 + 16]
        send[q, 16:88, :] = both


def finish_kernel(place, got, codes_t, cross, fresh):
    total = jnp.sum(got[...].astype(F32), axis=0)
    for n in range(8):
        cross[:, n * 128 : (n + 1) * 128] = total[2 * n : 2 * n + 2]
    sums, count = total[16:80], total[80:81] + total[81:82]
    sums = jnp.concatenate([sums, swap_halves(sums)], axis=0).T[:64]
    own = jnp.where(place[0] == 0, codes_t[:, :128], codes_t[:, 128:])
    fresh[...] = (sums + own) / (count + 1.0)


def codes_kernel(place, mine, other, codes_t):
    a, b = mine[...], other[...]
    codes_t[:, :128] = jnp.where(place[0] == 0, a, b)
    codes_t[:, 128:] = jnp.where(place[0] == 0, b, a)


def second_kernel(place, early, got_core, give_x, give_y, give_xy):
    xl, yl = place[1], place[3]
    for n, block in enumerate((early, got_core)):
        give_x[n] = block[(1 - xl) * 2 + yl]
        give_y[n] = block[xl * 2 + 1 - yl]
        give_xy[n] = block[(1 - xl) * 2 + 1 - yl]


def home_kernel(place, early, got_core, got_x, got_y, got_xy, recon):
    core, xl, yh, yl = place[0], place[1], place[2], place[3]
    low = half_mask((128, 128))
    own = [early[xl * 2 + yl], got_core[xl * 2 + yl]]
    for across, (same, far) in enumerate(((own, got_y), (got_x, got_xy))):
        blocks = []
        for c in range(2):
            near_c = jnp.where(core == c, same[0], same[1])
            far_c = jnp.where(core == c, far[0], far[1])
            for y in range(2):
                blocks.append(jnp.where(yl == y, near_c, far_c).astype(F32))
        side = (1 - xl) if across else xl
        for p, tile in enumerate(arrange(low, *blocks)):
            at = pl.multiple_of((side * 4 + ((yh + p) & 3)) * 128, 128)
            recon[:, pl.ds(at, 128)] = tile.astype(BF)


def call(kernel, name, outs, args, flops=0, moved=0, scratch=(), vmem=40):
    return pl.pallas_call(
        kernel,
        out_shape=tuple(jax.ShapeDtypeStruct(*o) for o in outs),
        in_specs=[SMEM if a.ndim == 1 else VMEM for a in args],
        out_specs=(VMEM,) * len(outs),
        scratch_shapes=list(scratch),
        compiler_params=pltpu.CompilerParams(vmem_limit_bytes=vmem * 1024 * 1024),
        cost_estimate=pl.CostEstimate(flops=flops, bytes_accessed=moved, transcendentals=0),
        name=name,
    )(*args)


def per_device(samples, rotation, codebook):
    core, xl = lax.axis_index("core"), lax.axis_index("xl")
    yh, yl = lax.axis_index("yh"), lax.axis_index("yl")
    chunk = lax.axis_index("z") * 2 + lax.axis_index("xh")
    place = jnp.stack([core, xl, yh, yl, chunk]).astype(jnp.int32)
    pack, copies = call(
        open_kernel,
        "open",
        [((64, 1408), BF), ((4, 128, 1024), BF)],
        (samples, rotation.T, codebook[0].T),
        vmem=60,
    )
    packs = []
    for steps in ((3, 2), (None, 1)):
        pairs = [
            (c * 8 + ((y + step if y & 1 else y - step) & 7), c * 8 + y)
            for c, step in enumerate(steps)
            for y in range(8)
            if step is not None
        ]
        packs.append(lax.ppermute(pack, ("core", "yh", "yl"), pairs))
    mine = lax.all_to_all(copies, ("xl", "yl"), 0, 0, tiled=True).reshape(512, 1024)
    tools = call(
        prepare_kernel,
        "prepare",
        [((128, 1024), BF), ((128, 512), BF), ((512, 256), BF)],
        (place, pack, *packs),
    )
    mine, *tools = lax.optimization_barrier((mine, *tools))
    swap = [(0, 1), (1, 0)]
    other = lax.ppermute(mine, "core", swap)
    block, pair = ((4, 128, 128), BF), ((2, 128, 128), BF)
    sums, cross, early = call(
        early_kernel,
        "early",
        [((512, 256), F32), ((128, 1024), F32), block],
        (mine, *tools),
        moved=8_000_000,
    )
    send, late, *totals = call(
        late_kernel,
        "late",
        [((32, 32, 128), BF), block, ((144, 128), BF), ((144, 128), BF)],
        (other, *tools, sums, cross),
        moved=8_000_000,
    )
    moved = []
    for i in range(2):
        pairs = [
            (c * 8 + y, c * 8 + (((y & 6) + PLACES[c][y & 1][i]) & 7)) for c in range(2) for y in range(8)
        ]
        moved.append(lax.ppermute(totals[i], ("core", "yh", "yl"), pairs))
    got_core = lax.ppermute(late, "core", swap)
    keep, give = call(half_kernel, "half", [((80, 128), F32), ((80, 128), BF)], (place, *moved))
    half = lax.ppermute(give, "core", swap)
    got = lax.all_to_all(send, NEAR, 0, 0, tiled=True)
    got, half, got_core = lax.optimization_barrier((got, half, got_core))
    (send,) = call(middle_kernel, "middle", [((16, 88, 128), BF)], (got, keep, half))
    gives = call(second_kernel, "second", [pair, pair, pair], (place, early, got_core))
    got_x = lax.ppermute(gives[0], "xl", swap)
    got_y = lax.ppermute(gives[1], "yl", swap)
    got_xy = lax.ppermute(gives[2], ("xl", "yl"), [(0, 3), (1, 2), (2, 1), (3, 0)])
    got = lax.all_to_all(send, FAR, 0, 0, tiled=True)
    got, got_x, got_y, got_xy = lax.optimization_barrier((got, got_x, got_y, got_xy))
    cross, fresh = call(
        finish_kernel,
        "finish",
        [((2, 1024), F32), ((64, 128), F32)],
        (place, got, codebook[0].T),
    )
    fresh_other = lax.ppermute(fresh, "core", swap)
    (recon,) = call(
        home_kernel, "home", [((128, 1024), BF)], (place, early, got_core, got_x, got_y, got_xy)
    )
    fresh_other, recon = lax.optimization_barrier((fresh_other, recon))
    (new_codes,) = call(codes_kernel, "codes", [((64, 256), F32)], (place, fresh, fresh_other))
    return recon, new_codes.T[None], cross


def solution(mesh):
    fine = Mesh(mesh.devices.reshape(SIZES), NAMES)
    rows = P(DP + SUB, None)
    return jax.shard_map(
        per_device,
        mesh=fine,
        in_specs=(rows, P(None, SUB), P(SUB, None, None)),
        out_specs=(rows, P(SUB, None, None), rows),
        check_vma=False,
    )
```

```python
import functools

import jax
import jax.numpy as jnp
from jax import lax
from jax.experimental import pallas as pl
from jax.experimental.pallas import tpu as pltpu
from jax.sharding import Mesh
from jax.sharding import PartitionSpec as P

SIZES = (8, 2, 2, 2, 4, 2)
NAMES = ("z", "xh", "core", "xl", "yh", "yl")
DP = ("z", "xh", "core")
SUB = ("xl", "yh", "yl")
PLACES = (((0, 5), (1, 4)), ((6, 7), (3, 2)))
FAR = ("z", "xh")
NEAR = ("core", "xl", "yh", "yl")
BF = jnp.bfloat16
F32 = jnp.float32
NT = (((1,), (1,)), ((), ()))
VMEM = pl.BlockSpec(memory_space=pltpu.VMEM)
ANY = pl.BlockSpec(memory_space=pl.ANY)


def half_mask(shape):
    return lax.broadcasted_iota(jnp.int32, shape, len(shape) - 1) < 64


def swap_halves(x):
    return pltpu.roll(x, 64, 1)


def split(x):
    high = x.astype(BF).astype(F32)
    return high, x - high


def open_kernel(samples, turn_t, codes_t, pack, copies, done):
    moves = [pltpu.make_async_copy(samples, copies.at[n], done.at[n]) for n in range(4)]
    for move in moves:
        move.start()
    codes = codes_t[...]
    square = jnp.sum(codes * codes, axis=0, keepdims=True)
    high = square.astype(BF).astype(F32)
    mid = (square - high).astype(BF).astype(F32)
    low = square - high - mid
    squares = jnp.concatenate([high, mid, low, jnp.zeros((13, 256), F32)], axis=0).astype(BF)
    pack[:, 0:1024] = turn_t[...]
    pack[:, 1024:1280] = codes.astype(BF)
    pack[0:16, 1280:] = squares[:, :128]
    pack[16:32, 1280:] = squares[:, 128:]
    pack[32:64, 1280:] = jnp.zeros((32, 128), BF)
    for move in moves:
        move.wait()


def prepare_kernel(pack, first, second, turn, codes_t, left):
    core = lax.axis_index("core")
    w0, w1, w2 = pack[...], first[...], second[...]
    wa = jnp.where(core == 0, w0, w1)
    wb = jnp.where(core == 0, w1, w2)
    turn[0:64, :] = wa[:, :1024]
    turn[64:128, :] = wb[:, :1024]
    zero = jnp.zeros((64, 256), BF)
    both = jnp.concatenate(
        [
            jnp.concatenate([wa[:, 1024:1280], zero], axis=1),
            jnp.concatenate([zero, wb[:, 1024:1280]], axis=1),
        ],
        axis=0,
    )
    codes_t[...] = both
    squares = jnp.concatenate(
        [wa[0:16, 1280:], wa[16:32, 1280:], wb[0:16, 1280:], wb[16:32, 1280:]], axis=1
    )
    left[...] = jnp.concatenate([both * BF(-2.0), squares, jnp.zeros((112, 512), BF)], axis=0).T


def assign_rows(samples, turn, codes_t, left, sums, cross, put):
    rows, chunk = 512, 256
    lane = lax.broadcasted_iota(jnp.int32, (chunk, 128), 1)
    three = jnp.where(lane < 3, 1.0, 0.0).astype(BF)
    ones = jnp.ones((chunk, 128), BF)
    row16 = lax.broadcasted_iota(jnp.int32, (16, 256), 0)
    pick = (lax.broadcasted_iota(jnp.int32, (16, 256), 1) & 64) == 0
    pick = jnp.where(pick == (row16 == 0), 1.0, 0.0).astype(BF)
    for c in range(rows // chunk):
        x = samples[c * chunk : (c + 1) * chunk, :]
        rot = lax.dot_general(x, turn[...], NT, preferred_element_type=F32).astype(BF)
        square_high, square_low = split(jnp.square(rot.astype(F32)))
        square = jnp.concatenate([square_high, square_low], axis=1).astype(BF)
        row_square = lax.dot_general(pick, square, NT, preferred_element_type=F32)
        near = lax.dot_general(
            left[...], jnp.concatenate([rot, three], axis=1), NT, preferred_element_type=F32
        )
        parts = []
        for i in range(2):
            logits = -0.125 * (row_square[i : i + 1] + near[i * 256 : (i + 1) * 256])
            e = jnp.exp(logits - jnp.max(logits, axis=0, keepdims=True))
            parts.append((e * (1.0 / jnp.sum(e, axis=0, keepdims=True))).astype(BF))
        weights = jnp.concatenate(parts, axis=0)
        rebuilt = jnp.dot(codes_t[...], weights, preferred_element_type=F32).astype(BF)
        s = jnp.dot(weights, jnp.concatenate([rot, ones], axis=1), preferred_element_type=F32)
        k = jnp.dot(rebuilt, x, preferred_element_type=F32)
        sums = s if sums is None else sums + s
        cross = k if cross is None else cross + k
        back = rebuilt.T
        put(2 * c, back[:128])
        put(2 * c + 1, back[128:])
    return sums, cross


def early_kernel(samples, turn, codes_t, left, sums, cross, recon):
    def put(block, tile):
        recon[block] = tile

    sums[...], cross[...] = assign_rows(samples, turn, codes_t, left, None, None, put)


def late_kernel(samples, turn, codes_t, left, sums, cross, send, recon, sums_a, sums_b):
    def put(block, tile):
        recon[block] = tile

    sums, cross = assign_rows(samples, turn, codes_t, left, sums[...], cross[...], put)
    cross = cross.astype(BF)
    r = lax.broadcasted_iota(jnp.int32, (256, 256), 0)
    wanted = ((r & 4) << 5) | ((r & 2) << 5) | ((r >> 3) << 1) | (r & 1)
    order = jnp.where(lax.broadcasted_iota(jnp.int32, (256, 256), 1) == wanted, 1.0, 0.0).astype(BF)
    pieces = [
        lax.dot_general(order, cross[:, n * 256 : (n + 1) * 256], NT, preferred_element_type=F32)
        for n in range(4)
    ]
    for d in range(32):
        tiles = [piece[8 * d : 8 * d + 8] for piece in pieces]
        send[d] = jnp.concatenate(tiles, axis=0).astype(BF)
    low = half_mask((64, 128))
    diagonal = (
        lax.broadcasted_iota(jnp.int32, (128, 128), 0)
        == lax.broadcasted_iota(jnp.int32, (128, 128), 1)
    )
    for i, out in enumerate((sums_a, sums_b)):
        lines = []
        for h in range(2):
            at = i * 256 + h * 128
            a, b = sums[at : at + 64, :128], sums[at + 64 : at + 128, :128]
            if i == 0:
                tile = jnp.where(low, a, swap_halves(b))
            else:
                tile = jnp.where(low, swap_halves(a), b)
            out[h * 64 : h * 64 + 64, :] = tile.astype(BF)
            count = jnp.where(diagonal, sums[at : at + 128, 128:], 0.0)
            lines += split(jnp.sum(count, axis=0, keepdims=True))
        out[128:144, :] = jnp.concatenate(lines + [jnp.zeros((12, 128), F32)], axis=0).astype(BF)


def half_kernel(first, second, keep, give):
    core = lax.axis_index("core")
    both = first[...].astype(F32) + second[...].astype(F32)
    empty = jnp.zeros((14, 128), F32)
    halves = []
    for h in range(2):
        line = both[128 + 2 * h : 129 + 2 * h] + both[129 + 2 * h : 130 + 2 * h]
        halves.append(jnp.concatenate([both[h * 64 : h * 64 + 64], *split(line), empty], axis=0))
    keep[...] = jnp.where(core == 0, halves[0], halves[1])
    give[...] = jnp.where(core == 0, halves[1], halves[0]).astype(BF)


def arrange(low, a, b, c, d):
    turned = swap_halves(b)
    return [jnp.where(low, a, turned), swap_halves(d), jnp.where(low, turned, a), c]


def middle_kernel(got, keep, half, send):
    low = half_mask((32, 128))
    columns = []
    for xl in range(2):
        total = [jnp.zeros((32, 128), F32)] * 4
        for yh in range(4):
            blocks = [got[core * 16 + xl * 8 + yh * 2 + yl].astype(F32) for core in range(2) for yl in range(2)]
            for p, tile in enumerate(arrange(low, *blocks)):
                total[(yh + p) & 3] += tile
        columns += total
    r = lax.broadcasted_iota(jnp.int32, (256, 256), 0)
    wanted = (((r >> 1) & 7) << 5) | ((r >> 4) << 1) | (r & 1)
    order = jnp.where(lax.broadcasted_iota(jnp.int32, (256, 256), 1) == wanted, 1.0, 0.0).astype(BF)
    cross = jnp.dot(
        order, jnp.concatenate(columns, axis=0).astype(BF), preferred_element_type=F32
    ).astype(BF)
    both = keep[...] + half[...].astype(F32)
    line = both[64:65] + both[65:66]
    both = jnp.concatenate([both[:64], *split(line), jnp.zeros((6, 128), F32)], axis=0).astype(BF)
    for q in range(16):
        send[q, 0:16, :] = cross[q * 16 : q * 16 + 16]
        send[q, 16:88, :] = both


def finish_kernel(got, codes_t, cross, fresh):
    total = jnp.sum(got[...].astype(F32), axis=0)
    for n in range(8):
        cross[:, n * 128 : (n + 1) * 128] = total[2 * n : 2 * n + 2]
    sums, count = total[16:80], total[80:81] + total[81:82]
    sums = jnp.concatenate([sums, swap_halves(sums)], axis=0).T[:64]
    own = jnp.where(lax.axis_index("core") == 0, codes_t[:, :128], codes_t[:, 128:])
    fresh[...] = (sums + own) / (count + 1.0)


def codes_kernel(mine, other, codes_t):
    a, b = mine[...], other[...]
    codes_t[:, :128] = jnp.where(lax.axis_index("core") == 0, a, b)
    codes_t[:, 128:] = jnp.where(lax.axis_index("core") == 0, b, a)


def second_kernel(early, got_core, give_x, give_y, give_xy):
    xl, yl = lax.axis_index("xl"), lax.axis_index("yl")
    for n, block in enumerate((early, got_core)):
        give_x[n] = block[(1 - xl) * 2 + yl]
        give_y[n] = block[xl * 2 + 1 - yl]
        give_xy[n] = block[(1 - xl) * 2 + 1 - yl]


def home_kernel(early, got_core, got_x, got_y, got_xy, recon):
    core, xl = lax.axis_index("core"), lax.axis_index("xl")
    yh, yl = lax.axis_index("yh"), lax.axis_index("yl")
    low = half_mask((128, 128))
    own = [early[xl * 2 + yl], got_core[xl * 2 + yl]]
    for across, (same, far) in enumerate(((own, got_y), (got_x, got_xy))):
        blocks = []
        for c in range(2):
            near_c = jnp.where(core == c, same[0], same[1])
            far_c = jnp.where(core == c, far[0], far[1])
            for y in range(2):
                blocks.append(jnp.where(yl == y, near_c, far_c).astype(F32))
        side = (1 - xl) if across else xl
        for p, tile in enumerate(arrange(low, *blocks)):
            at = pl.multiple_of((side * 4 + ((yh + p) & 3)) * 128, 128)
            recon[:, pl.ds(at, 128)] = tile.astype(BF)


def call(kernel, name, outs, args, flops=0, moved=0):
    return pl.pallas_call(
        kernel,
        out_shape=tuple(jax.ShapeDtypeStruct(*o) for o in outs),
        in_specs=[VMEM] * len(args),
        out_specs=(VMEM,) * len(outs),
        compiler_params=pltpu.CompilerParams(vmem_limit_bytes=40 * 1024 * 1024),
        cost_estimate=pl.CostEstimate(flops=flops, bytes_accessed=moved, transcendentals=0),
        name=name,
    )(*args)


def per_device(samples, rotation, codebook):
    pack, copies = pl.pallas_call(
        open_kernel,
        out_shape=(
            jax.ShapeDtypeStruct((64, 1408), BF),
            jax.ShapeDtypeStruct((4, 128, 1024), BF),
        ),
        in_specs=[ANY, VMEM, VMEM],
        out_specs=(VMEM, ANY),
        scratch_shapes=[pltpu.SemaphoreType.DMA((4,))],
        compiler_params=pltpu.CompilerParams(vmem_limit_bytes=60 * 1024 * 1024),
        name="open",
    )(samples, rotation.T, codebook[0].T)
    packs = []
    for steps in ((3, 2), (None, 1)):
        pairs = [
            (c * 8 + ((y + step if y & 1 else y - step) & 7), c * 8 + y)
            for c, step in enumerate(steps)
            for y in range(8)
            if step is not None
        ]
        packs.append(lax.ppermute(pack, ("core", "yh", "yl"), pairs))
    mine = lax.all_to_all(copies, ("xl", "yl"), 0, 0, tiled=True).reshape(512, 1024)
    tools = call(
        prepare_kernel,
        "prepare",
        [((128, 1024), BF), ((128, 512), BF), ((512, 256), BF)],
        (pack, *packs),
    )
    mine, *tools = lax.optimization_barrier((mine, *tools))
    swap = [(0, 1), (1, 0)]
    other = lax.ppermute(mine, "core", swap)
    block, pair = ((4, 128, 128), BF), ((2, 128, 128), BF)
    sums, cross, early = call(
        early_kernel,
        "early",
        [((512, 256), F32), ((128, 1024), F32), block],
        (mine, *tools),
        moved=8_000_000,
    )
    send, late, *totals = call(
        late_kernel,
        "late",
        [((32, 32, 128), BF), block, ((144, 128), BF), ((144, 128), BF)],
        (other, *tools, sums, cross),
        moved=8_000_000,
    )
    moved = []
    for i in range(2):
        pairs = [
            (c * 8 + y, c * 8 + (((y & 6) + PLACES[c][y & 1][i]) & 7)) for c in range(2) for y in range(8)
        ]
        moved.append(lax.ppermute(totals[i], ("core", "yh", "yl"), pairs))
    got_core = lax.ppermute(late, "core", swap)
    keep, give = call(
        half_kernel, "half", [((80, 128), F32), ((80, 128), BF)], tuple(moved), flops=2 * 10**9
    )
    half = lax.ppermute(give, "core", swap)
    got = lax.all_to_all(send, NEAR, 0, 0, tiled=True)
    got, half, got_core = lax.optimization_barrier((got, half, got_core))
    (send,) = call(middle_kernel, "middle", [((16, 88, 128), BF)], (got, keep, half))
    gives = call(second_kernel, "second", [pair, pair, pair], (early, got_core))
    got_x = lax.ppermute(gives[0], "xl", swap)
    got_y = lax.ppermute(gives[1], "yl", swap)
    got_xy = lax.ppermute(gives[2], ("xl", "yl"), [(0, 3), (1, 2), (2, 1), (3, 0)])
    got = lax.all_to_all(send, FAR, 0, 0, tiled=True)
    got, got_x, got_y, got_xy = lax.optimization_barrier((got, got_x, got_y, got_xy))
    cross, fresh = call(
        finish_kernel,
        "finish",
        [((2, 1024), F32), ((64, 128), F32)],
        (got, codebook[0].T),
    )
    fresh_other = lax.ppermute(fresh, "core", swap)
    (recon,) = call(
        home_kernel, "home", [((128, 1024), BF)], (early, got_core, got_x, got_y, got_xy)
    )
    fresh_other, recon = lax.optimization_barrier((fresh_other, recon))
    (new_codes,) = call(codes_kernel, "codes", [((64, 256), F32)], (fresh, fresh_other))
    return recon, new_codes.T[None], cross


def solution(mesh):
    fine = Mesh(mesh.devices.reshape(SIZES), NAMES)
    rows = P(DP + SUB, None)
    return jax.shard_map(
        per_device,
        mesh=fine,
        in_specs=(rows, P(None, SUB), P(SUB, None, None)),
        out_specs=(rows, P(SUB, None, None), rows),
        check_vma=False,
    )
```

```python
import functools

import jax
import jax.numpy as jnp
from jax import lax
from jax.experimental import pallas as pl
from jax.experimental.pallas import tpu as pltpu
from jax.sharding import Mesh
from jax.sharding import PartitionSpec as P

SIZES = (8, 2, 2, 2, 4, 2)
NAMES = ("z", "xh", "core", "xl", "yh", "yl")
DP = ("z", "xh", "core")
SUB = ("xl", "yh", "yl")
PLACES = (((0, 5), (1, 4)), ((6, 7), (3, 2)))
FAR = ("z", "xh")
NEAR = ("core", "xl", "yh", "yl")
BF = jnp.bfloat16
F32 = jnp.float32
NT = (((1,), (1,)), ((), ()))
VMEM = pl.BlockSpec(memory_space=pltpu.VMEM)
ANY = pl.BlockSpec(memory_space=pl.ANY)


def half_mask(shape):
    return lax.broadcasted_iota(jnp.int32, shape, len(shape) - 1) < 64


def swap_halves(x):
    return pltpu.roll(x, 64, 1)


def split(x):
    high = x.astype(BF).astype(F32)
    return high, x - high


def open_kernel(samples, turn_t, codes_t, pack, copies, done):
    moves = [pltpu.make_async_copy(samples, copies.at[n], done.at[n]) for n in range(4)]
    for move in moves:
        move.start()
    codes = codes_t[...]
    square = jnp.sum(codes * codes, axis=0, keepdims=True)
    high = square.astype(BF).astype(F32)
    mid = (square - high).astype(BF).astype(F32)
    low = square - high - mid
    squares = jnp.concatenate([high, mid, low, jnp.zeros((13, 256), F32)], axis=0).astype(BF)
    pack[:, 0:1024] = turn_t[...]
    pack[:, 1024:1280] = codes.astype(BF)
    pack[0:16, 1280:] = squares[:, :128]
    pack[16:32, 1280:] = squares[:, 128:]
    pack[32:64, 1280:] = jnp.zeros((32, 128), BF)
    for move in moves:
        move.wait()


def prepare_kernel(pack, first, second, turn, codes_t, left):
    core = lax.axis_index("core")
    w0, w1, w2 = pack[...], first[...], second[...]
    wa = jnp.where(core == 0, w0, w1)
    wb = jnp.where(core == 0, w1, w2)
    turn[0:64, :] = wa[:, :1024]
    turn[64:128, :] = wb[:, :1024]
    zero = jnp.zeros((64, 256), BF)
    both = jnp.concatenate(
        [
            jnp.concatenate([wa[:, 1024:1280], zero], axis=1),
            jnp.concatenate([zero, wb[:, 1024:1280]], axis=1),
        ],
        axis=0,
    )
    codes_t[...] = both
    squares = jnp.concatenate(
        [wa[0:16, 1280:], wa[16:32, 1280:], wb[0:16, 1280:], wb[16:32, 1280:]], axis=1
    )
    left[...] = jnp.concatenate([both * BF(-2.0), squares, jnp.zeros((112, 512), BF)], axis=0).T


def assign_rows(samples, turn, codes_t, left, sums, cross, put):
    rows, chunk = 512, 256
    lane = lax.broadcasted_iota(jnp.int32, (chunk, 128), 1)
    three = jnp.where(lane < 3, 1.0, 0.0).astype(BF)
    ones = jnp.ones((chunk, 128), BF)
    row16 = lax.broadcasted_iota(jnp.int32, (16, 256), 0)
    pick = (lax.broadcasted_iota(jnp.int32, (16, 256), 1) & 64) == 0
    pick = jnp.where(pick == (row16 == 0), 1.0, 0.0).astype(BF)
    for c in range(rows // chunk):
        x = samples[c * chunk : (c + 1) * chunk, :]
        rot = lax.dot_general(x, turn[...], NT, preferred_element_type=F32).astype(BF)
        square_high, square_low = split(jnp.square(rot.astype(F32)))
        square = jnp.concatenate([square_high, square_low], axis=1).astype(BF)
        row_square = lax.dot_general(pick, square, NT, preferred_element_type=F32)
        near = lax.dot_general(
            left[...], jnp.concatenate([rot, three], axis=1), NT, preferred_element_type=F32
        )
        parts = []
        for i in range(2):
            logits = -0.125 * (row_square[i : i + 1] + near[i * 256 : (i + 1) * 256])
            e = jnp.exp(logits - jnp.max(logits, axis=0, keepdims=True))
            parts.append((e * (1.0 / jnp.sum(e, axis=0, keepdims=True))).astype(BF))
        weights = jnp.concatenate(parts, axis=0)
        rebuilt = jnp.dot(codes_t[...], weights, preferred_element_type=F32).astype(BF)
        s = jnp.dot(weights, jnp.concatenate([rot, ones], axis=1), preferred_element_type=F32)
        k = jnp.dot(rebuilt, x, preferred_element_type=F32)
        sums = s if sums is None else sums + s
        cross = k if cross is None else cross + k
        back = rebuilt.T
        put(2 * c, back[:128])
        put(2 * c + 1, back[128:])
    return sums, cross


def early_kernel(samples, turn, codes_t, left, sums, cross, recon):
    def put(block, tile):
        recon[block] = tile

    sums[...], cross[...] = assign_rows(samples, turn, codes_t, left, None, None, put)


def late_kernel(samples, turn, codes_t, left, sums, cross, send, recon, sums_a, sums_b):
    def put(block, tile):
        recon[block] = tile

    sums, cross = assign_rows(samples, turn, codes_t, left, sums[...], cross[...], put)
    cross = cross.astype(BF)
    r = lax.broadcasted_iota(jnp.int32, (256, 256), 0)
    wanted = ((r & 4) << 5) | ((r & 2) << 5) | ((r >> 3) << 1) | (r & 1)
    order = jnp.where(lax.broadcasted_iota(jnp.int32, (256, 256), 1) == wanted, 1.0, 0.0).astype(BF)
    pieces = [
        lax.dot_general(order, cross[:, n * 256 : (n + 1) * 256], NT, preferred_element_type=F32)
        for n in range(4)
    ]
    for d in range(32):
        tiles = [piece[8 * d : 8 * d + 8] for piece in pieces]
        send[d] = jnp.concatenate(tiles, axis=0).astype(BF)
    low = half_mask((64, 128))
    diagonal = (
        lax.broadcasted_iota(jnp.int32, (128, 128), 0)
        == lax.broadcasted_iota(jnp.int32, (128, 128), 1)
    )
    for i, out in enumerate((sums_a, sums_b)):
        lines = []
        for h in range(2):
            at = i * 256 + h * 128
            a, b = sums[at : at + 64, :128], sums[at + 64 : at + 128, :128]
            if i == 0:
                tile = jnp.where(low, a, swap_halves(b))
            else:
                tile = jnp.where(low, swap_halves(a), b)
            out[h * 64 : h * 64 + 64, :] = tile.astype(BF)
            count = jnp.where(diagonal, sums[at : at + 128, 128:], 0.0)
            lines += split(jnp.sum(count, axis=0, keepdims=True))
        out[128:144, :] = jnp.concatenate(lines + [jnp.zeros((12, 128), F32)], axis=0).astype(BF)


def half_kernel(first, second, keep, give):
    core = lax.axis_index("core")
    both = first[...].astype(F32) + second[...].astype(F32)
    empty = jnp.zeros((14, 128), F32)
    halves = []
    for h in range(2):
        line = both[128 + 2 * h : 129 + 2 * h] + both[129 + 2 * h : 130 + 2 * h]
        halves.append(jnp.concatenate([both[h * 64 : h * 64 + 64], *split(line), empty], axis=0))
    keep[...] = jnp.where(core == 0, halves[0], halves[1])
    give[...] = jnp.where(core == 0, halves[1], halves[0]).astype(BF)


def arrange(low, a, b, c, d):
    turned = swap_halves(b)
    return [jnp.where(low, a, turned), swap_halves(d), jnp.where(low, turned, a), c]


def middle_kernel(got, keep, half, send):
    low = half_mask((32, 128))
    columns = []
    for xl in range(2):
        total = [jnp.zeros((32, 128), F32)] * 4
        for yh in range(4):
            blocks = [got[core * 16 + xl * 8 + yh * 2 + yl].astype(F32) for core in range(2) for yl in range(2)]
            for p, tile in enumerate(arrange(low, *blocks)):
                total[(yh + p) & 3] += tile
        columns += total
    r = lax.broadcasted_iota(jnp.int32, (256, 256), 0)
    wanted = (((r >> 1) & 7) << 5) | ((r >> 4) << 1) | (r & 1)
    order = jnp.where(lax.broadcasted_iota(jnp.int32, (256, 256), 1) == wanted, 1.0, 0.0).astype(BF)
    cross = jnp.dot(
        order, jnp.concatenate(columns, axis=0).astype(BF), preferred_element_type=F32
    ).astype(BF)
    both = keep[...] + half[...].astype(F32)
    line = both[64:65] + both[65:66]
    both = jnp.concatenate([both[:64], *split(line), jnp.zeros((6, 128), F32)], axis=0).astype(BF)
    for q in range(16):
        send[q, 0:16, :] = cross[q * 16 : q * 16 + 16]
        send[q, 16:88, :] = both


def finish_kernel(got, codes_t, cross, fresh):
    total = jnp.sum(got[...].astype(F32), axis=0)
    for n in range(8):
        cross[:, n * 128 : (n + 1) * 128] = total[2 * n : 2 * n + 2]
    sums, count = total[16:80], total[80:81] + total[81:82]
    sums = jnp.concatenate([sums, swap_halves(sums)], axis=0).T[:64]
    own = jnp.where(lax.axis_index("core") == 0, codes_t[:, :128], codes_t[:, 128:])
    fresh[...] = (sums + own) / (count + 1.0)


def codes_kernel(mine, other, codes_t):
    a, b = mine[...], other[...]
    codes_t[:, :128] = jnp.where(lax.axis_index("core") == 0, a, b)
    codes_t[:, 128:] = jnp.where(lax.axis_index("core") == 0, b, a)


def second_kernel(early, got_core, give_x, give_y, give_xy):
    xl, yl = lax.axis_index("xl"), lax.axis_index("yl")
    for n, block in enumerate((early, got_core)):
        give_x[n] = block[(1 - xl) * 2 + yl]
        give_y[n] = block[xl * 2 + 1 - yl]
        give_xy[n] = block[(1 - xl) * 2 + 1 - yl]


def home_kernel(early, got_core, got_x, got_y, got_xy, recon):
    core, xl = lax.axis_index("core"), lax.axis_index("xl")
    yh, yl = lax.axis_index("yh"), lax.axis_index("yl")
    low = half_mask((128, 128))
    own = [early[xl * 2 + yl], got_core[xl * 2 + yl]]
    for across, (same, far) in enumerate(((own, got_y), (got_x, got_xy))):
        blocks = []
        for c in range(2):
            near_c = jnp.where(core == c, same[0], same[1])
            far_c = jnp.where(core == c, far[0], far[1])
            for y in range(2):
                blocks.append(jnp.where(yl == y, near_c, far_c).astype(F32))
        side = (1 - xl) if across else xl
        for p, tile in enumerate(arrange(low, *blocks)):
            at = pl.multiple_of((side * 4 + ((yh + p) & 3)) * 128, 128)
            recon[:, pl.ds(at, 128)] = tile.astype(BF)


def call(kernel, name, outs, args, flops=0, moved=0):
    return pl.pallas_call(
        kernel,
        out_shape=tuple(jax.ShapeDtypeStruct(*o) for o in outs),
        in_specs=[VMEM] * len(args),
        out_specs=(VMEM,) * len(outs),
        compiler_params=pltpu.CompilerParams(vmem_limit_bytes=40 * 1024 * 1024),
        cost_estimate=pl.CostEstimate(flops=flops, bytes_accessed=moved, transcendentals=0),
        name=name,
    )(*args)


def per_device(samples, rotation, codebook):
    pack, copies = pl.pallas_call(
        open_kernel,
        out_shape=(
            jax.ShapeDtypeStruct((64, 1408), BF),
            jax.ShapeDtypeStruct((4, 128, 1024), BF),
        ),
        in_specs=[VMEM, VMEM, VMEM],
        out_specs=(VMEM, ANY),
        scratch_shapes=[pltpu.SemaphoreType.DMA((4,))],
        compiler_params=pltpu.CompilerParams(vmem_limit_bytes=60 * 1024 * 1024),
        name="open",
    )(samples, rotation.T, codebook[0].T)
    packs = []
    for steps in ((3, 2), (None, 1)):
        pairs = [
            (c * 8 + ((y + step if y & 1 else y - step) & 7), c * 8 + y)
            for c, step in enumerate(steps)
            for y in range(8)
            if step is not None
        ]
        packs.append(lax.ppermute(pack, ("core", "yh", "yl"), pairs))
    mine = lax.all_to_all(copies, ("xl", "yl"), 0, 0, tiled=True).reshape(512, 1024)
    tools = call(
        prepare_kernel,
        "prepare",
        [((128, 1024), BF), ((128, 512), BF), ((512, 256), BF)],
        (pack, *packs),
    )
    mine, *tools = lax.optimization_barrier((mine, *tools))
    swap = [(0, 1), (1, 0)]
    other = lax.ppermute(mine, "core", swap)
    block, pair = ((4, 128, 128), BF), ((2, 128, 128), BF)
    sums, cross, early = call(
        early_kernel,
        "early",
        [((512, 256), F32), ((128, 1024), F32), block],
        (mine, *tools),
        moved=8_000_000,
    )
    send, late, *totals = call(
        late_kernel,
        "late",
        [((32, 32, 128), BF), block, ((144, 128), BF), ((144, 128), BF)],
        (other, *tools, sums, cross),
        moved=8_000_000,
    )
    moved = []
    for i in range(2):
        pairs = [
            (c * 8 + y, c * 8 + (((y & 6) + PLACES[c][y & 1][i]) & 7)) for c in range(2) for y in range(8)
        ]
        moved.append(lax.ppermute(totals[i], ("core", "yh", "yl"), pairs))
    got_core = lax.ppermute(late, "core", swap)
    keep, give = call(
        half_kernel, "half", [((80, 128), F32), ((80, 128), BF)], tuple(moved), flops=2 * 10**9
    )
    half = lax.ppermute(give, "core", swap)
    got = lax.all_to_all(send, NEAR, 0, 0, tiled=True)
    got, half, got_core = lax.optimization_barrier((got, half, got_core))
    (send,) = call(middle_kernel, "middle", [((16, 88, 128), BF)], (got, keep, half))
    gives = call(second_kernel, "second", [pair, pair, pair], (early, got_core))
    got_x = lax.ppermute(gives[0], "xl", swap)
    got_y = lax.ppermute(gives[1], "yl", swap)
    got_xy = lax.ppermute(gives[2], ("xl", "yl"), [(0, 3), (1, 2), (2, 1), (3, 0)])
    got = lax.all_to_all(send, FAR, 0, 0, tiled=True)
    got, got_x, got_y, got_xy = lax.optimization_barrier((got, got_x, got_y, got_xy))
    cross, fresh = call(
        finish_kernel,
        "finish",
        [((2, 1024), F32), ((64, 128), F32)],
        (got, codebook[0].T),
    )
    fresh_other = lax.ppermute(fresh, "core", swap)
    (recon,) = call(
        home_kernel, "home", [((128, 1024), BF)], (early, got_core, got_x, got_y, got_xy)
    )
    fresh_other, recon = lax.optimization_barrier((fresh_other, recon))
    (new_codes,) = call(codes_kernel, "codes", [((64, 256), F32)], (fresh, fresh_other))
    return recon, new_codes.T[None], cross


def solution(mesh):
    fine = Mesh(mesh.devices.reshape(SIZES), NAMES)
    rows = P(DP + SUB, None)
    return jax.shard_map(
        per_device,
        mesh=fine,
        in_specs=(rows, P(None, SUB), P(SUB, None, None)),
        out_specs=(rows, P(SUB, None, None), rows),
        check_vma=False,
    )
```

```python
import functools

import jax
import jax.numpy as jnp
from jax import lax
from jax.experimental import pallas as pl
from jax.experimental.pallas import tpu as pltpu
from jax.sharding import Mesh
from jax.sharding import PartitionSpec as P

SIZES = (4, 2, 2, 2, 2, 8)
NAMES = ("zh", "zl", "xh", "core", "xl", "y")
DP = ("zh", "zl", "xh", "core")
SUB = ("xl", "y")
OFFSETS = (((0, -1), (4, 1)), ((2, -3), (-2, 3)))
FAR = ("zh", "zl", "xh")
NEAR = ("core", "xl", "y")
LINE = ("zl", "core", "y")
BF = jnp.bfloat16
F32 = jnp.float32
NT = (((1,), (1,)), ((), ()))
VMEM = pl.BlockSpec(memory_space=pltpu.VMEM)


def half_mask(shape):
    return lax.broadcasted_iota(jnp.int32, shape, len(shape) - 1) < 64


def swap_halves(x):
    return pltpu.roll(x, 64, 1)


def split(x):
    high = x.astype(BF).astype(F32)
    return high, x - high


def open_kernel(samples, turn_t, codes_t, pack, copies):
    for n in range(4):
        copies[n] = samples[...]
    codes = codes_t[...]
    square = jnp.sum(codes * codes, axis=0, keepdims=True)
    high = square.astype(BF).astype(F32)
    mid = (square - high).astype(BF).astype(F32)
    low = square - high - mid
    squares = jnp.concatenate([high, mid, low, jnp.zeros((13, 256), F32)], axis=0).astype(BF)
    pack[:, 0:1024] = turn_t[...]
    pack[:, 1024:1280] = codes.astype(BF)
    pack[0:16, 1280:] = squares[:, :128]
    pack[16:32, 1280:] = squares[:, 128:]
    pack[32:64, 1280:] = jnp.zeros((32, 128), BF)


def prepare_kernel(pack, first, second, turn, codes_t, left):
    near = lax.axis_index("zl") + lax.axis_index("core")
    wa = jnp.where(near == 0, pack[...], first[...])
    wb = second[...]
    turn[0:64, :] = wa[:, :1024]
    turn[64:128, :] = wb[:, :1024]
    zero = jnp.zeros((64, 256), BF)
    both = jnp.concatenate(
        [
            jnp.concatenate([wa[:, 1024:1280], zero], axis=1),
            jnp.concatenate([zero, wb[:, 1024:1280]], axis=1),
        ],
        axis=0,
    )
    codes_t[...] = both
    squares = jnp.concatenate(
        [wa[0:16, 1280:], wa[16:32, 1280:], wb[0:16, 1280:], wb[16:32, 1280:]], axis=1
    )
    left[...] = jnp.concatenate([both * BF(-2.0), squares, jnp.zeros((112, 512), BF)], axis=0).T


def assign_rows(samples, turn, codes_t, left, sums, cross, put):
    rows, chunk = 512, 256
    lane = lax.broadcasted_iota(jnp.int32, (chunk, 128), 1)
    three = jnp.where(lane < 3, 1.0, 0.0).astype(BF)
    ones = jnp.ones((chunk, 128), BF)
    row16 = lax.broadcasted_iota(jnp.int32, (16, 256), 0)
    pick = (lax.broadcasted_iota(jnp.int32, (16, 256), 1) & 64) == 0
    pick = jnp.where(pick == (row16 == 0), 1.0, 0.0).astype(BF)
    for c in range(rows // chunk):
        x = samples[c * chunk : (c + 1) * chunk, :]
        rot = lax.dot_general(x, turn[...], NT, preferred_element_type=F32).astype(BF)
        square_high, square_low = split(jnp.square(rot.astype(F32)))
        square = jnp.concatenate([square_high, square_low], axis=1).astype(BF)
        row_square = lax.dot_general(pick, square, NT, preferred_element_type=F32)
        near = lax.dot_general(
            left[...], jnp.concatenate([rot, three], axis=1), NT, preferred_element_type=F32
        )
        parts = []
        for i in range(2):
            logits = -0.125 * (row_square[i : i + 1] + near[i * 256 : (i + 1) * 256])
            e = jnp.exp(logits - jnp.max(logits, axis=0, keepdims=True))
            parts.append((e * (1.0 / jnp.sum(e, axis=0, keepdims=True))).astype(BF))
        weights = jnp.concatenate(parts, axis=0)
        rebuilt = jnp.dot(codes_t[...], weights, preferred_element_type=F32).astype(BF)
        s = jnp.dot(weights, jnp.concatenate([rot, ones], axis=1), preferred_element_type=F32)
        k = jnp.dot(rebuilt, x, preferred_element_type=F32)
        sums = s if sums is None else sums + s
        cross = k if cross is None else cross + k
        back = rebuilt.T
        put(2 * c, back[:128])
        put(2 * c + 1, back[128:])
    return sums, cross


def early_kernel(samples, turn, codes_t, left, sums, cross, recon):
    def put(block, tile):
        recon[block] = tile

    sums[...], cross[...] = assign_rows(samples, turn, codes_t, left, None, None, put)


def late_kernel(samples, turn, codes_t, left, sums, cross, send, recon, sums_a, sums_b):
    def put(block, tile):
        recon[block] = tile

    sums, cross = assign_rows(samples, turn, codes_t, left, sums[...], cross[...], put)
    cross = cross.astype(BF)
    r = lax.broadcasted_iota(jnp.int32, (256, 256), 0)
    wanted = ((r & 4) << 5) | ((r & 2) << 5) | ((r >> 3) << 1) | (r & 1)
    order = jnp.where(lax.broadcasted_iota(jnp.int32, (256, 256), 1) == wanted, 1.0, 0.0).astype(BF)
    pieces = [
        lax.dot_general(order, cross[:, n * 256 : (n + 1) * 256], NT, preferred_element_type=F32)
        for n in range(4)
    ]
    for d in range(32):
        tiles = [piece[8 * d : 8 * d + 8] for piece in pieces]
        send[d] = jnp.concatenate(tiles, axis=0).astype(BF)
    low = half_mask((64, 128))
    diagonal = (
        lax.broadcasted_iota(jnp.int32, (128, 128), 0)
        == lax.broadcasted_iota(jnp.int32, (128, 128), 1)
    )
    for i, out in enumerate((sums_a, sums_b)):
        lines = []
        for h in range(2):
            at = i * 256 + h * 128
            a, b = sums[at : at + 64, :128], sums[at + 64 : at + 128, :128]
            if i == 0:
                tile = jnp.where(low, a, swap_halves(b))
            else:
                tile = jnp.where(low, swap_halves(a), b)
            out[h * 64 : h * 64 + 64, :] = tile.astype(BF)
            count = jnp.where(diagonal, sums[at : at + 128, 128:], 0.0)
            lines += split(jnp.sum(count, axis=0, keepdims=True))
        out[128:144, :] = jnp.concatenate(lines + [jnp.zeros((12, 128), F32)], axis=0).astype(BF)


def half_kernel(first, second, keep, give):
    core = lax.axis_index("core")
    both = first[...].astype(F32) + second[...].astype(F32)
    empty = jnp.zeros((14, 128), F32)
    halves = []
    for h in range(2):
        line = both[128 + 2 * h : 129 + 2 * h] + both[129 + 2 * h : 130 + 2 * h]
        halves.append(jnp.concatenate([both[h * 64 : h * 64 + 64], *split(line), empty], axis=0))
    keep[...] = jnp.where(core == 0, halves[0], halves[1])
    give[...] = jnp.where(core == 0, halves[1], halves[0]).astype(BF)


def middle_kernel(got, keep, half, send, columns):
    low = half_mask((32, 128))
    for zl in range(2):

        @pl.when(lax.axis_index("zl") == zl)
        def _():
            for xl in range(2):
                even = [None] * 4
                odd = [None] * 4
                for y in range(8):
                    for core in range(2):
                        block = got[core * 16 + xl * 8 + y].astype(F32)
                        ends = [((y + step) & 7) >> 1 for step in OFFSETS[zl][core]]
                        if y & 1:
                            block = swap_halves(block)
                            ends.reverse()
                        for sums, p in zip((even, odd), ends):
                            sums[p] = block if sums[p] is None else sums[p] + block
                for p in range(4):
                    at = (xl * 4 + p) * 32
                    columns[at : at + 32, :] = jnp.where(low, even[p], odd[p])

    r = lax.broadcasted_iota(jnp.int32, (256, 256), 0)
    wanted = (((r >> 1) & 7) << 5) | ((r >> 4) << 1) | (r & 1)
    order = jnp.where(lax.broadcasted_iota(jnp.int32, (256, 256), 1) == wanted, 1.0, 0.0).astype(BF)
    cross = jnp.dot(
        order, columns[...].astype(BF), preferred_element_type=F32
    ).astype(BF)
    both = keep[...] + half[...].astype(F32)
    line = both[64:65] + both[65:66]
    both = jnp.concatenate([both[:64], *split(line), jnp.zeros((6, 128), F32)], axis=0).astype(BF)
    for q in range(16):
        send[q, 0:16, :] = cross[q * 16 : q * 16 + 16]
        send[q, 16:88, :] = both


def finish_kernel(got, codes_t, cross, fresh):
    total = jnp.sum(got[...].astype(F32), axis=0)
    for n in range(8):
        cross[:, n * 128 : (n + 1) * 128] = total[2 * n : 2 * n + 2]
    sums, count = total[16:80], total[80:81] + total[81:82]
    sums = jnp.concatenate([sums, swap_halves(sums)], axis=0).T[:64]
    own = jnp.where(lax.axis_index("core") == 0, codes_t[:, :128], codes_t[:, 128:])
    fresh[...] = (sums + own) / (count + 1.0)


def codes_kernel(mine, other, codes_t):
    a, b = mine[...], other[...]
    codes_t[:, :128] = jnp.where(lax.axis_index("core") == 0, a, b)
    codes_t[:, 128:] = jnp.where(lax.axis_index("core") == 0, b, a)


def second_kernel(early, got_core, give_x, give_z, give_xz):
    zl, xl = lax.axis_index("zl"), lax.axis_index("xl")
    for n, block in enumerate((early, got_core)):
        give_x[n] = block[zl * 2 + 1 - xl]
        give_z[n] = block[(1 - zl) * 2 + xl]
        give_xz[n] = block[(1 - zl) * 2 + 1 - xl]


def home_kernel(early, got_core, got_x, got_z, got_xz, recon):
    zl, core = lax.axis_index("zl"), lax.axis_index("core")
    xl, y = lax.axis_index("xl"), lax.axis_index("y")
    low = half_mask((128, 128))
    is_odd = (y & 1) == 1
    own = [early[zl * 2 + xl], got_core[zl * 2 + xl]]
    for across, (same, far) in enumerate(((own, got_z), (got_x, got_xz))):
        blocks = []
        for z in range(2):
            for c in range(2):
                near_c = jnp.where(core == c, same[0], same[1])
                far_c = jnp.where(core == c, far[0], far[1])
                block = jnp.where(zl == z, near_c, far_c).astype(F32)
                blocks.append(jnp.where(is_odd, swap_halves(block), block))
        side = (1 - xl) if across else xl
        for p in range(4):
            ends = []
            for i in range(2):
                found = []
                for parity in range(2):
                    for n in range(4):
                        step = OFFSETS[n >> 1][n & 1][i ^ parity]
                        if ((parity + step) & 7) >> 1 == p:
                            found.append(blocks[n])
                ends.append(found[0] if found[0] is found[1] else jnp.where(is_odd, found[1], found[0]))
            at = pl.multiple_of((side * 4 + (((y >> 1) + p) & 3)) * 128, 128)
            recon[:, pl.ds(at, 128)] = jnp.where(low, *ends).astype(BF)


def call(kernel, name, outs, args, flops=0, moved=0, scratch=()):
    return pl.pallas_call(
        kernel,
        out_shape=tuple(jax.ShapeDtypeStruct(*o) for o in outs),
        in_specs=[VMEM] * len(args),
        out_specs=(VMEM,) * len(outs),
        scratch_shapes=list(scratch),
        compiler_params=pltpu.CompilerParams(vmem_limit_bytes=40 * 1024 * 1024),
        cost_estimate=pl.CostEstimate(flops=flops, bytes_accessed=moved, transcendentals=0),
        name=name,
    )(*args)


def per_device(samples, rotation, codebook):
    pack, copies = pl.pallas_call(
        open_kernel,
        out_shape=(
            jax.ShapeDtypeStruct((64, 1408), BF),
            jax.ShapeDtypeStruct((4, 128, 1024), BF),
        ),
        in_specs=[VMEM, VMEM, VMEM],
        out_specs=(VMEM, VMEM),
        compiler_params=pltpu.CompilerParams(vmem_limit_bytes=60 * 1024 * 1024),
        name="open",
    )(samples, rotation.T, codebook[0].T)
    packs, lines = [], []
    for i in range(2):
        lines.append(
            [
                (at + y, at + ((y + OFFSETS[at >> 4][(at >> 3) & 1][i]) & 7))
                for at in range(0, 32, 8)
                for y in range(8)
            ]
        )
        pairs = [(b, a) for a, b in lines[i] if i == 1 or a >= 8]
        packs.append(lax.ppermute(pack, LINE, pairs))
    mine = lax.all_to_all(copies, ("zl", "xl"), 0, 0, tiled=True).reshape(512, 1024)
    tools = call(
        prepare_kernel,
        "prepare",
        [((128, 1024), BF), ((128, 512), BF), ((512, 256), BF)],
        (pack, *packs),
    )
    mine, *tools = lax.optimization_barrier((mine, *tools))
    swap = [(0, 1), (1, 0)]
    other = lax.ppermute(mine, "core", swap)
    block, pair = ((4, 128, 128), BF), ((2, 128, 128), BF)
    sums, cross, early = call(
        early_kernel,
        "early",
        [((512, 256), F32), ((128, 1024), F32), block],
        (mine, *tools),
        moved=8_000_000,
    )
    send, late, *totals = call(
        late_kernel,
        "late",
        [((32, 32, 128), BF), block, ((144, 128), BF), ((144, 128), BF)],
        (other, *tools, sums, cross),
        moved=8_000_000,
    )
    moved = [lax.ppermute(totals[i], LINE, lines[i]) for i in range(2)]
    got_core = lax.ppermute(late, "core", swap)
    keep, give = call(
        half_kernel, "half", [((80, 128), F32), ((80, 128), BF)], tuple(moved), flops=2 * 10**9
    )
    half = lax.ppermute(give, "core", swap)
    got = lax.all_to_all(send, NEAR, 0, 0, tiled=True)
    got, half, got_core = lax.optimization_barrier((got, half, got_core))
    (send,) = call(
        middle_kernel,
        "middle",
        [((16, 88, 128), BF)],
        (got, keep, half),
        scratch=[pltpu.VMEM((256, 128), F32)],
    )
    gives = call(second_kernel, "second", [pair, pair, pair], (early, got_core))
    got_x = lax.ppermute(gives[0], "xl", swap)
    got_z = lax.ppermute(gives[1], "zl", swap)
    got_xz = lax.ppermute(gives[2], ("zl", "xl"), [(0, 3), (1, 2), (2, 1), (3, 0)])
    got = lax.all_to_all(send, FAR, 0, 0, tiled=True)
    got, got_x, got_z, got_xz = lax.optimization_barrier((got, got_x, got_z, got_xz))
    cross, fresh = call(
        finish_kernel,
        "finish",
        [((2, 1024), F32), ((64, 128), F32)],
        (got, codebook[0].T),
    )
    fresh_other = lax.ppermute(fresh, "core", swap)
    (recon,) = call(
        home_kernel, "home", [((128, 1024), BF)], (early, got_core, got_x, got_z, got_xz)
    )
    fresh_other, recon = lax.optimization_barrier((fresh_other, recon))
    (new_codes,) = call(codes_kernel, "codes", [((64, 256), F32)], (fresh, fresh_other))
    return recon, new_codes.T[None], cross


def solution(mesh):
    fine = Mesh(mesh.devices.reshape(SIZES), NAMES)
    rows = P(DP + SUB, None)
    return jax.shard_map(
        per_device,
        mesh=fine,
        in_specs=(rows, P(None, SUB), P(SUB, None, None)),
        out_specs=(rows, P(SUB, None, None), rows),
        check_vma=False,
    )
```

```python
import functools

import jax
import jax.numpy as jnp
from jax import lax
from jax.experimental import pallas as pl
from jax.experimental.pallas import tpu as pltpu
from jax.sharding import Mesh
from jax.sharding import PartitionSpec as P

SIZES = (8, 2, 2, 2, 4, 2)
NAMES = ("z", "xh", "core", "xl", "yh", "yl")
DP = ("z", "xh", "core")
SUB = ("xl", "yh", "yl")
PLACES = (((0, 5), (1, 4)), ((6, 7), (3, 2)))
FAR = ("z", "xh")
NEAR = ("core", "xl", "yh", "yl")
BF = jnp.bfloat16
F32 = jnp.float32
NT = (((1,), (1,)), ((), ()))
VMEM = pl.BlockSpec(memory_space=pltpu.VMEM)


def half_mask(shape):
    return lax.broadcasted_iota(jnp.int32, shape, len(shape) - 1) < 64


def swap_halves(x):
    return pltpu.roll(x, 64, 1)


def split(x):
    high = x.astype(BF).astype(F32)
    return high, x - high


def open_kernel(samples, turn_t, codes_t, pack, copies):
    for n in range(4):
        copies[n] = samples[...]
    codes = codes_t[...]
    square = jnp.sum(codes * codes, axis=0, keepdims=True)
    high = square.astype(BF).astype(F32)
    mid = (square - high).astype(BF).astype(F32)
    low = square - high - mid
    squares = jnp.concatenate([high, mid, low, jnp.zeros((13, 256), F32)], axis=0).astype(BF)
    pack[:, 0:1024] = turn_t[...]
    pack[:, 1024:1280] = codes.astype(BF)
    pack[0:16, 1280:] = squares[:, :128]
    pack[16:32, 1280:] = squares[:, 128:]
    pack[32:64, 1280:] = jnp.zeros((32, 128), BF)


def prepare_kernel(pack, first, second, turn, codes_t, left):
    core = lax.axis_index("core")
    w0, w1, w2 = pack[...], first[...], second[...]
    wa = jnp.where(core == 0, w0, w1)
    wb = jnp.where(core == 0, w1, w2)
    turn[0:64, :] = wa[:, :1024]
    turn[64:128, :] = wb[:, :1024]
    zero = jnp.zeros((64, 256), BF)
    both = jnp.concatenate(
        [
            jnp.concatenate([wa[:, 1024:1280], zero], axis=1),
            jnp.concatenate([zero, wb[:, 1024:1280]], axis=1),
        ],
        axis=0,
    )
    codes_t[...] = both
    squares = jnp.concatenate(
        [wa[0:16, 1280:], wa[16:32, 1280:], wb[0:16, 1280:], wb[16:32, 1280:]], axis=1
    )
    left[...] = jnp.concatenate([both * BF(-2.0), squares, jnp.zeros((112, 512), BF)], axis=0).T


def assign_rows(samples, turn, codes_t, left, sums, cross, put):
    rows, chunk = 512, 256
    lane = lax.broadcasted_iota(jnp.int32, (chunk, 128), 1)
    three = jnp.where(lane < 3, 1.0, 0.0).astype(BF)
    ones = jnp.ones((chunk, 128), BF)
    row16 = lax.broadcasted_iota(jnp.int32, (16, 256), 0)
    pick = (lax.broadcasted_iota(jnp.int32, (16, 256), 1) & 64) == 0
    pick = jnp.where(pick == (row16 == 0), 1.0, 0.0).astype(BF)
    for c in range(rows // chunk):
        x = samples[c * chunk : (c + 1) * chunk, :]
        rot = lax.dot_general(x, turn[...], NT, preferred_element_type=F32).astype(BF)
        square_high, square_low = split(jnp.square(rot.astype(F32)))
        square = jnp.concatenate([square_high, square_low], axis=1).astype(BF)
        row_square = lax.dot_general(pick, square, NT, preferred_element_type=F32)
        near = lax.dot_general(
            left[...], jnp.concatenate([rot, three], axis=1), NT, preferred_element_type=F32
        )
        parts = []
        for i in range(2):
            logits = -0.125 * (row_square[i : i + 1] + near[i * 256 : (i + 1) * 256])
            e = jnp.exp(logits - jnp.max(logits, axis=0, keepdims=True))
            parts.append((e * (1.0 / jnp.sum(e, axis=0, keepdims=True))).astype(BF))
        weights = jnp.concatenate(parts, axis=0)
        rebuilt = jnp.dot(codes_t[...], weights, preferred_element_type=F32).astype(BF)
        s = jnp.dot(weights, jnp.concatenate([rot, ones], axis=1), preferred_element_type=F32)
        k = jnp.dot(rebuilt, x, preferred_element_type=F32)
        sums = s if sums is None else sums + s
        cross = k if cross is None else cross + k
        back = rebuilt.T
        put(2 * c, back[:128])
        put(2 * c + 1, back[128:])
    return sums, cross


def early_kernel(samples, turn, codes_t, left, sums, cross, recon):
    def put(block, tile):
        recon[block] = tile

    sums[...], cross[...] = assign_rows(samples, turn, codes_t, left, None, None, put)


def late_kernel(samples, turn, codes_t, left, sums, cross, send, recon, sums_a, sums_b):
    def put(block, tile):
        recon[block] = tile

    sums, cross = assign_rows(samples, turn, codes_t, left, sums[...], cross[...], put)
    cross = cross.astype(BF)
    r = lax.broadcasted_iota(jnp.int32, (256, 256), 0)
    wanted = ((r & 4) << 5) | ((r & 2) << 5) | ((r >> 3) << 1) | (r & 1)
    order = jnp.where(lax.broadcasted_iota(jnp.int32, (256, 256), 1) == wanted, 1.0, 0.0).astype(BF)
    pieces = [
        lax.dot_general(order, cross[:, n * 256 : (n + 1) * 256], NT, preferred_element_type=F32)
        for n in range(4)
    ]
    for d in range(32):
        tiles = [piece[8 * d : 8 * d + 8] for piece in pieces]
        send[d] = jnp.concatenate(tiles, axis=0).astype(BF)
    low = half_mask((64, 128))
    diagonal = (
        lax.broadcasted_iota(jnp.int32, (128, 128), 0)
        == lax.broadcasted_iota(jnp.int32, (128, 128), 1)
    )
    for i, out in enumerate((sums_a, sums_b)):
        lines = []
        for h in range(2):
            at = i * 256 + h * 128
            a, b = sums[at : at + 64, :128], sums[at + 64 : at + 128, :128]
            if i == 0:
                tile = jnp.where(low, a, swap_halves(b))
            else:
                tile = jnp.where(low, swap_halves(a), b)
            out[h * 64 : h * 64 + 64, :] = tile.astype(BF)
            count = jnp.where(diagonal, sums[at : at + 128, 128:], 0.0)
            lines += split(jnp.sum(count, axis=0, keepdims=True))
        out[128:144, :] = jnp.concatenate(lines + [jnp.zeros((12, 128), F32)], axis=0).astype(BF)


def half_kernel(first, second, keep, give):
    core = lax.axis_index("core")
    both = first[...].astype(F32) + second[...].astype(F32)
    empty = jnp.zeros((14, 128), F32)
    halves = []
    for h in range(2):
        line = both[128 + 2 * h : 129 + 2 * h] + both[129 + 2 * h : 130 + 2 * h]
        halves.append(jnp.concatenate([both[h * 64 : h * 64 + 64], *split(line), empty], axis=0))
    keep[...] = jnp.where(core == 0, halves[0], halves[1])
    give[...] = jnp.where(core == 0, halves[1], halves[0]).astype(BF)


def arrange(low, a, b, c, d):
    turned = swap_halves(b)
    return [jnp.where(low, a, turned), swap_halves(d), jnp.where(low, turned, a), c]


def middle_kernel(got, keep, half, send):
    low = half_mask((32, 128))
    columns = []
    for xl in range(2):
        total = [jnp.zeros((32, 128), F32)] * 4
        for yh in range(4):
            blocks = [got[core * 16 + xl * 8 + yh * 2 + yl].astype(F32) for core in range(2) for yl in range(2)]
            for p, tile in enumerate(arrange(low, *blocks)):
                total[(yh + p) & 3] += tile
        columns += total
    r = lax.broadcasted_iota(jnp.int32, (256, 256), 0)
    wanted = (((r >> 1) & 7) << 5) | ((r >> 4) << 1) | (r & 1)
    order = jnp.where(lax.broadcasted_iota(jnp.int32, (256, 256), 1) == wanted, 1.0, 0.0).astype(BF)
    cross = jnp.dot(
        order, jnp.concatenate(columns, axis=0).astype(BF), preferred_element_type=F32
    ).astype(BF)
    both = keep[...] + half[...].astype(F32)
    line = both[64:65] + both[65:66]
    both = jnp.concatenate([both[:64], *split(line), jnp.zeros((6, 128), F32)], axis=0).astype(BF)
    for q in range(16):
        send[q, 0:16, :] = cross[q * 16 : q * 16 + 16]
        send[q, 16:88, :] = both


def finish_kernel(got, codes_t, cross, fresh):
    total = jnp.sum(got[...].astype(F32), axis=0)
    for n in range(8):
        cross[:, n * 128 : (n + 1) * 128] = total[2 * n : 2 * n + 2]
    sums, count = total[16:80], total[80:81] + total[81:82]
    sums = jnp.concatenate([sums, swap_halves(sums)], axis=0).T[:64]
    own = jnp.where(lax.axis_index("core") == 0, codes_t[:, :128], codes_t[:, 128:])
    fresh[...] = (sums + own) / (count + 1.0)


def codes_kernel(mine, other, codes_t):
    a, b = mine[...], other[...]
    codes_t[:, :128] = jnp.where(lax.axis_index("core") == 0, a, b)
    codes_t[:, 128:] = jnp.where(lax.axis_index("core") == 0, b, a)


def second_kernel(early, got_core, give_x, give_y, give_xy):
    xl, yl = lax.axis_index("xl"), lax.axis_index("yl")
    for n, block in enumerate((early, got_core)):
        give_x[n] = block[(1 - xl) * 2 + yl]
        give_y[n] = block[xl * 2 + 1 - yl]
        give_xy[n] = block[(1 - xl) * 2 + 1 - yl]


def home_kernel(early, got_core, got_x, got_y, got_xy, recon):
    core, xl = lax.axis_index("core"), lax.axis_index("xl")
    yh, yl = lax.axis_index("yh"), lax.axis_index("yl")
    low = half_mask((128, 128))
    own = [early[xl * 2 + yl], got_core[xl * 2 + yl]]
    for across, (same, far) in enumerate(((own, got_y), (got_x, got_xy))):
        blocks = []
        for c in range(2):
            near_c = jnp.where(core == c, same[0], same[1])
            far_c = jnp.where(core == c, far[0], far[1])
            for y in range(2):
                blocks.append(jnp.where(yl == y, near_c, far_c).astype(F32))
        side = (1 - xl) if across else xl
        for p, tile in enumerate(arrange(low, *blocks)):
            at = pl.multiple_of((side * 4 + ((yh + p) & 3)) * 128, 128)
            recon[:, pl.ds(at, 128)] = tile.astype(BF)


def call(kernel, name, outs, args, flops=0, moved=0):
    return pl.pallas_call(
        kernel,
        out_shape=tuple(jax.ShapeDtypeStruct(*o) for o in outs),
        in_specs=[VMEM] * len(args),
        out_specs=(VMEM,) * len(outs),
        compiler_params=pltpu.CompilerParams(vmem_limit_bytes=40 * 1024 * 1024),
        cost_estimate=pl.CostEstimate(flops=flops, bytes_accessed=moved, transcendentals=0),
        name=name,
    )(*args)


def per_device(samples, rotation, codebook):
    pack, copies = pl.pallas_call(
        open_kernel,
        out_shape=(
            jax.ShapeDtypeStruct((64, 1408), BF),
            jax.ShapeDtypeStruct((4, 128, 1024), BF),
        ),
        in_specs=[VMEM, VMEM, VMEM],
        out_specs=(VMEM, VMEM),
        compiler_params=pltpu.CompilerParams(vmem_limit_bytes=60 * 1024 * 1024),
        name="open",
    )(samples, rotation.T, codebook[0].T)
    packs = []
    for steps in ((3, 2), (None, 1)):
        pairs = [
            (c * 8 + ((y + step if y & 1 else y - step) & 7), c * 8 + y)
            for c, step in enumerate(steps)
            for y in range(8)
            if step is not None
        ]
        packs.append(lax.ppermute(pack, ("core", "yh", "yl"), pairs))
    mine = lax.all_to_all(copies, ("xl", "yl"), 0, 0, tiled=True).reshape(512, 1024)
    tools = call(
        prepare_kernel,
        "prepare",
        [((128, 1024), BF), ((128, 512), BF), ((512, 256), BF)],
        (pack, *packs),
    )
    mine, *tools = lax.optimization_barrier((mine, *tools))
    swap = [(0, 1), (1, 0)]
    other = lax.ppermute(mine, "core", swap)
    block, pair = ((4, 128, 128), BF), ((2, 128, 128), BF)
    sums, cross, early = call(
        early_kernel,
        "early",
        [((512, 256), F32), ((128, 1024), F32), block],
        (mine, *tools),
        moved=8_000_000,
    )
    send, late, *totals = call(
        late_kernel,
        "late",
        [((32, 32, 128), BF), block, ((144, 128), BF), ((144, 128), BF)],
        (other, *tools, sums, cross),
        moved=8_000_000,
    )
    moved = []
    for i in range(2):
        pairs = [
            (c * 8 + y, c * 8 + (((y & 6) + PLACES[c][y & 1][i]) & 7)) for c in range(2) for y in range(8)
        ]
        moved.append(lax.ppermute(totals[i], ("core", "yh", "yl"), pairs))
    got_core = lax.ppermute(late, "core", swap)
    keep, give = call(
        half_kernel, "half", [((80, 128), F32), ((80, 128), BF)], tuple(moved), flops=2 * 10**9
    )
    half = lax.ppermute(give, "core", swap)
    got = lax.all_to_all(send, NEAR, 0, 0, tiled=True)
    got, half, got_core = lax.optimization_barrier((got, half, got_core))
    (send,) = call(middle_kernel, "middle", [((16, 88, 128), BF)], (got, keep, half))
    gives = call(second_kernel, "second", [pair, pair, pair], (early, got_core))
    got_x = lax.ppermute(gives[0], "xl", swap)
    got_y = lax.ppermute(gives[1], "yl", swap)
    got_xy = lax.ppermute(gives[2], ("xl", "yl"), [(0, 3), (1, 2), (2, 1), (3, 0)])
    got = lax.all_to_all(send, FAR, 0, 0, tiled=True)
    got, got_x, got_y, got_xy = lax.optimization_barrier((got, got_x, got_y, got_xy))
    cross, fresh = call(
        finish_kernel,
        "finish",
        [((2, 1024), F32), ((64, 128), F32)],
        (got, codebook[0].T),
    )
    fresh_other = lax.ppermute(fresh, "core", swap)
    (recon,) = call(
        home_kernel, "home", [((128, 1024), BF)], (early, got_core, got_x, got_y, got_xy)
    )
    fresh_other, recon = lax.optimization_barrier((fresh_other, recon))
    (new_codes,) = call(codes_kernel, "codes", [((64, 256), F32)], (fresh, fresh_other))
    return recon, new_codes.T[None], cross


def solution(mesh):
    fine = Mesh(mesh.devices.reshape(SIZES), NAMES)
    rows = P(DP + SUB, None)
    return jax.shard_map(
        per_device,
        mesh=fine,
        in_specs=(rows, P(None, SUB), P(SUB, None, None)),
        out_specs=(rows, P(SUB, None, None), rows),
        check_vma=False,
    )
```

```python
import functools

import jax
import jax.numpy as jnp
from jax import lax
from jax.experimental import pallas as pl
from jax.experimental.pallas import tpu as pltpu
from jax.sharding import Mesh
from jax.sharding import PartitionSpec as P

SIZES = (8, 2, 2, 2, 4, 2)
NAMES = ("z", "xh", "core", "xl", "yh", "yl")
DP = ("z", "xh", "core")
SUB = ("xl", "yh", "yl")
PLACES = (((0, 5), (1, 4)), ((6, 7), (3, 2)))
FAR = ("z", "xh")
NEAR = ("core", "xl", "yh", "yl")
BF = jnp.bfloat16
F32 = jnp.float32
NT = (((1,), (1,)), ((), ()))
VMEM = pl.BlockSpec(memory_space=pltpu.VMEM)


def half_mask(shape):
    return lax.broadcasted_iota(jnp.int32, shape, len(shape) - 1) < 64


def swap_halves(x):
    return pltpu.roll(x, 64, 1)


def split(x):
    high = x.astype(BF).astype(F32)
    return high, x - high


def open_kernel(samples, turn_t, codes_t, pack, copies):
    for n in range(4):
        copies[n] = samples[...]
    codes = codes_t[...]
    square = jnp.sum(codes * codes, axis=0, keepdims=True)
    high = square.astype(BF).astype(F32)
    mid = (square - high).astype(BF).astype(F32)
    low = square - high - mid
    squares = jnp.concatenate([high, mid, low, jnp.zeros((13, 256), F32)], axis=0).astype(BF)
    pack[:, 0:1024] = turn_t[...]
    pack[:, 1024:1280] = codes.astype(BF)
    pack[0:16, 1280:] = squares[:, :128]
    pack[16:32, 1280:] = squares[:, 128:]
    pack[32:64, 1280:] = jnp.zeros((32, 128), BF)


def prepare_kernel(pack, first, second, turn, codes_t, left):
    core = lax.axis_index("core")
    w0, w1, w2 = pack[...], first[...], second[...]
    wa = jnp.where(core == 0, w0, w1)
    wb = jnp.where(core == 0, w1, w2)
    turn[0:64, :] = wa[:, :1024]
    turn[64:128, :] = wb[:, :1024]
    zero = jnp.zeros((64, 256), BF)
    both = jnp.concatenate(
        [
            jnp.concatenate([wa[:, 1024:1280], zero], axis=1),
            jnp.concatenate([zero, wb[:, 1024:1280]], axis=1),
        ],
        axis=0,
    )
    codes_t[...] = both
    squares = jnp.concatenate(
        [wa[0:16, 1280:], wa[16:32, 1280:], wb[0:16, 1280:], wb[16:32, 1280:]], axis=1
    )
    left[...] = jnp.concatenate([both * BF(-2.0), squares, jnp.zeros((112, 512), BF)], axis=0).T


def assign_rows(samples, turn, codes_t, left, sums, cross, put):
    rows, chunk = 512, 256
    lane = lax.broadcasted_iota(jnp.int32, (chunk, 128), 1)
    three = jnp.where(lane < 3, 1.0, 0.0).astype(BF)
    ones = jnp.ones((chunk, 128), BF)
    row16 = lax.broadcasted_iota(jnp.int32, (16, 256), 0)
    pick = (lax.broadcasted_iota(jnp.int32, (16, 256), 1) & 64) == 0
    pick = jnp.where(pick == (row16 == 0), 1.0, 0.0).astype(BF)
    for c in range(rows // chunk):
        x = samples[c * chunk : (c + 1) * chunk, :]
        rot = lax.dot_general(x, turn[...], NT, preferred_element_type=F32).astype(BF)
        square_high, square_low = split(jnp.square(rot.astype(F32)))
        square = jnp.concatenate([square_high, square_low], axis=1).astype(BF)
        row_square = lax.dot_general(pick, square, NT, preferred_element_type=F32)
        near = lax.dot_general(
            left[...], jnp.concatenate([rot, three], axis=1), NT, preferred_element_type=F32
        )
        parts = []
        for i in range(2):
            logits = -0.125 * (row_square[i : i + 1] + near[i * 256 : (i + 1) * 256])
            e = jnp.exp(logits - jnp.max(logits, axis=0, keepdims=True))
            parts.append((e * (1.0 / jnp.sum(e, axis=0, keepdims=True))).astype(BF))
        weights = jnp.concatenate(parts, axis=0)
        rebuilt = jnp.dot(codes_t[...], weights, preferred_element_type=F32).astype(BF)
        s = jnp.dot(weights, jnp.concatenate([rot, ones], axis=1), preferred_element_type=F32)
        k = jnp.dot(rebuilt, x, preferred_element_type=F32)
        sums = s if sums is None else sums + s
        cross = k if cross is None else cross + k
        back = rebuilt.T
        put(2 * c, back[:128])
        put(2 * c + 1, back[128:])
    return sums, cross


def early_kernel(samples, turn, codes_t, left, sums, cross, recon):
    def put(block, tile):
        recon[block] = tile

    sums[...], cross[...] = assign_rows(samples, turn, codes_t, left, None, None, put)


def late_kernel(samples, turn, codes_t, left, sums, cross, send, recon, sums_a, sums_b):
    def put(block, tile):
        recon[block] = tile

    sums, cross = assign_rows(samples, turn, codes_t, left, sums[...], cross[...], put)
    cross = cross.astype(BF)
    r = lax.broadcasted_iota(jnp.int32, (256, 256), 0)
    wanted = ((r & 4) << 5) | ((r & 2) << 5) | ((r >> 3) << 1) | (r & 1)
    order = jnp.where(lax.broadcasted_iota(jnp.int32, (256, 256), 1) == wanted, 1.0, 0.0).astype(BF)
    pieces = [
        lax.dot_general(order, cross[:, n * 256 : (n + 1) * 256], NT, preferred_element_type=F32)
        for n in range(4)
    ]
    for d in range(32):
        tiles = [piece[8 * d : 8 * d + 8] for piece in pieces]
        send[d] = jnp.concatenate(tiles, axis=0).astype(BF)
    low = half_mask((64, 128))
    diagonal = (
        lax.broadcasted_iota(jnp.int32, (128, 128), 0)
        == lax.broadcasted_iota(jnp.int32, (128, 128), 1)
    )
    for i, out in enumerate((sums_a, sums_b)):
        lines = []
        for h in range(2):
            at = i * 256 + h * 128
            a, b = sums[at : at + 64, :128], sums[at + 64 : at + 128, :128]
            if i == 0:
                tile = jnp.where(low, a, swap_halves(b))
            else:
                tile = jnp.where(low, swap_halves(a), b)
            out[h * 64 : h * 64 + 64, :] = tile.astype(BF)
            count = jnp.where(diagonal, sums[at : at + 128, 128:], 0.0)
            lines += split(jnp.sum(count, axis=0, keepdims=True))
        out[128:144, :] = jnp.concatenate(lines + [jnp.zeros((12, 128), F32)], axis=0).astype(BF)


def half_kernel(first, second, keep, give):
    core = lax.axis_index("core")
    both = first[...].astype(F32) + second[...].astype(F32)
    empty = jnp.zeros((14, 128), F32)
    halves = []
    for h in range(2):
        line = both[128 + 2 * h : 129 + 2 * h] + both[129 + 2 * h : 130 + 2 * h]
        halves.append(jnp.concatenate([both[h * 64 : h * 64 + 64], *split(line), empty], axis=0))
    keep[...] = jnp.where(core == 0, halves[0], halves[1])
    give[...] = jnp.where(core == 0, halves[1], halves[0]).astype(BF)


def arrange(low, a, b, c, d):
    turned = swap_halves(b)
    return [jnp.where(low, a, turned), swap_halves(d), jnp.where(low, turned, a), c]


def middle_kernel(got, keep, half, send):
    low = half_mask((32, 128))
    columns = []
    for xl in range(2):
        total = [jnp.zeros((32, 128), F32)] * 4
        for yh in range(4):
            blocks = [got[core * 16 + xl * 8 + yh * 2 + yl].astype(F32) for core in range(2) for yl in range(2)]
            for p, tile in enumerate(arrange(low, *blocks)):
                total[(yh + p) & 3] += tile
        columns += total
    r = lax.broadcasted_iota(jnp.int32, (256, 256), 0)
    wanted = (((r >> 1) & 7) << 5) | ((r >> 4) << 1) | (r & 1)
    order = jnp.where(lax.broadcasted_iota(jnp.int32, (256, 256), 1) == wanted, 1.0, 0.0).astype(BF)
    cross = jnp.dot(
        order, jnp.concatenate(columns, axis=0).astype(BF), preferred_element_type=F32
    ).astype(BF)
    both = keep[...] + half[...].astype(F32)
    line = both[64:65] + both[65:66]
    both = jnp.concatenate([both[:64], *split(line), jnp.zeros((6, 128), F32)], axis=0).astype(BF)
    for q in range(16):
        send[q, 0:16, :] = cross[q * 16 : q * 16 + 16]
        send[q, 16:88, :] = both


def finish_kernel(got, codes_t, cross, fresh):
    total = jnp.sum(got[...].astype(F32), axis=0)
    for n in range(8):
        cross[:, n * 128 : (n + 1) * 128] = total[2 * n : 2 * n + 2]
    sums, count = total[16:80], total[80:81] + total[81:82]
    sums = jnp.concatenate([sums, swap_halves(sums)], axis=0).T[:64]
    own = jnp.where(lax.axis_index("core") == 0, codes_t[:, :128], codes_t[:, 128:])
    fresh[...] = (sums + own) / (count + 1.0)


def codes_kernel(mine, other, codes_t):
    a, b = mine[...], other[...]
    codes_t[:, :128] = jnp.where(lax.axis_index("core") == 0, a, b)
    codes_t[:, 128:] = jnp.where(lax.axis_index("core") == 0, b, a)


def second_kernel(early, got_core, give_x, give_y, give_xy):
    xl, yl = lax.axis_index("xl"), lax.axis_index("yl")
    for n, block in enumerate((early, got_core)):
        give_x[n] = block[(1 - xl) * 2 + yl]
        give_y[n] = block[xl * 2 + 1 - yl]
        give_xy[n] = block[(1 - xl) * 2 + 1 - yl]


def home_kernel(early, got_core, got_x, got_y, got_xy, recon):
    core, xl = lax.axis_index("core"), lax.axis_index("xl")
    yh, yl = lax.axis_index("yh"), lax.axis_index("yl")
    low = half_mask((128, 128))
    own = [early[xl * 2 + yl], got_core[xl * 2 + yl]]
    for across, (same, far) in enumerate(((own, got_y), (got_x, got_xy))):
        blocks = []
        for c in range(2):
            near_c = jnp.where(core == c, same[0], same[1])
            far_c = jnp.where(core == c, far[0], far[1])
            for y in range(2):
                blocks.append(jnp.where(yl == y, near_c, far_c).astype(F32))
        side = (1 - xl) if across else xl
        for p, tile in enumerate(arrange(low, *blocks)):
            at = pl.multiple_of((side * 4 + ((yh + p) & 3)) * 128, 128)
            recon[:, pl.ds(at, 128)] = tile.astype(BF)


def call(kernel, name, outs, args, flops=0, moved=0):
    return pl.pallas_call(
        kernel,
        out_shape=tuple(jax.ShapeDtypeStruct(*o) for o in outs),
        in_specs=[VMEM] * len(args),
        out_specs=(VMEM,) * len(outs),
        compiler_params=pltpu.CompilerParams(vmem_limit_bytes=40 * 1024 * 1024),
        cost_estimate=pl.CostEstimate(flops=flops, bytes_accessed=moved, transcendentals=0),
        name=name,
    )(*args)


def per_device(samples, rotation, codebook):
    pack, copies = pl.pallas_call(
        open_kernel,
        out_shape=(
            jax.ShapeDtypeStruct((64, 1408), BF),
            jax.ShapeDtypeStruct((4, 128, 1024), BF),
        ),
        in_specs=[VMEM, VMEM, VMEM],
        out_specs=(VMEM, VMEM),
        compiler_params=pltpu.CompilerParams(vmem_limit_bytes=60 * 1024 * 1024),
        name="open",
    )(samples, rotation.T, codebook[0].T)
    packs = []
    for steps in ((3, 2), (None, 1)):
        pairs = [
            (c * 8 + ((y + step if y & 1 else y - step) & 7), c * 8 + y)
            for c, step in enumerate(steps)
            for y in range(8)
            if step is not None
        ]
        packs.append(lax.ppermute(pack, ("core", "yh", "yl"), pairs))
    mine = lax.all_to_all(copies, ("xl", "yl"), 0, 0, tiled=True).reshape(512, 1024)
    tools = call(
        prepare_kernel,
        "prepare",
        [((128, 1024), BF), ((128, 512), BF), ((512, 256), BF)],
        (pack, *packs),
        flops=16 * 10**9,
    )
    swap = [(0, 1), (1, 0)]
    other = lax.ppermute(mine, "core", swap)
    block, pair = ((4, 128, 128), BF), ((2, 128, 128), BF)
    sums, cross, early = call(
        early_kernel,
        "early",
        [((512, 256), F32), ((128, 1024), F32), block],
        (mine, *tools),
        moved=8_000_000,
    )
    send, late, *totals = call(
        late_kernel,
        "late",
        [((32, 32, 128), BF), block, ((144, 128), BF), ((144, 128), BF)],
        (other, *tools, sums, cross),
        moved=8_000_000,
    )
    moved = []
    for i in range(2):
        pairs = [
            (c * 8 + y, c * 8 + (((y & 6) + PLACES[c][y & 1][i]) & 7)) for c in range(2) for y in range(8)
        ]
        moved.append(lax.ppermute(totals[i], ("core", "yh", "yl"), pairs))
    got_core = lax.ppermute(late, "core", swap)
    keep, give = call(
        half_kernel, "half", [((80, 128), F32), ((80, 128), BF)], tuple(moved), flops=2 * 10**9
    )
    half = lax.ppermute(give, "core", swap)
    got = lax.all_to_all(send, NEAR, 0, 0, tiled=True)
    got, half, got_core = lax.optimization_barrier((got, half, got_core))
    (send,) = call(middle_kernel, "middle", [((16, 88, 128), BF)], (got, keep, half))
    gives = call(second_kernel, "second", [pair, pair, pair], (early, got_core))
    got_x = lax.ppermute(gives[0], "xl", swap)
    got_y = lax.ppermute(gives[1], "yl", swap)
    got_xy = lax.ppermute(gives[2], ("xl", "yl"), [(0, 3), (1, 2), (2, 1), (3, 0)])
    got = lax.all_to_all(send, FAR, 0, 0, tiled=True)
    got, got_x, got_y, got_xy = lax.optimization_barrier((got, got_x, got_y, got_xy))
    cross, fresh = call(
        finish_kernel,
        "finish",
        [((2, 1024), F32), ((64, 128), F32)],
        (got, codebook[0].T),
    )
    fresh_other = lax.ppermute(fresh, "core", swap)
    (recon,) = call(
        home_kernel, "home", [((128, 1024), BF)], (early, got_core, got_x, got_y, got_xy)
    )
    fresh_other, recon = lax.optimization_barrier((fresh_other, recon))
    (new_codes,) = call(codes_kernel, "codes", [((64, 256), F32)], (fresh, fresh_other))
    return recon, new_codes.T[None], cross


def solution(mesh):
    fine = Mesh(mesh.devices.reshape(SIZES), NAMES)
    rows = P(DP + SUB, None)
    return jax.shard_map(
        per_device,
        mesh=fine,
        in_specs=(rows, P(None, SUB), P(SUB, None, None)),
        out_specs=(rows, P(SUB, None, None), rows),
        check_vma=False,
    )
```

```python
import functools

import jax
import jax.numpy as jnp
from jax import lax
from jax.experimental import pallas as pl
from jax.experimental.pallas import tpu as pltpu
from jax.sharding import Mesh
from jax.sharding import PartitionSpec as P

SIZES = (8, 2, 2, 2, 4, 2)
NAMES = ("z", "xh", "core", "xl", "yh", "yl")
DP = ("z", "xh", "core")
SUB = ("xl", "yh", "yl")
PLACES = (((0, 5), (1, 4)), ((6, 7), (3, 2)))
FAR = ("z", "xh")
NEAR = ("core", "xl", "yh", "yl")
BF = jnp.bfloat16
F32 = jnp.float32
NT = (((1,), (1,)), ((), ()))
VMEM = pl.BlockSpec(memory_space=pltpu.VMEM)


def half_mask(shape):
    return lax.broadcasted_iota(jnp.int32, shape, len(shape) - 1) < 64


def swap_halves(x):
    return pltpu.roll(x, 64, 1)


def split(x):
    high = x.astype(BF).astype(F32)
    return high, x - high


def open_kernel(samples, turn_t, codes_t, pack, copies):
    for n in range(4):
        copies[n] = samples[...]
    codes = codes_t[...]
    square = jnp.sum(codes * codes, axis=0, keepdims=True)
    high = square.astype(BF).astype(F32)
    mid = (square - high).astype(BF).astype(F32)
    low = square - high - mid
    squares = jnp.concatenate([high, mid, low, jnp.zeros((13, 256), F32)], axis=0).astype(BF)
    pack[:, 0:1024] = turn_t[...]
    pack[:, 1024:1280] = codes.astype(BF)
    pack[0:16, 1280:] = squares[:, :128]
    pack[16:32, 1280:] = squares[:, 128:]
    pack[32:64, 1280:] = jnp.zeros((32, 128), BF)


def prepare_kernel(pack, first, second, turn, codes_t, left):
    core = lax.axis_index("core")
    w0, w1, w2 = pack[...], first[...], second[...]
    wa = jnp.where(core == 0, w0, w1)
    wb = jnp.where(core == 0, w1, w2)
    turn[0:64, :] = wa[:, :1024]
    turn[64:128, :] = wb[:, :1024]
    zero = jnp.zeros((64, 256), BF)
    both = jnp.concatenate(
        [
            jnp.concatenate([wa[:, 1024:1280], zero], axis=1),
            jnp.concatenate([zero, wb[:, 1024:1280]], axis=1),
        ],
        axis=0,
    )
    codes_t[...] = both
    squares = jnp.concatenate(
        [wa[0:16, 1280:], wa[16:32, 1280:], wb[0:16, 1280:], wb[16:32, 1280:]], axis=1
    )
    left[...] = jnp.concatenate([both * BF(-2.0), squares, jnp.zeros((112, 512), BF)], axis=0).T


def assign_rows(samples, turn, codes_t, left, sums, cross, put):
    rows, chunk = 512, 512
    lane = lax.broadcasted_iota(jnp.int32, (chunk, 128), 1)
    three = jnp.where(lane < 3, 1.0, 0.0).astype(BF)
    ones = jnp.ones((chunk, 128), BF)
    row16 = lax.broadcasted_iota(jnp.int32, (16, 256), 0)
    pick = (lax.broadcasted_iota(jnp.int32, (16, 256), 1) & 64) == 0
    pick = jnp.where(pick == (row16 == 0), 1.0, 0.0).astype(BF)
    for c in range(rows // chunk):
        x = samples[c * chunk : (c + 1) * chunk, :]
        rot = lax.dot_general(x, turn[...], NT, preferred_element_type=F32).astype(BF)
        square_high, square_low = split(jnp.square(rot.astype(F32)))
        square = jnp.concatenate([square_high, square_low], axis=1).astype(BF)
        row_square = lax.dot_general(pick, square, NT, preferred_element_type=F32)
        near = lax.dot_general(
            left[...], jnp.concatenate([rot, three], axis=1), NT, preferred_element_type=F32
        )
        parts = []
        for i in range(2):
            logits = -0.125 * (row_square[i : i + 1] + near[i * 256 : (i + 1) * 256])
            e = jnp.exp(logits - jnp.max(logits, axis=0, keepdims=True))
            parts.append((e * (1.0 / jnp.sum(e, axis=0, keepdims=True))).astype(BF))
        weights = jnp.concatenate(parts, axis=0)
        rebuilt = jnp.dot(codes_t[...], weights, preferred_element_type=F32).astype(BF)
        s = jnp.dot(weights, jnp.concatenate([rot, ones], axis=1), preferred_element_type=F32)
        k = jnp.dot(rebuilt, x, preferred_element_type=F32)
        sums = s if sums is None else sums + s
        cross = k if cross is None else cross + k
        back = rebuilt.T
        for n in range(chunk // 128):
            put(chunk // 128 * c + n, back[n * 128 : (n + 1) * 128])
    return sums, cross


def early_kernel(samples, turn, codes_t, left, sums, cross, recon):
    def put(block, tile):
        recon[block] = tile

    sums[...], cross[...] = assign_rows(samples, turn, codes_t, left, None, None, put)


def late_kernel(samples, turn, codes_t, left, sums, cross, send, recon, sums_a, sums_b):
    def put(block, tile):
        recon[block] = tile

    sums, cross = assign_rows(samples, turn, codes_t, left, sums[...], cross[...], put)
    cross = cross.astype(BF)
    r = lax.broadcasted_iota(jnp.int32, (256, 256), 0)
    wanted = ((r & 4) << 5) | ((r & 2) << 5) | ((r >> 3) << 1) | (r & 1)
    order = jnp.where(lax.broadcasted_iota(jnp.int32, (256, 256), 1) == wanted, 1.0, 0.0).astype(BF)
    pieces = [
        lax.dot_general(order, cross[:, n * 256 : (n + 1) * 256], NT, preferred_element_type=F32)
        for n in range(4)
    ]
    for d in range(32):
        tiles = [piece[8 * d : 8 * d + 8] for piece in pieces]
        send[d] = jnp.concatenate(tiles, axis=0).astype(BF)
    low = half_mask((64, 128))
    diagonal = (
        lax.broadcasted_iota(jnp.int32, (128, 128), 0)
        == lax.broadcasted_iota(jnp.int32, (128, 128), 1)
    )
    for i, out in enumerate((sums_a, sums_b)):
        lines = []
        for h in range(2):
            at = i * 256 + h * 128
            a, b = sums[at : at + 64, :128], sums[at + 64 : at + 128, :128]
            if i == 0:
                tile = jnp.where(low, a, swap_halves(b))
            else:
                tile = jnp.where(low, swap_halves(a), b)
            out[h * 64 : h * 64 + 64, :] = tile.astype(BF)
            count = jnp.where(diagonal, sums[at : at + 128, 128:], 0.0)
            lines += split(jnp.sum(count, axis=0, keepdims=True))
        out[128:144, :] = jnp.concatenate(lines + [jnp.zeros((12, 128), F32)], axis=0).astype(BF)


def half_kernel(first, second, keep, give):
    core = lax.axis_index("core")
    both = first[...].astype(F32) + second[...].astype(F32)
    empty = jnp.zeros((14, 128), F32)
    halves = []
    for h in range(2):
        line = both[128 + 2 * h : 129 + 2 * h] + both[129 + 2 * h : 130 + 2 * h]
        halves.append(jnp.concatenate([both[h * 64 : h * 64 + 64], *split(line), empty], axis=0))
    keep[...] = jnp.where(core == 0, halves[0], halves[1])
    give[...] = jnp.where(core == 0, halves[1], halves[0]).astype(BF)


def arrange(low, a, b, c, d):
    turned = swap_halves(b)
    return [jnp.where(low, a, turned), swap_halves(d), jnp.where(low, turned, a), c]


def middle_kernel(got, keep, half, send):
    low = half_mask((32, 128))
    columns = []
    for xl in range(2):
        total = [jnp.zeros((32, 128), F32)] * 4
        for yh in range(4):
            blocks = [got[core * 16 + xl * 8 + yh * 2 + yl].astype(F32) for core in range(2) for yl in range(2)]
            for p, tile in enumerate(arrange(low, *blocks)):
                total[(yh + p) & 3] += tile
        columns += total
    r = lax.broadcasted_iota(jnp.int32, (256, 256), 0)
    wanted = (((r >> 1) & 7) << 5) | ((r >> 4) << 1) | (r & 1)
    order = jnp.where(lax.broadcasted_iota(jnp.int32, (256, 256), 1) == wanted, 1.0, 0.0).astype(BF)
    cross = jnp.dot(
        order, jnp.concatenate(columns, axis=0).astype(BF), preferred_element_type=F32
    ).astype(BF)
    both = keep[...] + half[...].astype(F32)
    line = both[64:65] + both[65:66]
    both = jnp.concatenate([both[:64], *split(line), jnp.zeros((6, 128), F32)], axis=0).astype(BF)
    for q in range(16):
        send[q, 0:16, :] = cross[q * 16 : q * 16 + 16]
        send[q, 16:88, :] = both


def finish_kernel(got, codes_t, cross, fresh):
    total = jnp.sum(got[...].astype(F32), axis=0)
    for n in range(8):
        cross[:, n * 128 : (n + 1) * 128] = total[2 * n : 2 * n + 2]
    sums, count = total[16:80], total[80:81] + total[81:82]
    sums = jnp.concatenate([sums, swap_halves(sums)], axis=0).T[:64]
    own = jnp.where(lax.axis_index("core") == 0, codes_t[:, :128], codes_t[:, 128:])
    fresh[...] = (sums + own) / (count + 1.0)


def codes_kernel(mine, other, codes_t):
    a, b = mine[...], other[...]
    codes_t[:, :128] = jnp.where(lax.axis_index("core") == 0, a, b)
    codes_t[:, 128:] = jnp.where(lax.axis_index("core") == 0, b, a)


def second_kernel(early, got_core, give_x, give_y, give_xy):
    xl, yl = lax.axis_index("xl"), lax.axis_index("yl")
    for n, block in enumerate((early, got_core)):
        give_x[n] = block[(1 - xl) * 2 + yl]
        give_y[n] = block[xl * 2 + 1 - yl]
        give_xy[n] = block[(1 - xl) * 2 + 1 - yl]


def home_kernel(early, got_core, got_x, got_y, got_xy, recon):
    core, xl = lax.axis_index("core"), lax.axis_index("xl")
    yh, yl = lax.axis_index("yh"), lax.axis_index("yl")
    low = half_mask((128, 128))
    own = [early[xl * 2 + yl], got_core[xl * 2 + yl]]
    for across, (same, far) in enumerate(((own, got_y), (got_x, got_xy))):
        blocks = []
        for c in range(2):
            near_c = jnp.where(core == c, same[0], same[1])
            far_c = jnp.where(core == c, far[0], far[1])
            for y in range(2):
                blocks.append(jnp.where(yl == y, near_c, far_c).astype(F32))
        side = (1 - xl) if across else xl
        for p, tile in enumerate(arrange(low, *blocks)):
            at = pl.multiple_of((side * 4 + ((yh + p) & 3)) * 128, 128)
            recon[:, pl.ds(at, 128)] = tile.astype(BF)


def call(kernel, name, outs, args, flops=0, moved=0):
    return pl.pallas_call(
        kernel,
        out_shape=tuple(jax.ShapeDtypeStruct(*o) for o in outs),
        in_specs=[VMEM] * len(args),
        out_specs=(VMEM,) * len(outs),
        compiler_params=pltpu.CompilerParams(vmem_limit_bytes=40 * 1024 * 1024),
        cost_estimate=pl.CostEstimate(flops=flops, bytes_accessed=moved, transcendentals=0),
        name=name,
    )(*args)


def per_device(samples, rotation, codebook):
    pack, copies = pl.pallas_call(
        open_kernel,
        out_shape=(
            jax.ShapeDtypeStruct((64, 1408), BF),
            jax.ShapeDtypeStruct((4, 128, 1024), BF),
        ),
        in_specs=[VMEM, VMEM, VMEM],
        out_specs=(VMEM, VMEM),
        compiler_params=pltpu.CompilerParams(vmem_limit_bytes=60 * 1024 * 1024),
        name="open",
    )(samples, rotation.T, codebook[0].T)
    packs = []
    for steps in ((3, 2), (None, 1)):
        pairs = [
            (c * 8 + ((y + step if y & 1 else y - step) & 7), c * 8 + y)
            for c, step in enumerate(steps)
            for y in range(8)
            if step is not None
        ]
        packs.append(lax.ppermute(pack, ("core", "yh", "yl"), pairs))
    mine = lax.all_to_all(copies, ("xl", "yl"), 0, 0, tiled=True).reshape(512, 1024)
    tools = call(
        prepare_kernel,
        "prepare",
        [((128, 1024), BF), ((128, 512), BF), ((512, 256), BF)],
        (pack, *packs),
        flops=16 * 10**9,
    )
    swap = [(0, 1), (1, 0)]
    other = lax.ppermute(mine, "core", swap)
    block, pair = ((4, 128, 128), BF), ((2, 128, 128), BF)
    sums, cross, early = call(
        early_kernel,
        "early",
        [((512, 256), F32), ((128, 1024), F32), block],
        (mine, *tools),
        moved=8_000_000,
    )
    send, late, *totals = call(
        late_kernel,
        "late",
        [((32, 32, 128), BF), block, ((144, 128), BF), ((144, 128), BF)],
        (other, *tools, sums, cross),
        moved=8_000_000,
    )
    moved = []
    for i in range(2):
        pairs = [
            (c * 8 + y, c * 8 + (((y & 6) + PLACES[c][y & 1][i]) & 7)) for c in range(2) for y in range(8)
        ]
        moved.append(lax.ppermute(totals[i], ("core", "yh", "yl"), pairs))
    got_core = lax.ppermute(late, "core", swap)
    keep, give = call(
        half_kernel, "half", [((80, 128), F32), ((80, 128), BF)], tuple(moved), flops=2 * 10**9
    )
    half = lax.ppermute(give, "core", swap)
    got = lax.all_to_all(send, NEAR, 0, 0, tiled=True)
    got, half, got_core = lax.optimization_barrier((got, half, got_core))
    (send,) = call(middle_kernel, "middle", [((16, 88, 128), BF)], (got, keep, half))
    gives = call(second_kernel, "second", [pair, pair, pair], (early, got_core))
    got_x = lax.ppermute(gives[0], "xl", swap)
    got_y = lax.ppermute(gives[1], "yl", swap)
    got_xy = lax.ppermute(gives[2], ("xl", "yl"), [(0, 3), (1, 2), (2, 1), (3, 0)])
    got = lax.all_to_all(send, FAR, 0, 0, tiled=True)
    got, got_x, got_y, got_xy = lax.optimization_barrier((got, got_x, got_y, got_xy))
    cross, fresh = call(
        finish_kernel,
        "finish",
        [((2, 1024), F32), ((64, 128), F32)],
        (got, codebook[0].T),
    )
    fresh_other = lax.ppermute(fresh, "core", swap)
    (recon,) = call(
        home_kernel, "home", [((128, 1024), BF)], (early, got_core, got_x, got_y, got_xy)
    )
    fresh_other, recon = lax.optimization_barrier((fresh_other, recon))
    (new_codes,) = call(codes_kernel, "codes", [((64, 256), F32)], (fresh, fresh_other))
    return recon, new_codes.T[None], cross


def solution(mesh):
    fine = Mesh(mesh.devices.reshape(SIZES), NAMES)
    rows = P(DP + SUB, None)
    return jax.shard_map(
        per_device,
        mesh=fine,
        in_specs=(rows, P(None, SUB), P(SUB, None, None)),
        out_specs=(rows, P(SUB, None, None), rows),
        check_vma=False,
    )
```

```python
import functools

import jax
import jax.numpy as jnp
from jax import lax
from jax.experimental import pallas as pl
from jax.experimental.pallas import tpu as pltpu
from jax.sharding import Mesh
from jax.sharding import PartitionSpec as P

SIZES = (8, 2, 2, 2, 4, 2)
NAMES = ("z", "xh", "core", "xl", "yh", "yl")
DP = ("z", "xh", "core")
SUB = ("xl", "yh", "yl")
PLACES = (((0, 5), (1, 4)), ((6, 7), (3, 2)))
FAR = ("z", "xh")
NEAR = ("core", "xl", "yh", "yl")
BF = jnp.bfloat16
F32 = jnp.float32
NT = (((1,), (1,)), ((), ()))
VMEM = pl.BlockSpec(memory_space=pltpu.VMEM)


def half_mask(shape):
    return lax.broadcasted_iota(jnp.int32, shape, len(shape) - 1) < 64


def swap_halves(x):
    return pltpu.roll(x, 64, 1)


def split(x):
    high = x.astype(BF).astype(F32)
    return high, x - high


def open_kernel(samples, turn_t, codes_t, pack, copies):
    for n in range(4):
        copies[n] = samples[...]
    codes = codes_t[...]
    square = jnp.sum(codes * codes, axis=0, keepdims=True)
    high = square.astype(BF).astype(F32)
    mid = (square - high).astype(BF).astype(F32)
    low = square - high - mid
    squares = jnp.concatenate([high, mid, low, jnp.zeros((13, 256), F32)], axis=0).astype(BF)
    pack[:, 0:1024] = turn_t[...]
    pack[:, 1024:1280] = codes.astype(BF)
    pack[0:16, 1280:] = squares[:, :128]
    pack[16:32, 1280:] = squares[:, 128:]
    pack[32:64, 1280:] = jnp.zeros((32, 128), BF)


def prepare_kernel(pack, first, second, turn, codes_t, left):
    core = lax.axis_index("core")
    w0, w1, w2 = pack[...], first[...], second[...]
    wa = jnp.where(core == 0, w0, w1)
    wb = jnp.where(core == 0, w1, w2)
    turn[0:64, :] = wa[:, :1024]
    turn[64:128, :] = wb[:, :1024]
    zero = jnp.zeros((64, 256), BF)
    both = jnp.concatenate(
        [
            jnp.concatenate([wa[:, 1024:1280], zero], axis=1),
            jnp.concatenate([zero, wb[:, 1024:1280]], axis=1),
        ],
        axis=0,
    )
    codes_t[...] = both
    squares = jnp.concatenate(
        [wa[0:16, 1280:], wa[16:32, 1280:], wb[0:16, 1280:], wb[16:32, 1280:]], axis=1
    )
    left[...] = jnp.concatenate([both * BF(-2.0), squares, jnp.zeros((112, 512), BF)], axis=0).T


def assign_rows(samples, turn, codes_t, left, sums, cross, put):
    rows, chunk = 512, 512
    lane = lax.broadcasted_iota(jnp.int32, (chunk, 128), 1)
    three = jnp.where(lane < 3, 1.0, 0.0).astype(BF)
    ones = jnp.ones((chunk, 128), BF)
    row16 = lax.broadcasted_iota(jnp.int32, (16, 256), 0)
    pick = (lax.broadcasted_iota(jnp.int32, (16, 256), 1) & 64) == 0
    pick = jnp.where(pick == (row16 == 0), 1.0, 0.0).astype(BF)
    for c in range(rows // chunk):
        x = samples[c * chunk : (c + 1) * chunk, :]
        rot = lax.dot_general(x, turn[...], NT, preferred_element_type=F32).astype(BF)
        square_high, square_low = split(jnp.square(rot.astype(F32)))
        square = jnp.concatenate([square_high, square_low], axis=1).astype(BF)
        row_square = lax.dot_general(pick, square, NT, preferred_element_type=F32)
        near = lax.dot_general(
            left[...], jnp.concatenate([rot, three], axis=1), NT, preferred_element_type=F32
        )
        parts = []
        for i in range(2):
            logits = -0.125 * (row_square[i : i + 1] + near[i * 256 : (i + 1) * 256])
            e = jnp.exp(logits - jnp.max(logits, axis=0, keepdims=True))
            parts.append((e * (1.0 / jnp.sum(e, axis=0, keepdims=True))).astype(BF))
        weights = jnp.concatenate(parts, axis=0)
        rebuilt = jnp.dot(codes_t[...], weights, preferred_element_type=F32).astype(BF)
        s = jnp.dot(weights, jnp.concatenate([rot, ones], axis=1), preferred_element_type=F32)
        k = jnp.dot(rebuilt, x, preferred_element_type=F32)
        sums = s if sums is None else sums + s
        cross = k if cross is None else cross + k
        back = rebuilt.T
        for n in range(chunk // 128):
            put(chunk // 128 * c + n, back[n * 128 : (n + 1) * 128])
    return sums, cross


def early_kernel(samples, turn, codes_t, left, sums, cross, recon):
    def put(block, tile):
        recon[block] = tile

    sums[...], cross[...] = assign_rows(samples, turn, codes_t, left, None, None, put)


def late_kernel(samples, turn, codes_t, left, sums, cross, send, recon, sums_a, sums_b):
    def put(block, tile):
        recon[block] = tile

    sums, cross = assign_rows(samples, turn, codes_t, left, sums[...], cross[...], put)
    cross = cross.astype(BF)
    r = lax.broadcasted_iota(jnp.int32, (256, 256), 0)
    wanted = ((r & 4) << 5) | ((r & 2) << 5) | ((r >> 3) << 1) | (r & 1)
    order = jnp.where(lax.broadcasted_iota(jnp.int32, (256, 256), 1) == wanted, 1.0, 0.0).astype(BF)
    pieces = [
        lax.dot_general(order, cross[:, n * 256 : (n + 1) * 256], NT, preferred_element_type=F32)
        for n in range(4)
    ]
    for d in range(32):
        tiles = [piece[8 * d : 8 * d + 8] for piece in pieces]
        send[d] = jnp.concatenate(tiles, axis=0).astype(BF)
    low = half_mask((64, 128))
    diagonal = (
        lax.broadcasted_iota(jnp.int32, (128, 128), 0)
        == lax.broadcasted_iota(jnp.int32, (128, 128), 1)
    )
    for i, out in enumerate((sums_a, sums_b)):
        lines = []
        for h in range(2):
            at = i * 256 + h * 128
            a, b = sums[at : at + 64, :128], sums[at + 64 : at + 128, :128]
            if i == 0:
                tile = jnp.where(low, a, swap_halves(b))
            else:
                tile = jnp.where(low, swap_halves(a), b)
            out[h * 64 : h * 64 + 64, :] = tile.astype(BF)
            count = jnp.where(diagonal, sums[at : at + 128, 128:], 0.0)
            lines += split(jnp.sum(count, axis=0, keepdims=True))
        out[128:144, :] = jnp.concatenate(lines + [jnp.zeros((12, 128), F32)], axis=0).astype(BF)


def half_kernel(first, second, keep, give):
    core = lax.axis_index("core")
    both = first[...].astype(F32) + second[...].astype(F32)
    empty = jnp.zeros((14, 128), F32)
    halves = []
    for h in range(2):
        line = both[128 + 2 * h : 129 + 2 * h] + both[129 + 2 * h : 130 + 2 * h]
        halves.append(jnp.concatenate([both[h * 64 : h * 64 + 64], *split(line), empty], axis=0))
    keep[...] = jnp.where(core == 0, halves[0], halves[1])
    give[...] = jnp.where(core == 0, halves[1], halves[0]).astype(BF)


def arrange(low, a, b, c, d):
    turned = swap_halves(b)
    return [jnp.where(low, a, turned), swap_halves(d), jnp.where(low, turned, a), c]


def middle_kernel(got, keep, half, send):
    low = half_mask((32, 128))
    columns = []
    for xl in range(2):
        total = [jnp.zeros((32, 128), F32)] * 4
        for yh in range(4):
            blocks = [got[core * 16 + xl * 8 + yh * 2 + yl].astype(F32) for core in range(2) for yl in range(2)]
            for p, tile in enumerate(arrange(low, *blocks)):
                total[(yh + p) & 3] += tile
        columns += total
    r = lax.broadcasted_iota(jnp.int32, (256, 256), 0)
    wanted = (((r >> 1) & 7) << 5) | ((r >> 4) << 1) | (r & 1)
    order = jnp.where(lax.broadcasted_iota(jnp.int32, (256, 256), 1) == wanted, 1.0, 0.0).astype(BF)
    cross = jnp.dot(
        order, jnp.concatenate(columns, axis=0).astype(BF), preferred_element_type=F32
    ).astype(BF)
    both = keep[...] + half[...].astype(F32)
    line = both[64:65] + both[65:66]
    both = jnp.concatenate([both[:64], *split(line), jnp.zeros((6, 128), F32)], axis=0).astype(BF)
    for q in range(16):
        send[q, 0:16, :] = cross[q * 16 : q * 16 + 16]
        send[q, 16:88, :] = both


def finish_kernel(got, codes_t, cross, fresh):
    total = jnp.sum(got[...].astype(F32), axis=0)
    for n in range(8):
        cross[:, n * 128 : (n + 1) * 128] = total[2 * n : 2 * n + 2]
    sums, count = total[16:80], total[80:81] + total[81:82]
    sums = jnp.concatenate([sums, swap_halves(sums)], axis=0).T[:64]
    own = jnp.where(lax.axis_index("core") == 0, codes_t[:, :128], codes_t[:, 128:])
    fresh[...] = (sums + own) / (count + 1.0)


def codes_kernel(mine, other, codes_t):
    a, b = mine[...], other[...]
    codes_t[:, :128] = jnp.where(lax.axis_index("core") == 0, a, b)
    codes_t[:, 128:] = jnp.where(lax.axis_index("core") == 0, b, a)


def second_kernel(early, got_core, give_x, give_y, give_xy):
    xl, yl = lax.axis_index("xl"), lax.axis_index("yl")
    for n, block in enumerate((early, got_core)):
        give_x[n] = block[(1 - xl) * 2 + yl]
        give_y[n] = block[xl * 2 + 1 - yl]
        give_xy[n] = block[(1 - xl) * 2 + 1 - yl]


def home_kernel(early, got_core, got_x, got_y, got_xy, recon):
    core, xl = lax.axis_index("core"), lax.axis_index("xl")
    yh, yl = lax.axis_index("yh"), lax.axis_index("yl")
    low = half_mask((128, 128))
    own = [early[xl * 2 + yl], got_core[xl * 2 + yl]]
    for across, (same, far) in enumerate(((own, got_y), (got_x, got_xy))):
        blocks = []
        for c in range(2):
            near_c = jnp.where(core == c, same[0], same[1])
            far_c = jnp.where(core == c, far[0], far[1])
            for y in range(2):
                blocks.append(jnp.where(yl == y, near_c, far_c).astype(F32))
        side = (1 - xl) if across else xl
        for p, tile in enumerate(arrange(low, *blocks)):
            at = pl.multiple_of((side * 4 + ((yh + p) & 3)) * 128, 128)
            recon[:, pl.ds(at, 128)] = tile.astype(BF)


def call(kernel, name, outs, args, flops=0, moved=0):
    return pl.pallas_call(
        kernel,
        out_shape=tuple(jax.ShapeDtypeStruct(*o) for o in outs),
        in_specs=[VMEM] * len(args),
        out_specs=(VMEM,) * len(outs),
        compiler_params=pltpu.CompilerParams(vmem_limit_bytes=40 * 1024 * 1024),
        cost_estimate=pl.CostEstimate(flops=flops, bytes_accessed=moved, transcendentals=0),
        name=name,
    )(*args)


def per_device(samples, rotation, codebook):
    pack, copies = pl.pallas_call(
        open_kernel,
        out_shape=(
            jax.ShapeDtypeStruct((64, 1408), BF),
            jax.ShapeDtypeStruct((4, 128, 1024), BF),
        ),
        in_specs=[VMEM, VMEM, VMEM],
        out_specs=(VMEM, VMEM),
        compiler_params=pltpu.CompilerParams(vmem_limit_bytes=60 * 1024 * 1024),
        name="open",
    )(samples, rotation.T, codebook[0].T)
    packs = []
    for steps in ((3, 2), (None, 1)):
        pairs = [
            (c * 8 + ((y + step if y & 1 else y - step) & 7), c * 8 + y)
            for c, step in enumerate(steps)
            for y in range(8)
            if step is not None
        ]
        packs.append(lax.ppermute(pack, ("core", "yh", "yl"), pairs))
    mine = lax.all_to_all(copies, ("xl", "yl"), 0, 0, tiled=True).reshape(512, 1024)
    tools = call(
        prepare_kernel,
        "prepare",
        [((128, 1024), BF), ((128, 512), BF), ((512, 256), BF)],
        (pack, *packs),
        flops=16 * 10**9,
    )
    swap = [(0, 1), (1, 0)]
    other = lax.ppermute(mine, "core", swap)
    block, pair = ((4, 128, 128), BF), ((2, 128, 128), BF)
    sums, cross, early = call(
        early_kernel,
        "early",
        [((512, 256), F32), ((128, 1024), F32), block],
        (mine, *tools),
        moved=8_000_000,
    )
    send, late, *totals = call(
        late_kernel,
        "late",
        [((32, 32, 128), BF), block, ((144, 128), BF), ((144, 128), BF)],
        (other, *tools, sums, cross),
        moved=8_000_000,
    )
    moved = []
    for i in range(2):
        pairs = [
            (c * 8 + y, c * 8 + (((y & 6) + PLACES[c][y & 1][i]) & 7)) for c in range(2) for y in range(8)
        ]
        moved.append(lax.ppermute(totals[i], ("core", "yh", "yl"), pairs))
    got_core = lax.ppermute(late, "core", swap)
    keep, give = call(
        half_kernel, "half", [((80, 128), F32), ((80, 128), BF)], tuple(moved), flops=2 * 10**9
    )
    half = lax.ppermute(give, "core", swap)
    got = lax.all_to_all(send, NEAR, 0, 0, tiled=True)
    got, half, got_core = lax.optimization_barrier((got, half, got_core))
    (send,) = call(middle_kernel, "middle", [((16, 88, 128), BF)], (got, keep, half))
    gives = call(second_kernel, "second", [pair, pair, pair], (early, got_core))
    got_xy = lax.ppermute(gives[2], ("xl", "yl"), [(0, 3), (1, 2), (2, 1), (3, 0)])
    got_x = lax.ppermute(gives[0], "xl", swap)
    got_y = lax.ppermute(gives[1], "yl", swap)
    got = lax.all_to_all(send, FAR, 0, 0, tiled=True)
    got, got_xy, got_x, got_y = lax.optimization_barrier((got, got_xy, got_x, got_y))
    cross, fresh = call(
        finish_kernel,
        "finish",
        [((2, 1024), F32), ((64, 128), F32)],
        (got, codebook[0].T),
    )
    fresh_other = lax.ppermute(fresh, "core", swap)
    (recon,) = call(
        home_kernel, "home", [((128, 1024), BF)], (early, got_core, got_x, got_y, got_xy)
    )
    fresh_other, recon = lax.optimization_barrier((fresh_other, recon))
    (new_codes,) = call(codes_kernel, "codes", [((64, 256), F32)], (fresh, fresh_other))
    return recon, new_codes.T[None], cross


def solution(mesh):
    fine = Mesh(mesh.devices.reshape(SIZES), NAMES)
    rows = P(DP + SUB, None)
    return jax.shard_map(
        per_device,
        mesh=fine,
        in_specs=(rows, P(None, SUB), P(SUB, None, None)),
        out_specs=(rows, P(SUB, None, None), rows),
        check_vma=False,
    )
```

```python
import functools

import jax
import jax.numpy as jnp
from jax import lax
from jax.experimental import pallas as pl
from jax.experimental.pallas import tpu as pltpu
from jax.sharding import Mesh
from jax.sharding import PartitionSpec as P

SIZES = (8, 2, 2, 2, 4, 2)
NAMES = ("z", "xh", "core", "xl", "yh", "yl")
DP = ("z", "xh", "core")
SUB = ("xl", "yh", "yl")
PLACES = (((0, 5), (1, 4)), ((6, 7), (3, 2)))
FAR = ("z", "xh")
NEAR = ("xl", "yh", "yl")
BF = jnp.bfloat16
F32 = jnp.float32
NT = (((1,), (1,)), ((), ()))
VMEM = pl.BlockSpec(memory_space=pltpu.VMEM)


def half_mask(shape):
    return lax.broadcasted_iota(jnp.int32, shape, len(shape) - 1) < 64


def swap_halves(x):
    return pltpu.roll(x, 64, 1)


def split(x):
    high = x.astype(BF).astype(F32)
    return high, x - high


def open_kernel(samples, turn_t, codes_t, pack, copies):
    for n in range(4):
        copies[n] = samples[...]
    codes = codes_t[...]
    square = jnp.sum(codes * codes, axis=0, keepdims=True)
    high = square.astype(BF).astype(F32)
    mid = (square - high).astype(BF).astype(F32)
    low = square - high - mid
    squares = jnp.concatenate([high, mid, low, jnp.zeros((13, 256), F32)], axis=0).astype(BF)
    pack[:, 0:1024] = turn_t[...]
    pack[:, 1024:1280] = codes.astype(BF)
    pack[0:16, 1280:] = squares[:, :128]
    pack[16:32, 1280:] = squares[:, 128:]
    pack[32:64, 1280:] = jnp.zeros((32, 128), BF)


def prepare_kernel(pack, first, second, turn, codes_t, left):
    core = lax.axis_index("core")
    w0, w1, w2 = pack[...], first[...], second[...]
    wa = jnp.where(core == 0, w0, w1)
    wb = jnp.where(core == 0, w1, w2)
    turn[0:64, :] = wa[:, :1024]
    turn[64:128, :] = wb[:, :1024]
    zero = jnp.zeros((64, 256), BF)
    both = jnp.concatenate(
        [
            jnp.concatenate([wa[:, 1024:1280], zero], axis=1),
            jnp.concatenate([zero, wb[:, 1024:1280]], axis=1),
        ],
        axis=0,
    )
    codes_t[...] = both
    squares = jnp.concatenate(
        [wa[0:16, 1280:], wa[16:32, 1280:], wb[0:16, 1280:], wb[16:32, 1280:]], axis=1
    )
    left[...] = jnp.concatenate([both * BF(-2.0), squares, jnp.zeros((112, 512), BF)], axis=0).T


def assign_rows(samples, turn, codes_t, left, sums, cross, put):
    rows, chunk = 512, 512
    lane = lax.broadcasted_iota(jnp.int32, (chunk, 128), 1)
    three = jnp.where(lane < 3, 1.0, 0.0).astype(BF)
    ones = jnp.ones((chunk, 128), BF)
    row16 = lax.broadcasted_iota(jnp.int32, (16, 256), 0)
    pick = (lax.broadcasted_iota(jnp.int32, (16, 256), 1) & 64) == 0
    pick = jnp.where(pick == (row16 == 0), 1.0, 0.0).astype(BF)
    for c in range(rows // chunk):
        x = samples[c * chunk : (c + 1) * chunk, :]
        rot = lax.dot_general(x, turn[...], NT, preferred_element_type=F32).astype(BF)
        square_high, square_low = split(jnp.square(rot.astype(F32)))
        square = jnp.concatenate([square_high, square_low], axis=1).astype(BF)
        row_square = lax.dot_general(pick, square, NT, preferred_element_type=F32)
        near = lax.dot_general(
            left[...], jnp.concatenate([rot, three], axis=1), NT, preferred_element_type=F32
        )
        parts = []
        for i in range(2):
            logits = -0.125 * (row_square[i : i + 1] + near[i * 256 : (i + 1) * 256])
            e = jnp.exp(logits - jnp.max(logits, axis=0, keepdims=True))
            parts.append((e * (1.0 / jnp.sum(e, axis=0, keepdims=True))).astype(BF))
        weights = jnp.concatenate(parts, axis=0)
        rebuilt = jnp.dot(codes_t[...], weights, preferred_element_type=F32).astype(BF)
        s = jnp.dot(weights, jnp.concatenate([rot, ones], axis=1), preferred_element_type=F32)
        k = jnp.dot(rebuilt, x, preferred_element_type=F32)
        sums = s if sums is None else sums + s
        cross = k if cross is None else cross + k
        back = rebuilt.T
        for n in range(chunk // 128):
            put(chunk // 128 * c + n, back[n * 128 : (n + 1) * 128])
    return sums, cross


def early_kernel(samples, turn, codes_t, left, sums, cross, recon):
    def put(block, tile):
        recon[block] = tile

    sums[...], cross[...] = assign_rows(samples, turn, codes_t, left, None, None, put)


def late_kernel(samples, turn, codes_t, left, sums, cross, send, recon, sums_a, sums_b):
    def put(block, tile):
        recon[block] = tile

    sums, cross = assign_rows(samples, turn, codes_t, left, sums[...], cross[...], put)
    cross = cross.astype(BF)
    r = lax.broadcasted_iota(jnp.int32, (256, 256), 0)
    wanted = ((r & 4) << 5) | ((r & 2) << 5) | ((r >> 3) << 1) | (r & 1)
    order = jnp.where(lax.broadcasted_iota(jnp.int32, (256, 256), 1) == wanted, 1.0, 0.0).astype(BF)
    pieces = [
        lax.dot_general(order, cross[:, n * 256 : (n + 1) * 256], NT, preferred_element_type=F32)
        for n in range(4)
    ]
    for d in range(32):
        tiles = [piece[8 * d : 8 * d + 8] for piece in pieces]
        send[d & 15, (d >> 4) * 32 : (d >> 4) * 32 + 32, :] = jnp.concatenate(tiles, axis=0).astype(BF)
    low = half_mask((64, 128))
    diagonal = (
        lax.broadcasted_iota(jnp.int32, (128, 128), 0)
        == lax.broadcasted_iota(jnp.int32, (128, 128), 1)
    )
    for i, out in enumerate((sums_a, sums_b)):
        lines = []
        for h in range(2):
            at = i * 256 + h * 128
            a, b = sums[at : at + 64, :128], sums[at + 64 : at + 128, :128]
            if i == 0:
                tile = jnp.where(low, a, swap_halves(b))
            else:
                tile = jnp.where(low, swap_halves(a), b)
            out[h * 64 : h * 64 + 64, :] = tile.astype(BF)
            count = jnp.where(diagonal, sums[at : at + 128, 128:], 0.0)
            lines += split(jnp.sum(count, axis=0, keepdims=True))
        out[128:144, :] = jnp.concatenate(lines + [jnp.zeros((12, 128), F32)], axis=0).astype(BF)


def half_kernel(first, second, keep, give):
    core = lax.axis_index("core")
    both = first[...].astype(F32) + second[...].astype(F32)
    empty = jnp.zeros((14, 128), F32)
    halves = []
    for h in range(2):
        line = both[128 + 2 * h : 129 + 2 * h] + both[129 + 2 * h : 130 + 2 * h]
        halves.append(jnp.concatenate([both[h * 64 : h * 64 + 64], *split(line), empty], axis=0))
    keep[...] = jnp.where(core == 0, halves[0], halves[1])
    give[...] = jnp.where(core == 0, halves[1], halves[0]).astype(BF)


def arrange(low, a, b, c, d):
    turned = swap_halves(b)
    return [jnp.where(low, a, turned), swap_halves(d), jnp.where(low, turned, a), c]


def middle_kernel(got, keep, half, send, columns):
    low = half_mask((64, 128))
    for core in range(2):

        @pl.when(lax.axis_index("core") == core)
        def _():
            for xl in range(2):
                total = [None] * 4
                for yh in range(4):
                    a, b = (got[xl * 8 + yh * 2 + yl].astype(F32) for yl in range(2))
                    b = swap_halves(b)
                    if core == 0:
                        tiles = ((0, jnp.where(low, a, b)), (2, jnp.where(low, b, a)))
                    else:
                        tiles = ((1, b), (3, a))
                    for p, tile in tiles:
                        p = (yh + p) & 3
                        total[p] = tile if total[p] is None else total[p] + tile
                for p in range(4):
                    at = (xl * 4 + p) * 32
                    columns[0, at : at + 32, :] = total[p][:32]
                    columns[1, at : at + 32, :] = total[p][32:]

    r = lax.broadcasted_iota(jnp.int32, (256, 256), 0)
    wanted = (((r >> 1) & 7) << 5) | ((r >> 4) << 1) | (r & 1)
    order = jnp.where(lax.broadcasted_iota(jnp.int32, (256, 256), 1) == wanted, 1.0, 0.0).astype(BF)
    cross = [
        jnp.dot(order, columns[c].astype(BF), preferred_element_type=F32).astype(BF) for c in range(2)
    ]
    both = keep[...] + half[...].astype(F32)
    line = both[64:65] + both[65:66]
    both = jnp.concatenate([both[:64], *split(line), jnp.zeros((6, 128), F32)], axis=0).astype(BF)
    for q in range(16):
        for c in range(2):
            send[q, c * 16 : c * 16 + 16, :] = cross[c][q * 16 : q * 16 + 16]
        send[q, 32:104, :] = both


def finish_kernel(got, codes_t, keep, give):
    first = lax.axis_index("core") == 0
    total = jnp.sum(got[...].astype(F32), axis=0)
    keep[64:80, :] = jnp.where(first, total[:16], total[16:32])
    give[64:80, :] = jnp.where(first, total[16:32], total[:16])
    sums, count = total[32:96], total[96:97] + total[97:98]
    sums = jnp.concatenate([sums, swap_halves(sums)], axis=0).T[:64]
    own = jnp.where(first, codes_t[:, :128], codes_t[:, 128:])
    fresh = (sums + own) / (count + 1.0)
    keep[0:64, :] = fresh
    give[0:64, :] = fresh


def codes_kernel(mine, other, codes_t, cross):
    first = lax.axis_index("core") == 0
    a, b = mine[0:64, :], other[0:64, :]
    codes_t[:, :128] = jnp.where(first, a, b)
    codes_t[:, 128:] = jnp.where(first, b, a)
    total = mine[64:80, :] + other[64:80, :]
    for n in range(8):
        cross[:, n * 128 : (n + 1) * 128] = total[2 * n : 2 * n + 2]


def second_kernel(early, got_core, give_x, give_y, give_xy):
    xl, yl = lax.axis_index("xl"), lax.axis_index("yl")
    for n, block in enumerate((early, got_core)):
        give_x[n] = block[(1 - xl) * 2 + yl]
        give_y[n] = block[xl * 2 + 1 - yl]
        give_xy[n] = block[(1 - xl) * 2 + 1 - yl]


def home_kernel(early, got_core, got_x, got_y, got_xy, recon):
    core, xl = lax.axis_index("core"), lax.axis_index("xl")
    yh, yl = lax.axis_index("yh"), lax.axis_index("yl")
    low = half_mask((128, 128))
    own = [early[xl * 2 + yl], got_core[xl * 2 + yl]]
    for across, (same, far) in enumerate(((own, got_y), (got_x, got_xy))):
        blocks = []
        for c in range(2):
            near_c = jnp.where(core == c, same[0], same[1])
            far_c = jnp.where(core == c, far[0], far[1])
            for y in range(2):
                blocks.append(jnp.where(yl == y, near_c, far_c).astype(F32))
        side = (1 - xl) if across else xl
        for p, tile in enumerate(arrange(low, *blocks)):
            at = pl.multiple_of((side * 4 + ((yh + p) & 3)) * 128, 128)
            recon[:, pl.ds(at, 128)] = tile.astype(BF)


def call(kernel, name, outs, args, flops=0, moved=0, scratch=()):
    return pl.pallas_call(
        kernel,
        out_shape=tuple(jax.ShapeDtypeStruct(*o) for o in outs),
        in_specs=[VMEM] * len(args),
        out_specs=(VMEM,) * len(outs),
        scratch_shapes=list(scratch),
        compiler_params=pltpu.CompilerParams(vmem_limit_bytes=40 * 1024 * 1024),
        cost_estimate=pl.CostEstimate(flops=flops, bytes_accessed=moved, transcendentals=0),
        name=name,
    )(*args)


def per_device(samples, rotation, codebook):
    pack, copies = pl.pallas_call(
        open_kernel,
        out_shape=(
            jax.ShapeDtypeStruct((64, 1408), BF),
            jax.ShapeDtypeStruct((4, 128, 1024), BF),
        ),
        in_specs=[VMEM, VMEM, VMEM],
        out_specs=(VMEM, VMEM),
        compiler_params=pltpu.CompilerParams(vmem_limit_bytes=60 * 1024 * 1024),
        name="open",
    )(samples, rotation.T, codebook[0].T)
    packs = []
    for steps in ((3, 2), (None, 1)):
        pairs = [
            (c * 8 + ((y + step if y & 1 else y - step) & 7), c * 8 + y)
            for c, step in enumerate(steps)
            for y in range(8)
            if step is not None
        ]
        packs.append(lax.ppermute(pack, ("core", "yh", "yl"), pairs))
    mine = lax.all_to_all(copies, ("xl", "yl"), 0, 0, tiled=True).reshape(512, 1024)
    tools = call(
        prepare_kernel,
        "prepare",
        [((128, 1024), BF), ((128, 512), BF), ((512, 256), BF)],
        (pack, *packs),
        flops=16 * 10**9,
    )
    swap = [(0, 1), (1, 0)]
    other = lax.ppermute(mine, "core", swap)
    block, pair = ((4, 128, 128), BF), ((2, 128, 128), BF)
    sums, cross, early = call(
        early_kernel,
        "early",
        [((512, 256), F32), ((128, 1024), F32), block],
        (mine, *tools),
        moved=8_000_000,
    )
    send, late, *totals = call(
        late_kernel,
        "late",
        [((16, 64, 128), BF), block, ((144, 128), BF), ((144, 128), BF)],
        (other, *tools, sums, cross),
        moved=8_000_000,
    )
    moved = []
    for i in range(2):
        pairs = [
            (c * 8 + y, c * 8 + (((y & 6) + PLACES[c][y & 1][i]) & 7)) for c in range(2) for y in range(8)
        ]
        moved.append(lax.ppermute(totals[i], ("core", "yh", "yl"), pairs))
    got_core = lax.ppermute(late, "core", swap)
    keep, give = call(
        half_kernel, "half", [((80, 128), F32), ((80, 128), BF)], tuple(moved), flops=2 * 10**9
    )
    half = lax.ppermute(give, "core", swap)
    got = lax.all_to_all(send, NEAR, 0, 0, tiled=True)
    got, half, got_core = lax.optimization_barrier((got, half, got_core))
    (send,) = call(
        middle_kernel,
        "middle",
        [((16, 104, 128), BF)],
        (got, keep, half),
        scratch=[pltpu.VMEM((2, 256, 128), F32)],
    )
    gives = call(second_kernel, "second", [pair, pair, pair], (early, got_core))
    got_xy = lax.ppermute(gives[2], ("xl", "yl"), [(0, 3), (1, 2), (2, 1), (3, 0)])
    got_x = lax.ppermute(gives[0], "xl", swap)
    got_y = lax.ppermute(gives[1], "yl", swap)
    got = lax.all_to_all(send, FAR, 0, 0, tiled=True)
    got, got_xy, got_x, got_y = lax.optimization_barrier((got, got_xy, got_x, got_y))
    ends = [((80, 128), F32)] * 2
    mine, give = call(finish_kernel, "finish", ends, (got, codebook[0].T))
    other = lax.ppermute(give, "core", swap)
    (recon,) = call(
        home_kernel, "home", [((128, 1024), BF)], (early, got_core, got_x, got_y, got_xy)
    )
    other, recon = lax.optimization_barrier((other, recon))
    new_codes, cross = call(
        codes_kernel, "codes", [((64, 256), F32), ((2, 1024), F32)], (mine, other)
    )
    return recon, new_codes.T[None], cross


def solution(mesh):
    fine = Mesh(mesh.devices.reshape(SIZES), NAMES)
    rows = P(DP + SUB, None)
    return jax.shard_map(
        per_device,
        mesh=fine,
        in_specs=(rows, P(None, SUB), P(SUB, None, None)),
        out_specs=(rows, P(SUB, None, None), rows),
        check_vma=False,
    )
```

```python
import functools

import jax
import jax.numpy as jnp
from jax import lax
from jax.experimental import pallas as pl
from jax.experimental.pallas import tpu as pltpu
from jax.sharding import Mesh
from jax.sharding import PartitionSpec as P

SIZES = (8, 2, 2, 2, 4, 2)
NAMES = ("z", "xh", "core", "xl", "yh", "yl")
DP = ("z", "xh", "core")
SUB = ("xl", "yh", "yl")
PLACES = (((0, 6), (1, 3)), ((7, 5), (2, 4)))
FAR = ("z", "xh")
NEAR = ("core", "xl", "yh", "yl")
BF = jnp.bfloat16
F32 = jnp.float32
NT = (((1,), (1,)), ((), ()))
VMEM = pl.BlockSpec(memory_space=pltpu.VMEM)


def half_mask(shape):
    return lax.broadcasted_iota(jnp.int32, shape, len(shape) - 1) < 64


def swap_halves(x):
    return pltpu.roll(x, 64, 1)


def split(x):
    high = x.astype(BF).astype(F32)
    return high, x - high


def open_kernel(samples, turn_t, codes_t, pack, copies):
    for n in range(4):
        copies[n] = samples[...]
    codes = codes_t[...]
    square = jnp.sum(codes * codes, axis=0, keepdims=True)
    high = square.astype(BF).astype(F32)
    mid = (square - high).astype(BF).astype(F32)
    low = square - high - mid
    squares = jnp.concatenate([high, mid, low, jnp.zeros((13, 256), F32)], axis=0).astype(BF)
    pack[:, 0:1024] = turn_t[...]
    pack[:, 1024:1280] = codes.astype(BF)
    pack[0:16, 1280:] = squares[:, :128]
    pack[16:32, 1280:] = squares[:, 128:]
    pack[32:64, 1280:] = jnp.zeros((32, 128), BF)


def prepare_kernel(pack, first, second, turn, codes_t, left):
    core = lax.axis_index("core")
    w0, w1, w2 = pack[...], first[...], second[...]
    wa = jnp.where(core == 0, w0, w1)
    wb = jnp.where(core == 0, w1, w2)
    turn[0:64, :] = wa[:, :1024]
    turn[64:128, :] = wb[:, :1024]
    zero = jnp.zeros((64, 256), BF)
    both = jnp.concatenate(
        [
            jnp.concatenate([wa[:, 1024:1280], zero], axis=1),
            jnp.concatenate([zero, wb[:, 1024:1280]], axis=1),
        ],
        axis=0,
    )
    codes_t[...] = both
    squares = jnp.concatenate(
        [wa[0:16, 1280:], wa[16:32, 1280:], wb[0:16, 1280:], wb[16:32, 1280:]], axis=1
    )
    left[...] = jnp.concatenate([both * BF(-2.0), squares, jnp.zeros((112, 512), BF)], axis=0).T


def assign_rows(samples, turn, codes_t, left, sums, cross, put):
    rows, chunk = 512, 512
    lane = lax.broadcasted_iota(jnp.int32, (chunk, 128), 1)
    three = jnp.where(lane < 3, 1.0, 0.0).astype(BF)
    ones = jnp.ones((chunk, 128), BF)
    row16 = lax.broadcasted_iota(jnp.int32, (16, 256), 0)
    pick = (lax.broadcasted_iota(jnp.int32, (16, 256), 1) & 64) == 0
    pick = jnp.where(pick == (row16 == 0), 1.0, 0.0).astype(BF)
    for c in range(rows // chunk):
        x = samples[c * chunk : (c + 1) * chunk, :]
        rot = lax.dot_general(x, turn[...], NT, preferred_element_type=F32).astype(BF)
        square_high, square_low = split(jnp.square(rot.astype(F32)))
        square = jnp.concatenate([square_high, square_low], axis=1).astype(BF)
        row_square = lax.dot_general(pick, square, NT, preferred_element_type=F32)
        near = lax.dot_general(
            left[...], jnp.concatenate([rot, three], axis=1), NT, preferred_element_type=F32
        )
        parts = []
        for i in range(2):
            logits = -0.125 * (row_square[i : i + 1] + near[i * 256 : (i + 1) * 256])
            e = jnp.exp(logits - jnp.max(logits, axis=0, keepdims=True))
            parts.append((e * (1.0 / jnp.sum(e, axis=0, keepdims=True))).astype(BF))
        weights = jnp.concatenate(parts, axis=0)
        rebuilt = jnp.dot(codes_t[...], weights, preferred_element_type=F32).astype(BF)
        s = jnp.dot(weights, jnp.concatenate([rot, ones], axis=1), preferred_element_type=F32)
        k = jnp.dot(rebuilt, x, preferred_element_type=F32)
        sums = s if sums is None else sums + s
        cross = k if cross is None else cross + k
        back = rebuilt.T
        for n in range(chunk // 128):
            put(chunk // 128 * c + n, back[n * 128 : (n + 1) * 128])
    return sums, cross


def early_kernel(samples, turn, codes_t, left, sums, cross, recon):
    def put(block, tile):
        recon[block] = tile

    sums[...], cross[...] = assign_rows(samples, turn, codes_t, left, None, None, put)


def late_kernel(samples, turn, codes_t, left, sums, cross, send, recon, sums_a, sums_b):
    def put(block, tile):
        recon[block] = tile

    sums, cross = assign_rows(samples, turn, codes_t, left, sums[...], cross[...], put)
    cross = cross.astype(BF)
    r = lax.broadcasted_iota(jnp.int32, (256, 256), 0)
    wanted = ((r & 4) << 5) | ((r & 2) << 5) | ((r >> 3) << 1) | (r & 1)
    order = jnp.where(lax.broadcasted_iota(jnp.int32, (256, 256), 1) == wanted, 1.0, 0.0).astype(BF)
    pieces = [
        lax.dot_general(order, cross[:, n * 256 : (n + 1) * 256], NT, preferred_element_type=F32)
        for n in range(4)
    ]
    for d in range(32):
        tiles = [piece[8 * d : 8 * d + 8] for piece in pieces]
        send[d] = jnp.concatenate(tiles, axis=0).astype(BF)
    low = half_mask((64, 128))
    diagonal = (
        lax.broadcasted_iota(jnp.int32, (128, 128), 0)
        == lax.broadcasted_iota(jnp.int32, (128, 128), 1)
    )
    for i, out in enumerate((sums_a, sums_b)):
        lines = []
        for h in range(2):
            at = i * 256 + h * 128
            a, b = sums[at : at + 64, :128], sums[at + 64 : at + 128, :128]
            if i == 0:
                tile = jnp.where(low, a, swap_halves(b))
            else:
                tile = jnp.where(low, swap_halves(a), b)
            out[h * 64 : h * 64 + 64, :] = tile.astype(BF)
            count = jnp.where(diagonal, sums[at : at + 128, 128:], 0.0)
            lines += split(jnp.sum(count, axis=0, keepdims=True))
        out[128:144, :] = jnp.concatenate(lines + [jnp.zeros((12, 128), F32)], axis=0).astype(BF)


def half_kernel(first, second, keep, give):
    core = lax.axis_index("core")
    both = first[...].astype(F32) + second[...].astype(F32)
    empty = jnp.zeros((14, 128), F32)
    halves = []
    for h in range(2):
        line = both[128 + 2 * h : 129 + 2 * h] + both[129 + 2 * h : 130 + 2 * h]
        halves.append(jnp.concatenate([both[h * 64 : h * 64 + 64], *split(line), empty], axis=0))
    keep[...] = jnp.where(core == 0, halves[0], halves[1])
    give[...] = jnp.where(core == 0, halves[1], halves[0]).astype(BF)


def arrange(low, a, b, c, d):
    e, f, g, h = (swap_halves(x) for x in (a, b, c, d))
    return [jnp.where(low, a, f), jnp.where(low, d, b), jnp.where(low, h, c), jnp.where(low, e, g)]


def middle_kernel(got, keep, half, send):
    low = half_mask((32, 128))
    columns = []
    for xl in range(2):
        total = [jnp.zeros((32, 128), F32)] * 4
        for yh in range(4):
            blocks = [got[core * 16 + xl * 8 + yh * 2 + yl].astype(F32) for core in range(2) for yl in range(2)]
            for p, tile in enumerate(arrange(low, *blocks)):
                total[(yh + p) & 3] += tile
        columns += total
    r = lax.broadcasted_iota(jnp.int32, (256, 256), 0)
    wanted = (((r >> 1) & 7) << 5) | ((r >> 4) << 1) | (r & 1)
    order = jnp.where(lax.broadcasted_iota(jnp.int32, (256, 256), 1) == wanted, 1.0, 0.0).astype(BF)
    cross = jnp.dot(
        order, jnp.concatenate(columns, axis=0).astype(BF), preferred_element_type=F32
    ).astype(BF)
    both = keep[...] + half[...].astype(F32)
    line = both[64:65] + both[65:66]
    both = jnp.concatenate([both[:64], *split(line), jnp.zeros((6, 128), F32)], axis=0).astype(BF)
    for q in range(16):
        send[q, 0:16, :] = cross[q * 16 : q * 16 + 16]
        send[q, 16:88, :] = both


def finish_kernel(got, codes_t, cross, fresh):
    total = jnp.sum(got[...].astype(F32), axis=0)
    for n in range(8):
        cross[:, n * 128 : (n + 1) * 128] = total[2 * n : 2 * n + 2]
    sums, count = total[16:80], total[80:81] + total[81:82]
    sums = jnp.concatenate([sums, swap_halves(sums)], axis=0).T[:64]
    own = jnp.where(lax.axis_index("core") == 0, codes_t[:, :128], codes_t[:, 128:])
    fresh[...] = (sums + own) / (count + 1.0)


def codes_kernel(mine, other, codes_t):
    a, b = mine[...], other[...]
    codes_t[:, :128] = jnp.where(lax.axis_index("core") == 0, a, b)
    codes_t[:, 128:] = jnp.where(lax.axis_index("core") == 0, b, a)


def second_kernel(early, got_core, give_x, give_y, give_xy):
    xl, yl = lax.axis_index("xl"), lax.axis_index("yl")
    for n, block in enumerate((early, got_core)):
        give_x[n] = block[(1 - xl) * 2 + yl]
        give_y[n] = block[xl * 2 + 1 - yl]
        give_xy[n] = block[(1 - xl) * 2 + 1 - yl]


def home_kernel(early, got_core, got_x, got_y, got_xy, recon):
    core, xl = lax.axis_index("core"), lax.axis_index("xl")
    yh, yl = lax.axis_index("yh"), lax.axis_index("yl")
    low = half_mask((128, 128))
    own = [early[xl * 2 + yl], got_core[xl * 2 + yl]]
    for across, (same, far) in enumerate(((own, got_y), (got_x, got_xy))):
        blocks = []
        for c in range(2):
            near_c = jnp.where(core == c, same[0], same[1])
            far_c = jnp.where(core == c, far[0], far[1])
            for y in range(2):
                blocks.append(jnp.where(yl == y, near_c, far_c).astype(F32))
        side = (1 - xl) if across else xl
        for p, tile in enumerate(arrange(low, *blocks)):
            at = pl.multiple_of((side * 4 + ((yh + p) & 3)) * 128, 128)
            recon[:, pl.ds(at, 128)] = tile.astype(BF)


def call(kernel, name, outs, args, flops=0, moved=0):
    return pl.pallas_call(
        kernel,
        out_shape=tuple(jax.ShapeDtypeStruct(*o) for o in outs),
        in_specs=[VMEM] * len(args),
        out_specs=(VMEM,) * len(outs),
        compiler_params=pltpu.CompilerParams(vmem_limit_bytes=40 * 1024 * 1024),
        cost_estimate=pl.CostEstimate(flops=flops, bytes_accessed=moved, transcendentals=0),
        name=name,
    )(*args)


def per_device(samples, rotation, codebook):
    pack, copies = pl.pallas_call(
        open_kernel,
        out_shape=(
            jax.ShapeDtypeStruct((64, 1408), BF),
            jax.ShapeDtypeStruct((4, 128, 1024), BF),
        ),
        in_specs=[VMEM, VMEM, VMEM],
        out_specs=(VMEM, VMEM),
        compiler_params=pltpu.CompilerParams(vmem_limit_bytes=60 * 1024 * 1024),
        name="open",
    )(samples, rotation.T, codebook[0].T)
    packs = []
    for steps in ((2, 1), (None, 3)):
        pairs = [
            (c * 8 + ((y + step if y & 1 else y - step) & 7), c * 8 + y)
            for c, step in enumerate(steps)
            for y in range(8)
            if step is not None
        ]
        packs.append(lax.ppermute(pack, ("core", "yh", "yl"), pairs))
    mine = lax.all_to_all(copies, ("xl", "yl"), 0, 0, tiled=True).reshape(512, 1024)
    tools = call(
        prepare_kernel,
        "prepare",
        [((128, 1024), BF), ((128, 512), BF), ((512, 256), BF)],
        (pack, *packs),
        flops=16 * 10**9,
    )
    swap = [(0, 1), (1, 0)]
    other = lax.ppermute(mine, "core", swap)
    block, pair = ((4, 128, 128), BF), ((2, 128, 128), BF)
    sums, cross, early = call(
        early_kernel,
        "early",
        [((512, 256), F32), ((128, 1024), F32), block],
        (mine, *tools),
        moved=8_000_000,
    )
    send, late, *totals = call(
        late_kernel,
        "late",
        [((32, 32, 128), BF), block, ((144, 128), BF), ((144, 128), BF)],
        (other, *tools, sums, cross),
        moved=8_000_000,
    )
    moved = []
    for i in (1, 0):
        pairs = [
            (c * 8 + y, c * 8 + (((y & 6) + PLACES[c][y & 1][i]) & 7)) for c in range(2) for y in range(8)
        ]
        moved.append(lax.ppermute(totals[i], ("core", "yh", "yl"), pairs))
    got_core = lax.ppermute(late, "core", swap)
    keep, give = call(
        half_kernel, "half", [((80, 128), F32), ((80, 128), BF)], tuple(moved), flops=2 * 10**9
    )
    half = lax.ppermute(give, "core", swap)
    got = lax.all_to_all(send, NEAR, 0, 0, tiled=True)
    got, half, got_core = lax.optimization_barrier((got, half, got_core))
    (send,) = call(middle_kernel, "middle", [((16, 88, 128), BF)], (got, keep, half))
    gives = call(second_kernel, "second", [pair, pair, pair], (early, got_core))
    got_xy = lax.ppermute(gives[2], ("xl", "yl"), [(0, 3), (1, 2), (2, 1), (3, 0)])
    got_x = lax.ppermute(gives[0], "xl", swap)
    got_y = lax.ppermute(gives[1], "yl", swap)
    got = lax.all_to_all(send, FAR, 0, 0, tiled=True)
    got, got_xy, got_x, got_y = lax.optimization_barrier((got, got_xy, got_x, got_y))
    cross, fresh = call(
        finish_kernel,
        "finish",
        [((2, 1024), F32), ((64, 128), F32)],
        (got, codebook[0].T),
    )
    fresh_other = lax.ppermute(fresh, "core", swap)
    (recon,) = call(
        home_kernel, "home", [((128, 1024), BF)], (early, got_core, got_x, got_y, got_xy)
    )
    fresh_other, recon = lax.optimization_barrier((fresh_other, recon))
    (new_codes,) = call(codes_kernel, "codes", [((64, 256), F32)], (fresh, fresh_other))
    return recon, new_codes.T[None], cross


def solution(mesh):
    fine = Mesh(mesh.devices.reshape(SIZES), NAMES)
    rows = P(DP + SUB, None)
    return jax.shard_map(
        per_device,
        mesh=fine,
        in_specs=(rows, P(None, SUB), P(SUB, None, None)),
        out_specs=(rows, P(SUB, None, None), rows),
        check_vma=False,
    )
```

```python
import functools

import jax
import jax.numpy as jnp
from jax import lax
from jax.experimental import pallas as pl
from jax.experimental.pallas import tpu as pltpu
from jax.sharding import Mesh
from jax.sharding import PartitionSpec as P

SIZES = (8, 2, 2, 2, 4, 2)
NAMES = ("z", "xh", "core", "xl", "yh", "yl")
DP = ("z", "xh", "core")
SUB = ("xl", "yh", "yl")
PLACES = (((0, 6), (1, 3)), ((7, 5), (2, 4)))
FAR = ("z", "xh")
NEAR = ("core", "xl", "yh", "yl")
BF = jnp.bfloat16
F32 = jnp.float32
NT = (((1,), (1,)), ((), ()))
VMEM = pl.BlockSpec(memory_space=pltpu.VMEM)


def half_mask(shape):
    return lax.broadcasted_iota(jnp.int32, shape, len(shape) - 1) < 64


def swap_halves(x):
    return pltpu.roll(x, 64, 1)


def split(x):
    high = x.astype(BF).astype(F32)
    return high, x - high


def open_kernel(samples, turn_t, codes_t, pack, copies):
    for n in range(4):
        copies[n] = samples[...]
    codes = codes_t[...]
    square = jnp.sum(codes * codes, axis=0, keepdims=True)
    high = square.astype(BF).astype(F32)
    mid = (square - high).astype(BF).astype(F32)
    low = square - high - mid
    squares = jnp.concatenate([high, mid, low, jnp.zeros((13, 256), F32)], axis=0).astype(BF)
    pack[:, 0:1024] = turn_t[...]
    pack[:, 1024:1280] = codes.astype(BF)
    pack[0:16, 1280:] = squares[:, :128]
    pack[16:32, 1280:] = squares[:, 128:]
    pack[32:64, 1280:] = jnp.zeros((32, 128), BF)


def prepare_kernel(pack, first, second, turn, codes_t, left):
    core = lax.axis_index("core")
    w0, w1, w2 = pack[...], first[...], second[...]
    wa = jnp.where(core == 0, w0, w1)
    wb = jnp.where(core == 0, w1, w2)
    turn[0:64, :] = wa[:, :1024]
    turn[64:128, :] = wb[:, :1024]
    zero = jnp.zeros((64, 256), BF)
    both = jnp.concatenate(
        [
            jnp.concatenate([wa[:, 1024:1280], zero], axis=1),
            jnp.concatenate([zero, wb[:, 1024:1280]], axis=1),
        ],
        axis=0,
    )
    codes_t[...] = both
    squares = jnp.concatenate(
        [wa[0:16, 1280:], wa[16:32, 1280:], wb[0:16, 1280:], wb[16:32, 1280:]], axis=1
    )
    left[...] = jnp.concatenate([both * BF(-2.0), squares, jnp.zeros((112, 512), BF)], axis=0).T


def assign_rows(samples, turn, codes_t, left, sums, cross, put):
    rows, chunk = 512, 512
    lane = lax.broadcasted_iota(jnp.int32, (chunk, 128), 1)
    three = jnp.where(lane < 3, 1.0, 0.0).astype(BF)
    ones = jnp.ones((chunk, 128), BF)
    row16 = lax.broadcasted_iota(jnp.int32, (16, 256), 0)
    pick = (lax.broadcasted_iota(jnp.int32, (16, 256), 1) & 64) == 0
    pick = jnp.where(pick == (row16 == 0), 1.0, 0.0).astype(BF)
    for c in range(rows // chunk):
        x = samples[c * chunk : (c + 1) * chunk, :]
        rot = lax.dot_general(x, turn[...], NT, preferred_element_type=F32).astype(BF)
        square_high, square_low = split(jnp.square(rot.astype(F32)))
        square = jnp.concatenate([square_high, square_low], axis=1).astype(BF)
        row_square = lax.dot_general(pick, square, NT, preferred_element_type=F32)
        near = lax.dot_general(
            left[...], jnp.concatenate([rot, three], axis=1), NT, preferred_element_type=F32
        )
        parts = []
        for i in range(2):
            logits = -0.125 * (row_square[i : i + 1] + near[i * 256 : (i + 1) * 256])
            e = jnp.exp(logits - jnp.max(logits, axis=0, keepdims=True))
            parts.append((e * (1.0 / jnp.sum(e, axis=0, keepdims=True))).astype(BF))
        weights = jnp.concatenate(parts, axis=0)
        rebuilt = jnp.dot(codes_t[...], weights, preferred_element_type=F32).astype(BF)
        s = jnp.dot(weights, jnp.concatenate([rot, ones], axis=1), preferred_element_type=F32)
        k = jnp.dot(rebuilt, x, preferred_element_type=F32)
        sums = s if sums is None else sums + s
        cross = k if cross is None else cross + k
        back = rebuilt.T
        for n in range(chunk // 128):
            put(chunk // 128 * c + n, back[n * 128 : (n + 1) * 128])
    return sums, cross


def early_kernel(samples, turn, codes_t, left, sums, cross, recon):
    def put(block, tile):
        recon[block] = tile

    sums[...], cross[...] = assign_rows(samples, turn, codes_t, left, None, None, put)


def late_kernel(samples, turn, codes_t, left, sums, cross, send, recon, sums_a, sums_b):
    def put(block, tile):
        recon[block] = tile

    sums, cross = assign_rows(samples, turn, codes_t, left, sums[...], cross[...], put)
    cross = cross.astype(BF)
    r = lax.broadcasted_iota(jnp.int32, (256, 256), 0)
    wanted = ((r & 4) << 5) | ((r & 2) << 5) | ((r >> 3) << 1) | (r & 1)
    order = jnp.where(lax.broadcasted_iota(jnp.int32, (256, 256), 1) == wanted, 1.0, 0.0).astype(BF)
    pieces = [
        lax.dot_general(order, cross[:, n * 256 : (n + 1) * 256], NT, preferred_element_type=F32)
        for n in range(4)
    ]
    for d in range(32):
        tiles = [piece[8 * d : 8 * d + 8] for piece in pieces]
        send[d] = jnp.concatenate(tiles, axis=0).astype(BF)
    low = half_mask((64, 128))
    diagonal = (
        lax.broadcasted_iota(jnp.int32, (128, 128), 0)
        == lax.broadcasted_iota(jnp.int32, (128, 128), 1)
    )
    for i, out in enumerate((sums_a, sums_b)):
        lines = []
        for h in range(2):
            at = i * 256 + h * 128
            a, b = sums[at : at + 64, :128], sums[at + 64 : at + 128, :128]
            if i == 0:
                tile = jnp.where(low, a, swap_halves(b))
            else:
                tile = jnp.where(low, swap_halves(a), b)
            out[h * 64 : h * 64 + 64, :] = tile.astype(BF)
            count = jnp.where(diagonal, sums[at : at + 128, 128:], 0.0)
            lines += split(jnp.sum(count, axis=0, keepdims=True))
        out[128:144, :] = jnp.concatenate(lines + [jnp.zeros((12, 128), F32)], axis=0).astype(BF)


def half_kernel(first, second, keep, give):
    core = lax.axis_index("core")
    both = first[...].astype(F32) + second[...].astype(F32)
    empty = jnp.zeros((14, 128), F32)
    halves = []
    for h in range(2):
        line = both[128 + 2 * h : 129 + 2 * h] + both[129 + 2 * h : 130 + 2 * h]
        halves.append(jnp.concatenate([both[h * 64 : h * 64 + 64], *split(line), empty], axis=0))
    keep[...] = jnp.where(core == 0, halves[0], halves[1])
    give[...] = jnp.where(core == 0, halves[1], halves[0]).astype(BF)


def arrange(low, a, b, c, d):
    e, f, g, h = (swap_halves(x) for x in (a, b, c, d))
    return [jnp.where(low, a, f), jnp.where(low, d, b), jnp.where(low, h, c), jnp.where(low, e, g)]


def middle_kernel(got, keep, half, send):
    low = half_mask((32, 128))
    columns = []
    for xl in range(2):
        total = [jnp.zeros((32, 128), F32)] * 4
        for yh in range(4):
            blocks = [got[core * 16 + xl * 8 + yh * 2 + yl].astype(F32) for core in range(2) for yl in range(2)]
            for p, tile in enumerate(arrange(low, *blocks)):
                total[(yh + p) & 3] += tile
        columns += total
    r = lax.broadcasted_iota(jnp.int32, (256, 256), 0)
    wanted = (((r >> 1) & 7) << 5) | ((r >> 4) << 1) | (r & 1)
    order = jnp.where(lax.broadcasted_iota(jnp.int32, (256, 256), 1) == wanted, 1.0, 0.0).astype(BF)
    cross = jnp.dot(
        order, jnp.concatenate(columns, axis=0).astype(BF), preferred_element_type=F32
    ).astype(BF)
    both = keep[...] + half[...].astype(F32)
    line = both[64:65] + both[65:66]
    both = jnp.concatenate([both[:64], *split(line), jnp.zeros((6, 128), F32)], axis=0).astype(BF)
    for q in range(16):
        send[q, 0:16, :] = cross[q * 16 : q * 16 + 16]
        send[q, 16:88, :] = both


def finish_kernel(got, codes_t, cross, fresh):
    total = jnp.sum(got[...].astype(F32), axis=0)
    for n in range(8):
        cross[:, n * 128 : (n + 1) * 128] = total[2 * n : 2 * n + 2]
    sums, count = total[16:80], total[80:81] + total[81:82]
    sums = jnp.concatenate([sums, swap_halves(sums)], axis=0).T[:64]
    own = jnp.where(lax.axis_index("core") == 0, codes_t[:, :128], codes_t[:, 128:])
    fresh[...] = (sums + own) / (count + 1.0)


def codes_kernel(mine, other, codes_t):
    a, b = mine[...], other[...]
    codes_t[:, :128] = jnp.where(lax.axis_index("core") == 0, a, b)
    codes_t[:, 128:] = jnp.where(lax.axis_index("core") == 0, b, a)


def second_kernel(early, got_core, give_x, give_y, give_xy):
    xl, yl = lax.axis_index("xl"), lax.axis_index("yl")
    for n, block in enumerate((early, got_core)):
        give_x[n] = block[(1 - xl) * 2 + yl]
        give_y[n] = block[xl * 2 + 1 - yl]
        give_xy[n] = block[(1 - xl) * 2 + 1 - yl]


def home_kernel(early, got_core, got_x, got_y, got_xy, recon):
    core, xl = lax.axis_index("core"), lax.axis_index("xl")
    yh, yl = lax.axis_index("yh"), lax.axis_index("yl")
    low = half_mask((128, 128))
    own = [early[xl * 2 + yl], got_core[xl * 2 + yl]]
    for across, (same, far) in enumerate(((own, got_y), (got_x, got_xy))):
        blocks = []
        for c in range(2):
            near_c = jnp.where(core == c, same[0], same[1])
            far_c = jnp.where(core == c, far[0], far[1])
            for y in range(2):
                blocks.append(jnp.where(yl == y, near_c, far_c).astype(F32))
        side = (1 - xl) if across else xl
        for p, tile in enumerate(arrange(low, *blocks)):
            at = pl.multiple_of((side * 4 + ((yh + p) & 3)) * 128, 128)
            recon[:, pl.ds(at, 128)] = tile.astype(BF)


def call(kernel, name, outs, args, flops=0, moved=0):
    return pl.pallas_call(
        kernel,
        out_shape=tuple(jax.ShapeDtypeStruct(*o) for o in outs),
        in_specs=[VMEM] * len(args),
        out_specs=(VMEM,) * len(outs),
        compiler_params=pltpu.CompilerParams(vmem_limit_bytes=40 * 1024 * 1024),
        cost_estimate=pl.CostEstimate(flops=flops, bytes_accessed=moved, transcendentals=0),
        name=name,
    )(*args)


def per_device(samples, rotation, codebook):
    pack, copies = pl.pallas_call(
        open_kernel,
        out_shape=(
            jax.ShapeDtypeStruct((64, 1408), BF),
            jax.ShapeDtypeStruct((4, 128, 1024), BF),
        ),
        in_specs=[VMEM, VMEM, VMEM],
        out_specs=(VMEM, VMEM),
        compiler_params=pltpu.CompilerParams(vmem_limit_bytes=60 * 1024 * 1024),
        name="open",
    )(samples, rotation.T, codebook[0].T)
    packs = []
    for steps in ((2, 1), (None, 3)):
        pairs = [
            (c * 8 + ((y + step if y & 1 else y - step) & 7), c * 8 + y)
            for c, step in enumerate(steps)
            for y in range(8)
            if step is not None
        ]
        packs.append(lax.ppermute(pack, ("core", "yh", "yl"), pairs))
    mine = lax.all_to_all(copies, ("xl", "yl"), 0, 0, tiled=True).reshape(512, 1024)
    tools = call(
        prepare_kernel,
        "prepare",
        [((128, 1024), BF), ((128, 512), BF), ((512, 256), BF)],
        (pack, *packs),
        flops=16 * 10**9,
    )
    swap = [(0, 1), (1, 0)]
    other = lax.ppermute(mine, "core", swap)
    block, pair = ((4, 128, 128), BF), ((2, 128, 128), BF)
    sums, cross, early = call(
        early_kernel,
        "early",
        [((512, 256), F32), ((128, 1024), F32), block],
        (mine, *tools),
        moved=8_000_000,
    )
    send, late, *totals = call(
        late_kernel,
        "late",
        [((32, 32, 128), BF), block, ((144, 128), BF), ((144, 128), BF)],
        (other, *tools, sums, cross),
        moved=8_000_000,
    )
    moved = []
    for i in (1, 0):
        pairs = [
            (c * 8 + y, c * 8 + (((y & 6) + PLACES[c][y & 1][i]) & 7)) for c in range(2) for y in range(8)
        ]
        moved.append(lax.ppermute(totals[i], ("core", "yh", "yl"), pairs))
    got_core = lax.ppermute(late, "core", swap)
    keep, give = call(
        half_kernel, "half", [((80, 128), F32), ((80, 128), BF)], tuple(moved), flops=2 * 10**9
    )
    half = lax.ppermute(give, "core", swap)
    got = lax.all_to_all(send, NEAR, 0, 0, tiled=True)
    gives = call(second_kernel, "second", [pair, pair, pair], (early, got_core))
    got, half, *gives = lax.optimization_barrier((got, half, *gives))
    (send,) = call(middle_kernel, "middle", [((16, 88, 128), BF)], (got, keep, half))
    got_xy = lax.ppermute(gives[2], ("xl", "yl"), [(0, 3), (1, 2), (2, 1), (3, 0)])
    got_x = lax.ppermute(gives[0], "xl", swap)
    got_y = lax.ppermute(gives[1], "yl", swap)
    got = lax.all_to_all(send, FAR, 0, 0, tiled=True)
    got, got_xy, got_x, got_y = lax.optimization_barrier((got, got_xy, got_x, got_y))
    cross, fresh = call(
        finish_kernel,
        "finish",
        [((2, 1024), F32), ((64, 128), F32)],
        (got, codebook[0].T),
    )
    fresh_other = lax.ppermute(fresh, "core", swap)
    (recon,) = call(
        home_kernel, "home", [((128, 1024), BF)], (early, got_core, got_x, got_y, got_xy)
    )
    fresh_other, recon = lax.optimization_barrier((fresh_other, recon))
    (new_codes,) = call(codes_kernel, "codes", [((64, 256), F32)], (fresh, fresh_other))
    return recon, new_codes.T[None], cross


def solution(mesh):
    fine = Mesh(mesh.devices.reshape(SIZES), NAMES)
    rows = P(DP + SUB, None)
    return jax.shard_map(
        per_device,
        mesh=fine,
        in_specs=(rows, P(None, SUB), P(SUB, None, None)),
        out_specs=(rows, P(SUB, None, None), rows),
        check_vma=False,
    )
```
